32 devices in a mesh: img: 2 (over y), tile: 16 (over z, x, core).
Axes of the slice: x: 2, y: 2, z: 4, core: 2. Of those that a mesh axis runs over, the one named last changes fastest.
Arguments:
- means: float32 [3, 65536], P(None, ('img', 'tile')), may hold values from -3 to 3
- log_scales: float32 [3, 65536], P(None, ('img', 'tile')), may hold values from -6 to -3
- quat_w: float32 [1, 65536], P(None, ('img', 'tile')), may hold values from 1 to 2
- quat_v: float32 [3, 65536], P(None, ('img', 'tile')), may hold values from -1 to 1
- opacity: float32 [1, 65536], P(None, ('img', 'tile')), may hold values from -6 to 6
- sh_coeffs: float32 [48, 65536], P(None, ('img', 'tile')), may hold values from -3 to 3
- cameras: float32 [2, 10], replicated, may hold values from -300 to 300
- requests: int32 [2, 16, 2, 16, 16], P('img', 'tile'), may hold values from 0 to 2047, as said below
- lists: int32 [2, 128, 256], P('img', 'tile'), may hold values from 0 to 511, as said below
- counts: int32 [2, 128], P('img', 'tile'), may hold values from 1 to 256
- image_cot: float32 [2, 3, 128, 256], P('img', None, 'tile'), may hold values from -6 to 6
Outputs:
- rendered: float32 [2, 3, 128, 256], P('img', None, 'tile')
- param_grad: float32 [59, 65536], P(None, ('img', 'tile'))
- camera_grad: float32 [2, 10], replicated
The draws below stay inside these ranges and needn't reach their ends.
Inputs may be any that keep to these rules, and one draw needn't show every extreme that they name: Entries may repeat within a device's requests. `lists`: each entry names a request slot of the device that renders the tile; slot (a * 16 + b) * 16 + c is requests[i, t, a, b, c]; only the first counts entries of a list are live.
All inputs are finite; a program needn't handle non-finite values.
Results may differ from the reference program's by a relative error of at most 0.0003.
Values sent between devices are 32-bit elements; how exact they have to be, the bound alone decides.
A program may use at most 64 MiB of HBM per device.

```python
import math
import jax
import jax.numpy as jnp
from jax import lax

NG_DEV = 2048
TILES_DEV = 8
LIST = 256
CAP = 16
TILE_SIDE = 16
TW = 16
G = 65536
TILES = 128
SLOTS = 512
PIX = 256
N_IMG = 2
N_TILE = 16


def scene_integers(key):
    base = jax.random.fold_in(key, 4409)
    requests = jax.random.randint(jax.random.fold_in(base, 1), (N_IMG, N_TILE, N_IMG, N_TILE, CAP), 0, NG_DEV, dtype=jnp.int32)
    lists = jax.random.randint(jax.random.fold_in(base, 2), (N_IMG, TILES, LIST), 0, SLOTS, dtype=jnp.int32)
    counts = jax.random.randint(jax.random.fold_in(base, 3), (N_IMG, TILES), 1, LIST + 1, dtype=jnp.int32)
    return (requests, lists, counts)


def scene_cameras(key):
    base = jax.random.fold_in(key, 5501)
    quats = jax.random.normal(jax.random.fold_in(base, 1), (N_IMG, 4), dtype=jnp.float32)
    quats = quats / jnp.sqrt(jnp.sum(quats * quats, axis=1, keepdims=True))
    unit_w, unit_x, unit_y, unit_z = (quats[:, 0], quats[:, 1], quats[:, 2], quats[:, 3])
    first_row = jnp.stack([1.0 - 2.0 * (unit_y * unit_y + unit_z * unit_z), 2.0 * (unit_x * unit_y - unit_w * unit_z), 2.0 * (unit_x * unit_z + unit_w * unit_y)], axis=1)
    second_row = jnp.stack([2.0 * (unit_x * unit_y + unit_w * unit_z), 1.0 - 2.0 * (unit_x * unit_x + unit_z * unit_z), 2.0 * (unit_y * unit_z - unit_w * unit_x)], axis=1)
    third_row = jnp.stack([2.0 * (unit_x * unit_z - unit_w * unit_y), 2.0 * (unit_y * unit_z + unit_w * unit_x), 1.0 - 2.0 * (unit_x * unit_x + unit_y * unit_y)], axis=1)
    gain = jnp.exp(jax.random.uniform(jax.random.fold_in(base, 2), (N_IMG,), jnp.float32, math.log(150.0), math.log(300.0)))
    offset = jax.random.uniform(jax.random.fold_in(base, 3), (N_IMG, 2), jnp.float32, -20.0, 20.0)
    polar = jax.random.uniform(jax.random.fold_in(base, 4), (N_IMG, 1), jnp.float32, 0.3, 2.8)
    azimuth = jax.random.uniform(jax.random.fold_in(base, 5), (N_IMG, 1), jnp.float32, -math.pi, math.pi)
    cameras = jnp.concatenate([gain[:, None] * first_row, gain[:, None] * second_row, offset, polar, azimuth], axis=1)
    return (cameras, third_row, gain)


def draw_requests(key, part):
    return scene_integers(key)[0]


def draw_lists(key, part):
    return scene_integers(key)[1]


def draw_counts(key, part):
    return scene_integers(key)[2]


def draw_cameras(key, part):
    return scene_cameras(key)[0].astype(jnp.float32)


def draw_means(key, part):
    requests, lists, counts = scene_integers(key)
    cameras, depth_axis, gain = scene_cameras(key)
    tile_owner = (jnp.arange(TILES, dtype=jnp.int32) // TILES_DEV)[None, :, None]
    image_index = jnp.arange(N_IMG, dtype=jnp.int32)[:, None, None]
    owner_flat = lists // CAP
    choose = lists % CAP
    local = requests[image_index, tile_owner, owner_flat // N_TILE, owner_flat % N_TILE, choose]
    gaussian_ids = (owner_flat * NG_DEV + local).reshape(-1)
    entry_ids = jnp.arange(N_IMG * TILES * LIST, dtype=jnp.int32).reshape(N_IMG, TILES, LIST)
    live = jnp.arange(LIST, dtype=jnp.int32)[None, None, :] < counts[:, :, None]
    score = jnp.where(live, entry_ids, -1).reshape(-1)
    winner = jnp.full((G,), -1, dtype=jnp.int32).at[gaussian_ids].max(score)
    placed = winner >= 0
    safe = jnp.maximum(winner, 0)
    win_image = safe // (TILES * LIST)
    win_tile = safe // LIST % TILES
    place_key = jax.random.fold_in(key, 6607)
    jitter = jax.random.uniform(jax.random.fold_in(place_key, 1), (2, G), jnp.float32, -12.0, 12.0)
    height = TILE_SIDE * TILES / TW
    centre_x = (TILE_SIDE * (win_tile % TW)).astype(jnp.float32) + 0.5 * TILE_SIDE - 0.5 * TILE_SIDE * TW
    centre_y = (TILE_SIDE * (win_tile // TW)).astype(jnp.float32) + 0.5 * TILE_SIDE - 0.5 * height
    chosen = cameras[win_image]
    target_x = centre_x + jitter[0] - chosen[:, 6]
    target_y = centre_y + jitter[1] - chosen[:, 7]
    squared_gain = (gain * gain)[win_image]
    along = (chosen[:, 0:3] * target_x[:, None] + chosen[:, 3:6] * target_y[:, None]) / squared_gain[:, None]
    depth = jax.random.uniform(jax.random.fold_in(place_key, 2), (G,), jnp.float32, -1.0, 1.0)
    aimed = along + depth[:, None] * depth_axis[win_image]
    loose = jax.random.uniform(jax.random.fold_in(place_key, 3), (G, 3), jnp.float32, -1.0, 1.0)
    result = jnp.where(placed[:, None], aimed, loose)
    return result.T.astype(jnp.float32)


def block_scale(own_key, shape, split, smallest, top_value):
    level, own = 1.0, jax.random.fold_in(own_key, 6)
    for axis_at, parts in split:
        steps = jnp.exp(jax.random.uniform(jax.random.fold_in(own, axis_at), (parts,), jnp.float32, smallest / len(split), top_value / len(split)))
        level = level * jnp.repeat(steps, shape[axis_at] // parts).reshape([-1 if axis == axis_at else 1 for axis in range(len(shape))])
    return level


def scatter_about(stream_key, shape, spread, limit, pieces=(), kind=jnp.bfloat16):
    values = jax.random.normal(stream_key, shape, jnp.float32) * spread
    if len(pieces) > 0:
        values = block_scale(stream_key, shape, pieces, -0.22, 0.18) * values
    return jnp.clip(values, min=-limit, max=limit).astype(kind)


def setup_inputs(seed: int = 0) -> dict:
    arg_keys = jax.random.split(jax.random.key(seed), 12)
    return {
        "means": draw_means(jax.random.fold_in(arg_keys[11], 71), 0),
        "log_scales": jnp.clip(-6.0 + 3.0 * jax.random.uniform(arg_keys[1], (3, G), jnp.float32) ** block_scale(arg_keys[1], (3, G), ((1, 32),), -0.2, 0.2), -6.0, -3.0),
        "quat_w": jnp.clip(1.0 + 1.0 * jax.random.uniform(arg_keys[2], (1, G), jnp.float32) ** block_scale(arg_keys[2], (1, G), ((1, 32),), -0.2, 0.2), 1.0, 2.0),
        "quat_v": jnp.clip(jax.random.uniform(arg_keys[3], (3, G), jnp.float32, -1.0, 1.0) * block_scale(arg_keys[3], (3, G), ((1, 32),), -0.4, 0.0), -1.0, 1.0),
        "opacity": jnp.clip(jax.random.uniform(arg_keys[4], (1, G), jnp.float32, -6.0, 6.0) * block_scale(arg_keys[4], (1, G), ((1, 32),), -0.4, 0.0), -6.0, 6.0),
        "sh_coeffs": scatter_about(arg_keys[5], (48, G), 0.5, 3.0, ((1, 32),), jnp.float32),
        "cameras": draw_cameras(jax.random.fold_in(arg_keys[11], 71), 0),
        "requests": draw_requests(jax.random.fold_in(arg_keys[11], 71), 0),
        "lists": draw_lists(jax.random.fold_in(arg_keys[11], 71), 0),
        "counts": draw_counts(jax.random.fold_in(arg_keys[11], 71), 0),
        "image_cot": scatter_about(arg_keys[10], (N_IMG, 3, TILES, PIX), 1.0, 6.0, ((0, 2), (2, 16)), jnp.float32),
    }


sh_first = 0.28209479177387814
sh_second = 0.4886025119029199
sh_third = (1.0925484305920792, -1.0925484305920792, 0.31539156525252005, -1.0925484305920792, 0.5462742152960396)
sh_fourth = (-0.5900435899266435, 2.890611442640554, -0.4570457994644658, 0.3731763325901154, -0.4570457994644658, 1.445305721320277, -0.5900435899266435)
dilation = 0.3

def harmonic_values(camera):
    polar_angle = camera[8]
    azimuth = camera[9]
    view_x = jnp.sin(polar_angle) * jnp.cos(azimuth)
    view_y = jnp.sin(polar_angle) * jnp.sin(azimuth)
    view_z = jnp.cos(polar_angle)
    square_x = view_x * view_x
    square_y = view_y * view_y
    square_z = view_z * view_z
    return jnp.stack([sh_first + 0.0 * view_x, -sh_second * view_y, sh_second * view_z, -sh_second * view_x, sh_third[0] * view_x * view_y, sh_third[1] * view_y * view_z, sh_third[2] * (2.0 * square_z - square_x - square_y), sh_third[3] * view_x * view_z, sh_third[4] * (square_x - square_y), sh_fourth[0] * view_y * (3.0 * square_x - square_y), sh_fourth[1] * view_x * view_y * view_z, sh_fourth[2] * view_y * (4.0 * square_z - square_x - square_y), sh_fourth[3] * view_z * (2.0 * square_z - 3.0 * square_x - 3.0 * square_y), sh_fourth[4] * view_x * (4.0 * square_z - square_x - square_y), sh_fourth[5] * view_z * (square_x - square_y), sh_fourth[6] * view_x * (square_x - 3.0 * square_y)])

def project(params, camera):
    trailing = params.shape[1:]
    mean_x, mean_y, mean_z = (params[0], params[1], params[2])
    screen_x = camera[0] * mean_x + camera[1] * mean_y + camera[2] * mean_z + camera[6]
    screen_y = camera[3] * mean_x + camera[4] * mean_y + camera[5] * mean_z + camera[7]
    quat_norm = jnp.sqrt(params[6] * params[6] + params[7] * params[7] + params[8] * params[8] + params[9] * params[9])
    unit_w = params[6] / quat_norm
    unit_x = params[7] / quat_norm
    unit_y = params[8] / quat_norm
    unit_z = params[9] / quat_norm
    rotation = ((1.0 - 2.0 * (unit_y * unit_y + unit_z * unit_z), 2.0 * (unit_x * unit_y - unit_w * unit_z), 2.0 * (unit_x * unit_z + unit_w * unit_y)), (2.0 * (unit_x * unit_y + unit_w * unit_z), 1.0 - 2.0 * (unit_x * unit_x + unit_z * unit_z), 2.0 * (unit_y * unit_z - unit_w * unit_x)), (2.0 * (unit_x * unit_z - unit_w * unit_y), 2.0 * (unit_y * unit_z + unit_w * unit_x), 1.0 - 2.0 * (unit_x * unit_x + unit_y * unit_y)))
    stretch = (jnp.exp(params[3]), jnp.exp(params[4]), jnp.exp(params[5]))

    def image_row(first_coef, second_coef, third_coef):
        return [(first_coef * rotation[0][col_idx] + second_coef * rotation[1][col_idx] + third_coef * rotation[2][col_idx]) * stretch[col_idx] for col_idx in range(3)]
    upper_row = image_row(camera[0], camera[1], camera[2])
    lower_row = image_row(camera[3], camera[4], camera[5])
    cov_xx = upper_row[0] * upper_row[0] + upper_row[1] * upper_row[1] + upper_row[2] * upper_row[2] + dilation
    cov_xy = upper_row[0] * lower_row[0] + upper_row[1] * lower_row[1] + upper_row[2] * lower_row[2]
    cov_yy = lower_row[0] * lower_row[0] + lower_row[1] * lower_row[1] + lower_row[2] * lower_row[2] + dilation
    determinant = cov_xx * cov_yy - cov_xy * cov_xy
    base_opacity = jax.nn.sigmoid(params[10])
    harmonics = harmonic_values(camera).reshape((1, 16) + (1,) * len(trailing))
    coeffs = params[11:59].reshape((3, 16) + trailing)
    colours = 0.5 + lax.optimization_barrier(jnp.sum(coeffs * harmonics, axis=1))
    return jnp.stack([screen_x, screen_y, cov_yy / determinant, -cov_xy / determinant, cov_xx / determinant, base_opacity, colours[0], colours[1], colours[2]], axis=0)

def render_tile(features, live_count, tile_number, height):
    entries = features.shape[1]
    pixel = jnp.arange(TILE_SIDE * TILE_SIDE, dtype=jnp.int32)
    tile_col = tile_number % TW
    tile_row = tile_number // TW
    pixel_x = (TILE_SIDE * tile_col + pixel % TILE_SIDE).astype(jnp.float32) + 0.5 - 0.5 * TILE_SIDE * TW
    pixel_y = (TILE_SIDE * tile_row + pixel // TILE_SIDE).astype(jnp.float32) + 0.5 - 0.5 * height
    delta_x = pixel_x[:, None] - features[0][None, :]
    delta_y = pixel_y[:, None] - features[1][None, :]
    power = -0.5 * (features[2][None, :] * delta_x * delta_x + features[4][None, :] * delta_y * delta_y) - features[3][None, :] * delta_x * delta_y
    live = jnp.arange(entries, dtype=jnp.int32) < live_count
    alpha = jnp.where(live[None, :], features[5][None, :] * jnp.exp(power), jnp.float32(0.0))
    log_keep = jnp.log1p(-alpha)
    log_before = jnp.cumsum(log_keep, axis=1) - log_keep
    weights = alpha * jnp.exp(log_before)
    return jnp.einsum('ce,pe->cp', features[6:9], weights, precision=lax.Precision.HIGHEST)

def reference(means, log_scales, quat_w, quat_v, opacity, sh_coeffs, cameras, requests, lists, counts, image_cot):
    params = jnp.concatenate([means, log_scales, quat_w, quat_v, opacity, sh_coeffs], axis=0)
    owners = jnp.arange(N_IMG * N_TILE, dtype=jnp.int32).reshape(N_IMG, N_TILE)
    global_ids = (owners[None, None, :, :, None] * NG_DEV + requests).reshape(N_IMG, N_TILE, SLOTS)
    tile_owner = jnp.arange(TILES, dtype=jnp.int32) // TILES_DEV
    image_index = jnp.arange(N_IMG, dtype=jnp.int32)
    tile_ids = global_ids[image_index[:, None, None], tile_owner[None, :, None], lists]
    height = TILE_SIDE * TILES / TW
    numbers = jnp.tile(jnp.arange(TILES, dtype=jnp.int32), N_IMG)
    flat_counts = counts.reshape(-1)

    def render_packed(packed):
        return render_tile(packed[0], packed[1], packed[2], height)

    def forward(all_params, all_cameras):
        gathered = all_params[:, tile_ids]
        features = jax.vmap(project, in_axes=(1, 0), out_axes=1)(gathered, all_cameras)
        flat = features.transpose(1, 2, 0, 3).reshape(N_IMG * TILES, 9, LIST)
        images = lax.map(jax.checkpoint(render_packed), (flat, flat_counts, numbers))
        return images.reshape(N_IMG, TILES, 3, PIX).transpose(0, 2, 1, 3)
    rendered, pullback = jax.vjp(forward, params, cameras)
    param_grad, camera_grad = pullback(image_cot)
    return (rendered, param_grad, camera_grad)
```

```python
import functools
import math

import jax
import jax.numpy as jnp
from jax import lax
from jax.experimental import pallas as pl
from jax.experimental.pallas import tpu as pltpu
from jax.sharding import PartitionSpec as P

TILE_SIDE = 16
TW = 16
NFEAT = 9
NSENT = 24
NBACK = 16
F32 = jnp.float32
BF16 = jnp.bfloat16
MESH = pl.DeviceIdType.MESH

sh_first = 0.28209479177387814
sh_second = 0.4886025119029199
sh_third = (
    1.0925484305920792,
    -1.0925484305920792,
    0.31539156525252005,
    -1.0925484305920792,
    0.5462742152960396,
)
sh_fourth = (
    -0.5900435899266435,
    2.890611442640554,
    -0.4570457994644658,
    0.3731763325901154,
    -0.4570457994644658,
    1.445305721320277,
    -0.5900435899266435,
)
dilation = 0.3


def harmonics(x, y, z):
    xx, yy, zz = x * x, y * y, z * z
    zero = jnp.zeros_like(x)
    a, b = sh_third, sh_fourth
    c = sh_second
    values = [
        zero + sh_first,
        -c * y,
        c * z,
        -c * x,
        a[0] * x * y,
        a[1] * y * z,
        a[2] * (2.0 * zz - xx - yy),
        a[3] * x * z,
        a[4] * (xx - yy),
        b[0] * y * (3.0 * xx - yy),
        b[1] * x * y * z,
        b[2] * y * (4.0 * zz - xx - yy),
        b[3] * z * (2.0 * zz - 3.0 * xx - 3.0 * yy),
        b[4] * x * (4.0 * zz - xx - yy),
        b[5] * z * (xx - yy),
        b[6] * x * (xx - 3.0 * yy),
    ]
    by_x = [
        zero,
        zero,
        zero,
        zero - c,
        a[0] * y,
        zero,
        -2.0 * a[2] * x,
        a[3] * z,
        2.0 * a[4] * x,
        6.0 * b[0] * x * y,
        b[1] * y * z,
        -2.0 * b[2] * x * y,
        -6.0 * b[3] * x * z,
        b[4] * (4.0 * zz - 3.0 * xx - yy),
        2.0 * b[5] * x * z,
        b[6] * (3.0 * xx - 3.0 * yy),
    ]
    by_y = [
        zero,
        zero - c,
        zero,
        zero,
        a[0] * x,
        a[1] * z,
        -2.0 * a[2] * y,
        zero,
        -2.0 * a[4] * y,
        b[0] * (3.0 * xx - 3.0 * yy),
        b[1] * x * z,
        b[2] * (4.0 * zz - xx - 3.0 * yy),
        -6.0 * b[3] * y * z,
        -2.0 * b[4] * x * y,
        -2.0 * b[5] * y * z,
        -6.0 * b[6] * x * y,
    ]
    by_z = [
        zero,
        zero,
        zero + c,
        zero,
        zero,
        a[1] * y,
        4.0 * a[2] * z,
        a[3] * x,
        zero,
        zero,
        b[1] * x * y,
        8.0 * b[2] * y * z,
        b[3] * (6.0 * zz - 3.0 * xx - 3.0 * yy),
        8.0 * b[4] * x * z,
        b[5] * (xx - yy),
        zero,
    ]
    return values, by_x, by_y, by_z


def split(value, parts):
    terms, rest = [], value
    for at in range(parts):
        term = rest.astype(BF16).astype(F32)
        terms.append(term)
        if at < parts - 1:
            rest = rest - term
    return terms


def dot(a, b):
    return jnp.dot(a, b, preferred_element_type=F32)


def dot_nt(a, b):
    return lax.dot_general(a, b, (((1,), (1,)), ((), ())), preferred_element_type=F32)


def conic(cam, sigma):
    a0, a1 = cam[0:3], cam[3:6]

    def times(a):
        return (
            a[0] * sigma[0] + a[1] * sigma[1] + a[2] * sigma[2],
            a[0] * sigma[1] + a[1] * sigma[3] + a[2] * sigma[4],
            a[0] * sigma[2] + a[1] * sigma[4] + a[2] * sigma[5],
        )

    v0, v1 = times(a0), times(a1)
    s00 = a0[0] * v0[0] + a0[1] * v0[1] + a0[2] * v0[2] + dilation
    s01 = a1[0] * v0[0] + a1[1] * v0[1] + a1[2] * v0[2]
    s11 = a1[0] * v1[0] + a1[1] * v1[1] + a1[2] * v1[2] + dilation
    inverse = 1.0 / (s00 * s11 - s01 * s01)
    return v0, v1, (s11 * inverse, -s01 * inverse, s00 * inverse)


def cov_grad(con, grad):
    ca, cb, cc = con
    ga, gb, gc = grad[0], 0.5 * grad[1], grad[2]
    p00, p01 = ca * ga + cb * gb, ca * gb + cb * gc
    p10, p11 = cb * ga + cc * gb, cb * gb + cc * gc
    return (
        -(p00 * ca + p01 * cb),
        -(p00 * cb + p01 * cc),
        -(p10 * cb + p11 * cc),
    )


def rotation_of(quat):
    w, x, y, z = quat
    return (
        (1.0 - 2.0 * (y * y + z * z), 2.0 * (x * y - w * z), 2.0 * (x * z + w * y)),
        (2.0 * (x * y + w * z), 1.0 - 2.0 * (x * x + z * z), 2.0 * (y * z - w * x)),
        (2.0 * (x * z - w * y), 2.0 * (y * z + w * x), 1.0 - 2.0 * (x * x + y * y)),
    )


def kernel(
    sizes,
    means,
    log_scales,
    quat_w,
    quat_v,
    opacity,
    sh,
    cams,
    requests,
    lists,
    counts,
    cot,
    rendered,
    param_grad,
    camera_grad,
    ask_recv,
    feat_send,
    feat_recv,
    grad_send,
    grad_recv,
    column,
    asked,
    picked,
    slot_grads,
    slots,
    feats,
    chosen,
    entry,
    entry_grad,
    harm,
    send_sem,
    recv_sem,
    own_sem,
):
    n_img, n_tile, cap, tiles_here, length, pix = sizes
    owned = means.shape[1]
    devices = n_img * n_tile
    n_slots = devices * cap
    per_img = n_tile * cap
    my_tile = lax.axis_index("tile")
    me = lax.axis_index("img") * n_tile + my_tile

    def peer(k):
        other = lax.rem(me + k, devices)
        return other, (other // n_tile, lax.rem(other, n_tile))

    barrier = pltpu.get_barrier_semaphore()

    @pl.loop(1, devices)
    def _(k):
        pl.semaphore_signal(barrier, inc=1, device_id=peer(k)[1], device_id_type=MESH)

    pl.semaphore_wait(barrier, devices - 1)

    def exchange(at, source, target):
        mine = pltpu.make_async_copy(source.at[me], target.at[me], own_sem.at[at])
        mine.start()

        @pl.loop(1, devices)
        def _(k):
            other, where = peer(k)
            pltpu.make_async_remote_copy(
                src_ref=source.at[other],
                dst_ref=target.at[me],
                send_sem=send_sem.at[at],
                recv_sem=recv_sem.at[at],
                device_id=where,
                device_id_type=MESH,
            ).start()

        return mine

    def arrive(at, target, mine):
        mine.wait()
        others = target.at[pl.ds(0, devices - 1)]
        pltpu.make_async_copy(others, others, recv_sem.at[at]).wait()

    def sent(at, source):
        others = source.at[pl.ds(0, devices - 1)]
        pltpu.make_async_copy(others, others, send_sem.at[at]).wait()

    asking = exchange(0, requests, ask_recv)

    cam = [[cams[i, c] for c in range(10)] for i in range(n_img)]
    row16 = lax.broadcasted_iota(jnp.int32, (16, 128), 0)
    for i in range(n_img):
        polar = jnp.full((16, 128), cam[i][8], F32)
        azimuth = jnp.full((16, 128), cam[i][9], F32)
        sp, cp = jnp.sin(polar), jnp.cos(polar)
        sz, cz = jnp.sin(azimuth), jnp.cos(azimuth)
        values, by_x, by_y, by_z = harmonics(sp * cz, sp * sz, cp)
        y_col = jnp.zeros((16, 128), F32)
        p_col = jnp.zeros((16, 128), F32)
        z_col = jnp.zeros((16, 128), F32)
        for m in range(16):
            here = row16 == m
            y_col = jnp.where(here, values[m], y_col)
            p_col = jnp.where(here, by_x[m] * cp * cz + by_y[m] * cp * sz - by_z[m] * sp, p_col)
            z_col = jnp.where(here, -by_x[m] * sp * sz + by_y[m] * sp * cz, z_col)
        harm[i, 0] = y_col
        harm[i, 1] = p_col
        harm[i, 2] = z_col

    def geometry():
        w, v = quat_w[...], quat_v[...]
        raw = (w, v[0:1], v[1:2], v[2:3])
        inverse = 1.0 / jnp.sqrt(
            raw[0] * raw[0] + raw[1] * raw[1] + raw[2] * raw[2] + raw[3] * raw[3]
        )
        quat = tuple(part * inverse for part in raw)
        rot = rotation_of(quat)
        wide = jnp.exp(2.0 * log_scales[...])
        squares = (wide[0:1], wide[1:2], wide[2:3])
        return quat, inverse, rot, squares

    quat, inverse, rot, squares = geometry()

    def sigma_entry(a, b):
        return (
            rot[a][0] * rot[b][0] * squares[0]
            + rot[a][1] * rot[b][1] * squares[1]
            + rot[a][2] * rot[b][2] * squares[2]
        )

    sigma = tuple(sigma_entry(a, b) for a, b in ((0, 0), (0, 1), (0, 2), (1, 1), (1, 2), (2, 2)))
    mean = tuple(means[a : a + 1, :] for a in range(3))
    base = 1.0 / (1.0 + jnp.exp(-opacity[...]))
    for i in range(n_img):
        c = cam[i]
        _, _, con = conic(c, sigma)
        rows = [
            c[0] * mean[0] + c[1] * mean[1] + c[2] * mean[2] + c[6],
            c[3] * mean[0] + c[4] * mean[1] + c[5] * mean[2] + c[7],
            con[0],
            con[1],
            con[2],
            base,
        ]
        for d in range(3):
            col = harm[i, d][:, 0:1]
            for k in range(3):
                total = jnp.sum(sh[16 * k : 16 * k + 16, :] * col, axis=0, keepdims=True)
                rows.append(total + 0.5 if d == 0 else total)
            if d == 0:
                rows += list(mean) + list(sigma)
        for at, row in enumerate(rows):
            picked[at : at + 1, :] = row
        for at, term in enumerate(split(picked[...], 3)):
            feats[i, NSENT * at : NSENT * (at + 1), :] = term

    slot_iota = lax.broadcasted_iota(jnp.int32, (n_slots, length), 0)
    for j in range(tiles_here):
        chosen[j] = (slot_iota == lists[j : j + 1, :]).astype(F32).astype(BF16)

    arrive(0, ask_recv, asking)
    asks = ask_recv[...].reshape(devices, cap)
    for c in range(cap):
        column[pl.ds(c, devices, stride=cap), 0:1] = asks[:, c : c + 1]
    own_iota = lax.broadcasted_iota(jnp.int32, (per_img, owned), 1)
    for i in range(n_img):
        mask = (own_iota == column[i * per_img : (i + 1) * per_img, 0:1]).astype(F32).astype(BF16)
        asked[i] = mask
        three = dot_nt(mask, feats[i].astype(BF16))
        slots[i * per_img : (i + 1) * per_img, 0:NSENT] = (
            three[:, 0:NSENT] + three[:, NSENT : 2 * NSENT] + three[:, 2 * NSENT : 3 * NSENT]
        )
    feat_send[...] = jnp.concatenate(
        [slots[pl.ds(c, devices, stride=cap), 0:NSENT] for c in range(cap)], axis=1
    ).reshape(devices, 1, cap * NSENT)
    sending = exchange(1, feat_send, feat_recv)

    pixel = lax.broadcasted_iota(jnp.int32, (pix, 24), 0)
    which = lax.rem(lax.broadcasted_iota(jnp.int32, (pix, 24), 1), 8)
    half = 0.5 * TILE_SIDE - 0.5

    def basis_of(pixel, which):
        x = lax.rem(pixel, TILE_SIDE).astype(F32) - half
        y = (pixel // TILE_SIDE).astype(F32) - half
        out = jnp.where(which == 0, 1.0, 0.0)
        for at, term in enumerate((x, y, x * x, x * y, y * y)):
            out = jnp.where(which == at + 1, term, out)
        return out.astype(BF16)

    basis_pe = basis_of(pixel, which)
    basis_ep = basis_of(
        lax.broadcasted_iota(jnp.int32, (16, pix), 1), lax.broadcasted_iota(jnp.int32, (16, pix), 0)
    )
    first = lax.broadcasted_iota(jnp.int32, (length, length), 0)
    second = lax.broadcasted_iota(jnp.int32, (length, length), 1)
    before = (first < second).astype(F32).astype(BF16)
    after = (first > second).astype(F32).astype(BF16)
    height = TILE_SIDE * tiles_here * n_tile / TW
    lane = lax.broadcasted_iota(jnp.int32, (1, length), 1)
    arrive(1, feat_recv, sending)
    packed = feat_recv[...].reshape(devices, cap * NSENT)
    for c in range(cap):
        slots[pl.ds(c, devices, stride=cap), 0:NSENT] = packed[:, c * NSENT : (c + 1) * NSENT]
    by_slot = jnp.transpose(slots[...])[0:NSENT, :]
    three = jnp.concatenate(split(by_slot[0:16], 3), axis=0).astype(BF16)

    @pl.loop(0, tiles_here)
    def _(j):
        number = my_tile * tiles_here + j
        centre_x = (lax.rem(number, TW) * TILE_SIDE).astype(F32) + 0.5 * TILE_SIDE * (1 - TW)
        centre_y = (number // TW * TILE_SIDE).astype(F32) + 0.5 * TILE_SIDE - 0.5 * height
        mask = chosen[j]
        got = dot(three, mask)
        got = got[0:16] + got[16:32] + got[32:48]
        lx, ly = got[0:1] - centre_x, got[1:2] - centre_y
        ca, cb, cc, op = got[2:3], got[3:4], got[4:5], got[5:6]
        ux = ca * lx + cb * ly
        uy = cc * ly + cb * lx
        entry[...] = jnp.zeros_like(entry)
        for at, row in enumerate(
            (-0.5 * (ux * lx + uy * ly), ux, uy, -0.5 * ca, -cb, -0.5 * cc)
        ):
            entry[at : at + 1, :] = row
        power = dot(basis_pe, jnp.concatenate(split(entry[...], 3), axis=0).astype(BF16))
        live = lane < counts[0, j]
        alpha = jnp.where(live, op, 0.0) * jnp.exp(power)
        keep = 1.0 - alpha
        log_keep = jnp.log(keep)
        hi = log_keep.astype(BF16)
        lo = (log_keep - hi.astype(F32)).astype(BF16)
        through = jnp.exp(dot(hi, before) + dot(lo, before))
        weight = alpha * through
        colour = jnp.concatenate(split(got[6:9], 2), axis=0)
        hi = weight.astype(BF16)
        lo = (weight - hi.astype(F32)).astype(BF16)
        colour_b = colour.astype(BF16)
        image = dot_nt(colour_b, hi) + dot_nt(colour_b, lo)
        cots = [cot[0, k, pl.ds(j, 1), :] for k in range(3)]
        for k in range(3):
            rendered[0, k, pl.ds(j, 1), :] = image[k : k + 1] + image[k + 3 : k + 4]
        cot3 = jnp.concatenate(cots, axis=0)
        c1, c2, c3 = split(cot3, 3)
        k1, k2, k3 = split(got[6:9], 3)
        left = jnp.concatenate([c1, c1, c2, c2, c1, c3, jnp.zeros((110, pix), F32)], axis=0)
        right = jnp.concatenate([k1, k2, k1, k2, k3, k1, jnp.zeros((110, length), F32)], axis=0)
        pull = dot(jnp.transpose(left).astype(BF16), right.astype(BF16))
        pulled = pull * weight
        hi = pulled.astype(BF16)
        lo = (pulled - hi.astype(F32)).astype(BF16)
        later = dot(hi, after) + dot(lo, after)
        force = pulled - later * (alpha / keep)
        d1 = force.astype(BF16)
        rest = force - d1.astype(F32)
        d2 = rest.astype(BF16)
        d3 = (rest - d2.astype(F32)).astype(BF16)
        moments = dot(basis_ep, d1) + dot(basis_ep, d2) + dot(basis_ep, d3)
        m0, mx, my = moments[0:1], moments[1:2], moments[2:3]
        nx, ny = mx - lx * m0, my - ly * m0
        nxx = moments[3:4] - 2.0 * lx * mx + lx * lx * m0
        nxy = moments[4:5] - lx * my - ly * mx + lx * ly * m0
        nyy = moments[5:6] - 2.0 * ly * my + ly * ly * m0
        cot_hi = jnp.concatenate([c1, c2, jnp.zeros((10, pix), F32)], axis=0).astype(BF16)
        by_colour = dot(cot_hi, weight.astype(BF16)) + dot(cot_hi, lo_of(weight))
        entry_grad[...] = jnp.zeros_like(entry_grad)
        for at, row in enumerate(
            (
                ca * nx + cb * ny,
                cc * ny + cb * nx,
                -0.5 * nxx,
                -nxy,
                -0.5 * nyy,
                m0 / op,
                by_colour[0:1] + by_colour[3:4],
                by_colour[1:2] + by_colour[4:5],
                by_colour[2:3] + by_colour[5:6],
            )
        ):
            entry_grad[at : at + 1, :] = row
        terms = jnp.concatenate(split(entry_grad[...], 2), axis=0).astype(BF16)
        back = dot_nt(terms, mask)
        back = back[0:NBACK] + back[NBACK : 2 * NBACK]

        @pl.when(j == 0)
        def _():
            slot_grads[...] = back

        @pl.when(j > 0)
        def _():
            slot_grads[...] += back

    my_img = lax.axis_index("img")
    grads = slot_grads[...]
    g = [grads[at : at + 1] for at in range(NFEAT)]
    f = [by_slot[at : at + 1] for at in range(NSENT)]
    c = [cams[my_img, at] for at in range(10)]
    v0, v1, _ = conic(c, f[12:18])
    h = cov_grad((f[2], f[3], f[4]), (g[2], g[3], g[4]))
    shares = [g[0] * f[9 + a] + 2.0 * (h[0] * v0[a] + h[1] * v1[a]) for a in range(3)]
    shares += [g[1] * f[9 + a] + 2.0 * (h[2] * v1[a] + h[1] * v0[a]) for a in range(3)]
    shares += [g[0], g[1]]
    shares += [sum(g[6 + k] * f[18 + 3 * d + k] for k in range(3)) for d in range(2)]
    slot_lane = lax.rem(lax.broadcasted_iota(jnp.int32, (1, n_slots), 1), cap)
    camera_row = jnp.zeros((1, n_slots), F32)
    for at, share in enumerate(shares):
        camera_row = jnp.where(slot_lane == at, jnp.sum(share, axis=1, keepdims=True), camera_row)
    slot_grads[NFEAT : NFEAT + 1, :] = camera_row
    slots[:, 0:NBACK] = jnp.transpose(slot_grads[...])
    grad_send[...] = jnp.concatenate(
        [slots[pl.ds(c, devices, stride=cap), 0:NBACK] for c in range(cap)], axis=1
    ).reshape(devices, 1, cap * NBACK)
    returning = exchange(2, grad_send, grad_recv)
    sent(0, ask_recv)
    sent(1, feat_send)
    arrive(2, grad_recv, returning)
    packed = grad_recv[...].reshape(devices, cap * NBACK)
    for c in range(cap):
        slots[pl.ds(c, devices, stride=cap), 0:NBACK] = packed[:, c * NBACK : (c + 1) * NBACK]
    by_slot = jnp.transpose(slots[...])[0:NBACK, :]

    g_mean = [0.0, 0.0, 0.0]
    g_base = 0.0
    g_sigma = [[0.0] * 3 for _ in range(3)]
    g_sh = [0.0, 0.0, 0.0]
    for i in range(n_img):
        mine = by_slot[:, i * per_img : (i + 1) * per_img]
        fold = mine[NFEAT : NFEAT + 1, 0:128]
        for at in range(128, per_img, 128):
            fold = fold + mine[NFEAT : NFEAT + 1, at : at + 128]
        shift = 64
        while shift >= cap:
            fold = fold + pltpu.roll(fold, shift, 1)
            shift //= 2
        camera_grad[i : i + 1, :] = fold[:, 0:10]
        terms = jnp.concatenate(split(mine, 2), axis=0).astype(BF16)
        full = dot(terms, asked[i])
        full = full[0:NBACK] + full[NBACK : 2 * NBACK]
        g = [full[at : at + 1] for at in range(NFEAT)]
        c = cam[i]
        _, _, con = conic(c, sigma)
        h = cov_grad(con, (g[2], g[3], g[4]))
        for a in range(3):
            g_mean[a] = g_mean[a] + c[a] * g[0] + c[3 + a] * g[1]
            for b in range(a, 3):
                g_sigma[a][b] = (
                    g_sigma[a][b]
                    + (c[a] * c[b]) * h[0]
                    + (c[a] * c[3 + b] + c[3 + a] * c[b]) * h[1]
                    + (c[3 + a] * c[3 + b]) * h[2]
                )
        g_base = g_base + g[5]
        col = harm[i, 0][:, 0:1]
        for k in range(3):
            g_sh[k] = g_sh[k] + col * g[6 + k]
    for a in range(3):
        param_grad[a : a + 1, :] = g_mean[a]
        for b in range(a):
            g_sigma[a][b] = g_sigma[b][a]
    g_rot = [[None] * 3 for _ in range(3)]
    for b in range(3):
        pull = [
            g_sigma[a][0] * rot[0][b] + g_sigma[a][1] * rot[1][b] + g_sigma[a][2] * rot[2][b]
            for a in range(3)
        ]
        twice = 2.0 * squares[b]
        for a in range(3):
            g_rot[a][b] = twice * pull[a]
        param_grad[3 + b : 4 + b, :] = (
            g_rot[0][b] * rot[0][b] + g_rot[1][b] * rot[1][b] + g_rot[2][b] * rot[2][b]
        )
    w, x, y, z = quat
    r = g_rot
    g_quat = (
        2.0 * (z * (r[1][0] - r[0][1]) + y * (r[0][2] - r[2][0]) + x * (r[2][1] - r[1][2])),
        2.0
        * (
            y * (r[0][1] + r[1][0])
            + z * (r[0][2] + r[2][0])
            + w * (r[2][1] - r[1][2])
            - 2.0 * x * (r[1][1] + r[2][2])
        ),
        2.0
        * (
            x * (r[0][1] + r[1][0])
            + z * (r[1][2] + r[2][1])
            + w * (r[0][2] - r[2][0])
            - 2.0 * y * (r[0][0] + r[2][2])
        ),
        2.0
        * (
            x * (r[0][2] + r[2][0])
            + y * (r[1][2] + r[2][1])
            + w * (r[1][0] - r[0][1])
            - 2.0 * z * (r[0][0] + r[1][1])
        ),
    )
    along = sum(quat[a] * g_quat[a] for a in range(4))
    for a in range(4):
        param_grad[6 + a : 7 + a, :] = (g_quat[a] - quat[a] * along) * inverse
    param_grad[10:11, :] = g_base * base * (1.0 - base)
    for k in range(3):
        param_grad[11 + 16 * k : 27 + 16 * k, :] = g_sh[k]
    sent(2, grad_send)


def lo_of(value):
    return (value - value.astype(BF16).astype(F32)).astype(BF16)


def local(
    means,
    log_scales,
    quat_w,
    quat_v,
    opacity,
    sh_coeffs,
    cameras,
    requests,
    lists,
    counts,
    image_cot,
):
    n_img, n_tile, cap = requests.shape[2:]
    devices = n_img * n_tile
    n_slots = devices * cap
    owned = means.shape[1]
    tiles_here, length = lists.shape[1:]
    pix = image_cot.shape[3]
    sizes = (n_img, n_tile, cap, tiles_here, length, pix)
    vmem = pl.BlockSpec(memory_space=pltpu.VMEM)
    smem = pl.BlockSpec(memory_space=pltpu.SMEM)
    rows = sum(part.shape[0] for part in (means, log_scales, quat_w, quat_v, opacity, sh_coeffs))
    return pl.pallas_call(
        functools.partial(kernel, sizes),
        out_shape=(
            jax.ShapeDtypeStruct(image_cot.shape, F32),
            jax.ShapeDtypeStruct((rows, owned), F32),
            jax.ShapeDtypeStruct(cameras.shape, F32),
        ),
        in_specs=[vmem] * 6 + [smem, vmem, vmem, smem, vmem],
        out_specs=(vmem, vmem, vmem),
        scratch_shapes=[
            pltpu.VMEM((devices, 1, cap), jnp.int32),
            pltpu.VMEM((devices, 1, cap * NSENT), F32),
            pltpu.VMEM((devices, 1, cap * NSENT), F32),
            pltpu.VMEM((devices, 1, cap * NBACK), F32),
            pltpu.VMEM((devices, 1, cap * NBACK), F32),
            pltpu.VMEM((n_slots, 128), jnp.int32),
            pltpu.VMEM((n_img, n_tile * cap, owned), BF16),
            pltpu.VMEM((NSENT, owned), F32),
            pltpu.VMEM((NBACK, n_slots), F32),
            pltpu.VMEM((n_slots, 128), F32),
            pltpu.VMEM((n_img, 3 * NSENT, owned), F32),
            pltpu.VMEM((tiles_here, n_slots, length), BF16),
            pltpu.VMEM((8, length), F32),
            pltpu.VMEM((NBACK, length), F32),
            pltpu.VMEM((n_img, 3, 16, 128), F32),
            pltpu.SemaphoreType.DMA((3,)),
            pltpu.SemaphoreType.DMA((3,)),
            pltpu.SemaphoreType.DMA((3,)),
        ],
        compiler_params=pltpu.CompilerParams(
            collective_id=0, has_side_effects=True, vmem_limit_bytes=60 * 1024 * 1024
        ),
    )(
        means,
        log_scales,
        quat_w,
        quat_v,
        opacity,
        sh_coeffs,
        cameras,
        requests.reshape(devices, 1, cap),
        lists[0],
        counts,
        image_cot,
    )


def solution(mesh):
    owners = P(None, ("img", "tile"))
    images = P("img", None, "tile", None)
    return jax.shard_map(
        local,
        mesh=mesh,
        in_specs=(owners,) * 6
        + (P(), P("img", "tile", None, None, None), P("img", "tile", None), P("img", "tile"), images),
        out_specs=(images, owners, P()),
        check_vma=False,
    )
```

```python
import functools
import math

import jax
import jax.numpy as jnp
from jax import lax
from jax.experimental import pallas as pl
from jax.experimental.pallas import tpu as pltpu
from jax.sharding import PartitionSpec as P

TILE_SIDE = 16
TW = 16
NFEAT = 9
NSENT = 24
NBACK = 16
LANES = 128
F32 = jnp.float32
BF16 = jnp.bfloat16
MESH = pl.DeviceIdType.MESH

sh_first = 0.28209479177387814
sh_second = 0.4886025119029199
sh_third = (
    1.0925484305920792,
    -1.0925484305920792,
    0.31539156525252005,
    -1.0925484305920792,
    0.5462742152960396,
)
sh_fourth = (
    -0.5900435899266435,
    2.890611442640554,
    -0.4570457994644658,
    0.3731763325901154,
    -0.4570457994644658,
    1.445305721320277,
    -0.5900435899266435,
)
dilation = 0.3


def harmonics(x, y, z):
    xx, yy, zz = x * x, y * y, z * z
    zero = jnp.zeros_like(x)
    a, b = sh_third, sh_fourth
    c = sh_second
    values = [
        zero + sh_first,
        -c * y,
        c * z,
        -c * x,
        a[0] * x * y,
        a[1] * y * z,
        a[2] * (2.0 * zz - xx - yy),
        a[3] * x * z,
        a[4] * (xx - yy),
        b[0] * y * (3.0 * xx - yy),
        b[1] * x * y * z,
        b[2] * y * (4.0 * zz - xx - yy),
        b[3] * z * (2.0 * zz - 3.0 * xx - 3.0 * yy),
        b[4] * x * (4.0 * zz - xx - yy),
        b[5] * z * (xx - yy),
        b[6] * x * (xx - 3.0 * yy),
    ]
    by_x = [
        zero,
        zero,
        zero,
        zero - c,
        a[0] * y,
        zero,
        -2.0 * a[2] * x,
        a[3] * z,
        2.0 * a[4] * x,
        6.0 * b[0] * x * y,
        b[1] * y * z,
        -2.0 * b[2] * x * y,
        -6.0 * b[3] * x * z,
        b[4] * (4.0 * zz - 3.0 * xx - yy),
        2.0 * b[5] * x * z,
        b[6] * (3.0 * xx - 3.0 * yy),
    ]
    by_y = [
        zero,
        zero - c,
        zero,
        zero,
        a[0] * x,
        a[1] * z,
        -2.0 * a[2] * y,
        zero,
        -2.0 * a[4] * y,
        b[0] * (3.0 * xx - 3.0 * yy),
        b[1] * x * z,
        b[2] * (4.0 * zz - xx - 3.0 * yy),
        -6.0 * b[3] * y * z,
        -2.0 * b[4] * x * y,
        -2.0 * b[5] * y * z,
        -6.0 * b[6] * x * y,
    ]
    by_z = [
        zero,
        zero,
        zero + c,
        zero,
        zero,
        a[1] * y,
        4.0 * a[2] * z,
        a[3] * x,
        zero,
        zero,
        b[1] * x * y,
        8.0 * b[2] * y * z,
        b[3] * (6.0 * zz - 3.0 * xx - 3.0 * yy),
        8.0 * b[4] * x * z,
        b[5] * (xx - yy),
        zero,
    ]
    return values, by_x, by_y, by_z


def split(value, parts):
    terms, rest = [], value
    for at in range(parts):
        term = rest.astype(BF16).astype(F32)
        terms.append(term)
        if at < parts - 1:
            rest = rest - term
    return terms


def dot(a, b):
    return jnp.dot(a, b, preferred_element_type=F32)


def dot_nt(a, b):
    return lax.dot_general(a, b, (((1,), (1,)), ((), ())), preferred_element_type=F32)


def conic(cam, sigma):
    a0, a1 = cam[0:3], cam[3:6]

    def times(a):
        return (
            a[0] * sigma[0] + a[1] * sigma[1] + a[2] * sigma[2],
            a[0] * sigma[1] + a[1] * sigma[3] + a[2] * sigma[4],
            a[0] * sigma[2] + a[1] * sigma[4] + a[2] * sigma[5],
        )

    v0, v1 = times(a0), times(a1)
    s00 = a0[0] * v0[0] + a0[1] * v0[1] + a0[2] * v0[2] + dilation
    s01 = a1[0] * v0[0] + a1[1] * v0[1] + a1[2] * v0[2]
    s11 = a1[0] * v1[0] + a1[1] * v1[1] + a1[2] * v1[2] + dilation
    inverse = 1.0 / (s00 * s11 - s01 * s01)
    return v0, v1, (s11 * inverse, -s01 * inverse, s00 * inverse)


def cov_grad(con, grad):
    ca, cb, cc = con
    ga, gb, gc = grad[0], 0.5 * grad[1], grad[2]
    p00, p01 = ca * ga + cb * gb, ca * gb + cb * gc
    p10, p11 = cb * ga + cc * gb, cb * gb + cc * gc
    return (
        -(p00 * ca + p01 * cb),
        -(p00 * cb + p01 * cc),
        -(p10 * cb + p11 * cc),
    )


def rotation_of(quat):
    w, x, y, z = quat
    return (
        (1.0 - 2.0 * (y * y + z * z), 2.0 * (x * y - w * z), 2.0 * (x * z + w * y)),
        (2.0 * (x * y + w * z), 1.0 - 2.0 * (x * x + z * z), 2.0 * (y * z - w * x)),
        (2.0 * (x * z - w * y), 2.0 * (y * z + w * x), 1.0 - 2.0 * (x * x + y * y)),
    )


def load_dense(refs, dense):
    at = 0
    for ref in refs:
        rows, owned = ref.shape
        high = owned // LANES
        for h in range(high):
            part = ref[:, h * LANES : (h + 1) * LANES]
            if rows == 1:
                dense[at * high + h : at * high + h + 1, :] = part
            else:
                dense[pl.ds(at * high + h, rows, stride=high), :] = part
        at += rows


def geometry(row):
    raw = tuple(row(6 + a) for a in range(4))
    inverse = 1.0 / jnp.sqrt(
        raw[0] * raw[0] + raw[1] * raw[1] + raw[2] * raw[2] + raw[3] * raw[3]
    )
    quat = tuple(part * inverse for part in raw)
    rot = rotation_of(quat)
    squares = tuple(jnp.exp(2.0 * row(3 + a)) for a in range(3))

    def entry(a, b):
        return (
            rot[a][0] * rot[b][0] * squares[0]
            + rot[a][1] * rot[b][1] * squares[1]
            + rot[a][2] * rot[b][2] * squares[2]
        )

    sigma = tuple(entry(a, b) for a, b in ((0, 0), (0, 1), (0, 2), (1, 1), (1, 2), (2, 2)))
    return quat, inverse, rot, squares, sigma


def mask_of(index, rows):
    return lax.broadcasted_iota(jnp.int32, (rows, index.shape[1]), 0) == index


def as_bf16(mask):
    return mask.astype(F32).astype(BF16)


def two(value):
    hi = value.astype(BF16)
    return hi, (value - hi.astype(F32)).astype(BF16)


def scatter_rows(ref, start, stride, value):
    for h in range(ref.shape[0]):
        ref[h, pl.ds(start, value.shape[0], stride=stride), :] = value[
            :, h * LANES : (h + 1) * LANES
        ]


def take_rows(ref, rows):
    return jnp.concatenate([ref[h, rows, :] for h in range(ref.shape[0])], axis=1)


def render_kernel(
    sizes,
    means,
    log_scales,
    quat_w,
    quat_v,
    opacity,
    sh,
    cams,
    requests,
    lists,
    counts,
    cot,
    rendered,
    back_out,
    ask_out,
    harm_out,
    ask_recv,
    feat_send,
    feat_recv,
    grad_send,
    grad_recv,
    dense,
    project,
    feats,
    slots,
    by_slot,
    low,
    gots,
    coefs,
    colours,
    cots,
    cots_t,
    live_op,
    moments,
    tints,
    grads,
    harm,
    send_sem,
    recv_sem,
    own_sem,
):
    n_img, n_tile, cap, tiles_here, length, pix = sizes
    owned = means.shape[1]
    high = owned // LANES
    devices = n_img * n_tile
    n_slots = devices * cap
    groups = n_slots // LANES
    per_img = n_tile * cap
    my_tile = lax.axis_index("tile")
    my_img = lax.axis_index("img")
    me = my_img * n_tile + my_tile

    def peer(k):
        other = lax.rem(me + k, devices)
        return other, (other // n_tile, lax.rem(other, n_tile))

    barrier = pltpu.get_barrier_semaphore()

    @pl.loop(1, devices)
    def _(k):
        pl.semaphore_signal(barrier, inc=1, device_id=peer(k)[1], device_id_type=MESH)

    def exchange(at, source, target):
        mine = pltpu.make_async_copy(source.at[me], target.at[me], own_sem.at[at])
        mine.start()

        @pl.loop(1, devices)
        def _(k):
            other, where = peer(k)
            pltpu.make_async_remote_copy(
                src_ref=source.at[other],
                dst_ref=target.at[me],
                send_sem=send_sem.at[at],
                recv_sem=recv_sem.at[at],
                device_id=where,
                device_id_type=MESH,
            ).start()

        return mine

    def arrive(at, target, mine):
        mine.wait()
        others = target.at[pl.ds(0, devices - 1)]
        pltpu.make_async_copy(others, others, recv_sem.at[at]).wait()

    def sent(at, source):
        others = source.at[pl.ds(0, devices - 1)]
        pltpu.make_async_copy(others, others, send_sem.at[at]).wait()

    load_dense((means, log_scales, quat_w, quat_v, opacity, sh), dense)
    cam = [[cams[i, c] for c in range(10)] for i in range(n_img)]
    row16 = lax.broadcasted_iota(jnp.int32, (16, LANES), 0)
    for i in range(n_img):
        polar = jnp.full((16, LANES), cam[i][8], F32)
        azimuth = jnp.full((16, LANES), cam[i][9], F32)
        sp, cp = jnp.sin(polar), jnp.cos(polar)
        sz, cz = jnp.sin(azimuth), jnp.cos(azimuth)
        values, by_x, by_y, by_z = harmonics(sp * cz, sp * sz, cp)
        y_col = jnp.zeros((16, LANES), F32)
        p_col = jnp.zeros((16, LANES), F32)
        z_col = jnp.zeros((16, LANES), F32)
        for m in range(16):
            here = row16 == m
            y_col = jnp.where(here, values[m], y_col)
            p_col = jnp.where(here, by_x[m] * cp * cz + by_y[m] * cp * sz - by_z[m] * sp, p_col)
            z_col = jnp.where(here, -by_x[m] * sp * sz + by_y[m] * sp * cz, z_col)
        harm[i, 0] = y_col
        harm[i, 1] = p_col
        harm[i, 2] = z_col
        harm_out[i] = y_col

    pl.semaphore_wait(barrier, devices - 1)
    asking = exchange(0, requests, ask_recv)

    def row(at):
        return dense[at * high : (at + 1) * high, :]

    _, _, _, _, sigma = geometry(row)
    mean = tuple(row(a) for a in range(3))
    base = 1.0 / (1.0 + jnp.exp(-row(10)))
    for i in range(n_img):
        c = cam[i]
        _, _, con = conic(c, sigma)
        rows = [
            c[0] * mean[0] + c[1] * mean[1] + c[2] * mean[2] + c[6],
            c[3] * mean[0] + c[4] * mean[1] + c[5] * mean[2] + c[7],
            con[0],
            con[1],
            con[2],
            base,
        ]
        sums = [[None] * 3 for _ in range(3)]
        for k in range(3):
            for m in range(16):
                coeff = row(11 + 16 * k + m)
                for d in range(3):
                    term = coeff * harm[i, d, m : m + 1, :]
                    sums[d][k] = term if m == 0 else sums[d][k] + term
        rows += [total + 0.5 for total in sums[0]] + list(mean) + list(sigma) + sums[1] + sums[2]
        for at, value in enumerate(rows):
            project[pl.ds(at, high, stride=NSENT), :] = value
        for at, term in enumerate(split(project[0 : high * NSENT, :], 3)):
            feats[i, :, at * LANES : (at + 1) * LANES] = term.astype(BF16)

    coefs[...] = jnp.zeros_like(coefs)
    colours[...] = jnp.zeros_like(colours)
    for j in range(tiles_here):
        low[j] = as_bf16(mask_of(jnp.bitwise_and(lists[j : j + 1, :], LANES - 1), LANES))
        cot3 = jnp.concatenate([cot[0, k, j : j + 1, :] for k in range(3)], axis=0)
        c1, c2, c3 = split(cot3, 3)
        stack = jnp.concatenate([c1, c1, c2, c2, c1, c3, jnp.zeros((14, pix), F32)], axis=0)
        cots[j] = stack.astype(BF16)
        cots_t[j] = jnp.transpose(stack).astype(BF16)

    def basis_of(pixel, which):
        half = 0.5 * TILE_SIDE - 0.5
        x = lax.rem(pixel, TILE_SIDE).astype(F32) - half
        y = (pixel // TILE_SIDE).astype(F32) - half
        out = jnp.where(which == 0, 1.0, 0.0)
        for at, term in enumerate((x, y, x * x, x * y, y * y)):
            out = jnp.where(which == at + 1, term, out)
        return out.astype(BF16)

    basis_pe = basis_of(
        lax.broadcasted_iota(jnp.int32, (pix, 32), 0),
        lax.rem(lax.broadcasted_iota(jnp.int32, (pix, 32), 1), 8),
    )
    basis_ep = basis_of(
        lax.broadcasted_iota(jnp.int32, (16, pix), 1), lax.broadcasted_iota(jnp.int32, (16, pix), 0)
    )
    first = lax.broadcasted_iota(jnp.int32, (length, length), 0)
    second = lax.broadcasted_iota(jnp.int32, (length, length), 1)
    before = as_bf16(first < second)
    after = as_bf16(first > second)
    height = TILE_SIDE * tiles_here * n_tile / TW

    arrive(0, ask_recv, asking)
    asks = ask_recv[...].reshape(devices, cap)
    halves = jnp.concatenate(
        [(asks // LANES).astype(F32), jnp.bitwise_and(asks, LANES - 1).astype(F32)], axis=0
    ).astype(BF16)
    repeat = as_bf16(
        lax.rem(lax.broadcasted_iota(jnp.int32, (cap, n_slots), 1), cap)
        == lax.broadcasted_iota(jnp.int32, (cap, n_slots), 0)
    )
    wide = dot(halves, repeat)
    here = (
        lax.broadcasted_iota(jnp.int32, (devices, n_slots), 1) // cap
        == lax.broadcasted_iota(jnp.int32, (devices, n_slots), 0)
    )
    ask_hi, ask_lo = (
        jnp.sum(
            jnp.where(here, wide[at * devices : (at + 1) * devices], 0.0), axis=0, keepdims=True
        ).astype(jnp.int32)
        for at in range(2)
    )
    ask_out[0:1, :] = ask_hi
    ask_out[1:2, :] = ask_lo
    for i in range(n_img):
        lanes = slice(i * per_img, (i + 1) * per_img)
        mask = as_bf16(mask_of(ask_lo[:, lanes], LANES))
        got = dot(feats[i], jnp.concatenate([mask] * 3, axis=0))
        pick = mask_of(ask_hi[:, lanes], high).astype(F32)
        total = got[0:NSENT] * pick[0:1]
        for h in range(1, high):
            total = total + got[h * NSENT : (h + 1) * NSENT] * pick[h : h + 1]
        slots[lanes, 0:NSENT] = jnp.transpose(total)
    feat_send[...] = jnp.concatenate(
        [slots[pl.ds(c, devices, stride=cap), 0:NSENT] for c in range(cap)], axis=1
    ).reshape(devices, 1, cap * NSENT)
    sending = exchange(1, feat_send, feat_recv)
    sent(0, ask_recv)
    arrive(1, feat_recv, sending)
    packed = feat_recv[...].reshape(devices, cap * NSENT)
    for c in range(cap):
        slots[pl.ds(c, devices, stride=cap), 0:NSENT] = packed[:, c * NSENT : (c + 1) * NSENT]
    heads = []
    for h in range(groups):
        turned = jnp.transpose(slots[h * LANES : (h + 1) * LANES, :])[0:NSENT]
        by_slot[h * NSENT : (h + 1) * NSENT, :] = turned
        heads.append(turned[0:16])
    heads = jnp.concatenate(
        [term.astype(BF16) for term in split(jnp.concatenate(heads, axis=0), 3)], axis=1
    )

    for j in range(tiles_here):
        got = dot(heads, jnp.concatenate([low[j]] * 3, axis=0))
        group = lists[j : j + 1, :] // LANES
        total = jnp.where(group == 0, got[0:16], 0.0)
        for h in range(1, groups):
            total = total + jnp.where(group == h, got[h * 16 : (h + 1) * 16], 0.0)
        scatter_rows(gots, j, tiles_here, total)

    def feature(at):
        return take_rows(gots, slice(at * tiles_here, (at + 1) * tiles_here))

    tile_row = lax.broadcasted_iota(jnp.int32, (tiles_here, length), 0)
    number = my_tile * tiles_here + tile_row
    lx = feature(0) - (
        (lax.rem(number, TW) * TILE_SIDE).astype(F32) + 0.5 * TILE_SIDE * (1 - TW)
    )
    ly = feature(1) - ((number // TW * TILE_SIDE).astype(F32) + 0.5 * TILE_SIDE - 0.5 * height)
    ca, cb, cc, op = (feature(at) for at in range(2, 6))
    ux = ca * lx + cb * ly
    uy = cc * ly + cb * lx
    live = jnp.zeros((tiles_here, length), jnp.int32)
    for j in range(tiles_here):
        live = jnp.where(tile_row == j, counts[0, j], live)
    lane = lax.broadcasted_iota(jnp.int32, (tiles_here, length), 1)
    live_op[...] = jnp.where(lane < live, op, 0.0)
    for at, value in enumerate((-0.5 * (ux * lx + uy * ly), ux, uy, -0.5 * ca, -cb, -0.5 * cc)):
        for term_at, term in enumerate(split(value, 3)):
            scatter_rows(coefs, 8 * term_at + at, 32, term)
    for k in range(3):
        terms = split(feature(6 + k), 3)
        for at, term_at in enumerate((0, 1, 0, 1, 2, 0)):
            scatter_rows(colours, 3 * at + k, 32, terms[term_at])

    def render(j):
        rows = pl.ds(pl.multiple_of(j * 32, 32), 32)
        power = dot(basis_pe, take_rows(coefs, rows).astype(BF16))
        alpha = live_op[pl.ds(j, 1), :] * jnp.exp(power)
        keep = 1.0 - alpha
        hi, lo = two(jnp.log(keep))
        weight = alpha * jnp.exp(dot(hi, before) + dot(lo, before))
        hi, lo = two(weight)
        colour = take_rows(colours, rows).astype(BF16)
        image = dot_nt(colour, hi) + dot_nt(colour, lo)
        for k in range(3):
            rendered[0, k, pl.ds(j, 1), :] = (
                image[k : k + 1] + image[k + 3 : k + 4] + image[k + 12 : k + 13]
            )
        tint = dot(cots[j], hi) + dot(cots[j], lo)
        scatter_rows(tints, j, tiles_here, tint[0:3] + tint[6:9] + tint[15:18])
        pulled = dot(cots_t[j], colour) * weight
        hi, lo = two(pulled)
        later = dot(hi, after) + dot(lo, after)
        rough = pl.reciprocal(keep, approx=True)
        hi, lo = two(pulled - later * (alpha * (rough * (2.0 - keep * rough))))
        moment = dot(basis_ep, hi) + dot(basis_ep, lo)
        scatter_rows(moments, j, tiles_here, moment[0:8])

    step = 2 if tiles_here % 2 == 0 else 1

    @pl.loop(0, tiles_here // step)
    def _(at):
        for more in range(step):
            render(at * step + more)

    def moment(at):
        return take_rows(moments, slice(at * tiles_here, (at + 1) * tiles_here))

    m0, mx, my = moment(0), moment(1), moment(2)
    nx, ny = mx - lx * m0, my - ly * m0
    nxx = moment(3) - 2.0 * lx * mx + lx * lx * m0
    nxy = moment(4) - lx * my - ly * mx + lx * ly * m0
    nyy = moment(5) - 2.0 * ly * my + ly * ly * m0
    grads[...] = jnp.zeros_like(grads)
    for at, value in enumerate(
        (ca * nx + cb * ny, cc * ny + cb * nx, -0.5 * nxx, -nxy, -0.5 * nyy, m0 / op)
    ):
        scatter_rows(grads, at, 16, value)
    for k in range(3):
        scatter_rows(
            grads, 6 + k, 16, take_rows(tints, slice(k * tiles_here, (k + 1) * tiles_here))
        )
    back = 0.0
    for j in range(tiles_here):
        hi, lo = split(take_rows(grads, slice(16 * j, 16 * (j + 1))), 2)
        group = lists[j : j + 1, :] // LANES
        spread = [
            jnp.where(group == h, term, 0.0) for h in range(groups) for term in (hi, lo)
        ]
        back = back + dot_nt(jnp.concatenate(spread, axis=0).astype(BF16), low[j])
    slot_rows = [back[32 * h : 32 * h + 16] + back[32 * h + 16 : 32 * h + 32] for h in range(groups)]

    g = [
        jnp.concatenate([rows[at : at + 1] for rows in slot_rows], axis=0) for at in range(NFEAT)
    ]
    f = [by_slot[pl.ds(at, groups, stride=NSENT), :] for at in range(NSENT)]
    c = [cams[my_img, at] for at in range(10)]
    v0, v1, _ = conic(c, f[12:18])
    h = cov_grad((f[2], f[3], f[4]), (g[2], g[3], g[4]))
    shares = [g[0] * f[9 + a] + 2.0 * (h[0] * v0[a] + h[1] * v1[a]) for a in range(3)]
    shares += [g[1] * f[9 + a] + 2.0 * (h[2] * v1[a] + h[1] * v0[a]) for a in range(3)]
    shares += [g[0], g[1]]
    shares += [sum(g[6 + k] * f[18 + 3 * d + k] for k in range(3)) for d in range(2)]
    slot_lane = lax.rem(lax.broadcasted_iota(jnp.int32, (16, LANES), 1), cap)
    is_camera = lax.broadcasted_iota(jnp.int32, (16, LANES), 0) == NFEAT
    camera_row = jnp.zeros((1, LANES), F32)
    for at, share in enumerate(shares):
        total = jnp.sum(jnp.sum(share, axis=0, keepdims=True), axis=1, keepdims=True)
        camera_row = jnp.where(slot_lane[0:1] == at, total, camera_row)
    for at, rows in enumerate(slot_rows):
        slots[at * LANES : (at + 1) * LANES, 0:NBACK] = jnp.transpose(
            jnp.where(is_camera, camera_row, rows)
        )
    grad_send[...] = jnp.concatenate(
        [slots[pl.ds(c, devices, stride=cap), 0:NBACK] for c in range(cap)], axis=1
    ).reshape(devices, 1, cap * NBACK)
    returning = exchange(2, grad_send, grad_recv)
    sent(1, feat_send)
    arrive(2, grad_recv, returning)
    back_out[...] = grad_recv[...].reshape(devices, cap * NBACK)
    sent(2, grad_send)


def owner_kernel(
    sizes,
    means,
    log_scales,
    quat_w,
    quat_v,
    opacity,
    cams,
    back,
    asked,
    harm,
    rendered_in,
    rendered,
    param_grad,
    camera_grad,
    dense,
    slots,
    result,
):
    n_img, n_tile, cap = sizes
    owned = means.shape[1]
    high = owned // LANES
    devices = n_img * n_tile
    per_img = n_tile * cap
    rendered[...] = rendered_in[...]
    load_dense((means, log_scales, quat_w, quat_v, opacity), dense)

    def row(at):
        return dense[at * high : (at + 1) * high, :]

    quat, inverse, rot, squares, sigma = geometry(row)
    base = 1.0 / (1.0 + jnp.exp(-row(10)))
    packed = back[...]
    for c in range(cap):
        slots[pl.ds(c, devices, stride=cap), 0:NBACK] = packed[:, c * NBACK : (c + 1) * NBACK]
    g_mean = [0.0, 0.0, 0.0]
    g_base = 0.0
    g_sigma = [[0.0] * 3 for _ in range(3)]
    g_colour = []
    for i in range(n_img):
        mine = jnp.concatenate(
            [
                jnp.transpose(slots[at : at + LANES, :])[0:NBACK]
                for at in range(i * per_img, (i + 1) * per_img, LANES)
            ],
            axis=1,
        )
        fold = mine[NFEAT : NFEAT + 1, 0:LANES]
        for at in range(LANES, per_img, LANES):
            fold = fold + mine[NFEAT : NFEAT + 1, at : at + LANES]
        shift = LANES // 2
        while shift >= cap:
            fold = fold + pltpu.roll(fold, shift, 1)
            shift //= 2
        camera_grad[i : i + 1, :] = fold[:, 0:10]
        lanes = slice(i * per_img, (i + 1) * per_img)
        pick = mask_of(asked[0:1, lanes], high)
        low = as_bf16(mask_of(asked[1:2, lanes], LANES))
        spread = jnp.concatenate(
            [
                jnp.concatenate(
                    [jnp.where(pick, term[at : at + 1], 0.0) for at in range(NFEAT)], axis=0
                ).astype(BF16)
                for term in split(mine, 2)
            ],
            axis=1,
        )
        full = dot_nt(spread, jnp.concatenate([low] * 2, axis=1))
        g = [full[at * high : (at + 1) * high] for at in range(NFEAT)]
        c = [cams[i, at] for at in range(8)]
        _, _, con = conic(c, sigma)
        h = cov_grad(con, (g[2], g[3], g[4]))
        for a in range(3):
            g_mean[a] = g_mean[a] + c[a] * g[0] + c[3 + a] * g[1]
            for b in range(a, 3):
                g_sigma[a][b] = (
                    g_sigma[a][b]
                    + (c[a] * c[b]) * h[0]
                    + (c[a] * c[3 + b] + c[3 + a] * c[b]) * h[1]
                    + (c[3 + a] * c[3 + b]) * h[2]
                )
        g_base = g_base + g[5]
        g_colour.append(g[6:9])

    def put(at, value):
        result[at * high : (at + 1) * high, :] = value

    for k in range(3):
        for m in range(16):
            put(
                11 + 16 * k + m,
                sum(harm[i, m : m + 1, :] * g_colour[i][k] for i in range(n_img)),
            )
    for a in range(3):
        put(a, g_mean[a])
        for b in range(a):
            g_sigma[a][b] = g_sigma[b][a]
    r = [[None] * 3 for _ in range(3)]
    for b in range(3):
        pull = [
            g_sigma[a][0] * rot[0][b] + g_sigma[a][1] * rot[1][b] + g_sigma[a][2] * rot[2][b]
            for a in range(3)
        ]
        twice = 2.0 * squares[b]
        for a in range(3):
            r[a][b] = twice * pull[a]
        put(3 + b, r[0][b] * rot[0][b] + r[1][b] * rot[1][b] + r[2][b] * rot[2][b])
    w, x, y, z = quat
    g_quat = (
        z * (r[1][0] - r[0][1]) + y * (r[0][2] - r[2][0]) + x * (r[2][1] - r[1][2]),
        y * (r[0][1] + r[1][0])
        + z * (r[0][2] + r[2][0])
        + w * (r[2][1] - r[1][2])
        - 2.0 * x * (r[1][1] + r[2][2]),
        x * (r[0][1] + r[1][0])
        + z * (r[1][2] + r[2][1])
        + w * (r[0][2] - r[2][0])
        - 2.0 * y * (r[0][0] + r[2][2]),
        x * (r[0][2] + r[2][0])
        + y * (r[1][2] + r[2][1])
        + w * (r[1][0] - r[0][1])
        - 2.0 * z * (r[0][0] + r[1][1]),
    )
    along = sum(quat[a] * g_quat[a] for a in range(4))
    for a in range(4):
        put(6 + a, 2.0 * (g_quat[a] - quat[a] * along) * inverse)
    put(10, g_base * base * (1.0 - base))
    rows = param_grad.shape[0]
    for h in range(high):
        param_grad[:, h * LANES : (h + 1) * LANES] = result[pl.ds(h, rows, stride=high), :]


def local(
    means,
    log_scales,
    quat_w,
    quat_v,
    opacity,
    sh_coeffs,
    cameras,
    requests,
    lists,
    counts,
    image_cot,
):
    n_img, n_tile, cap = requests.shape[2:]
    devices = n_img * n_tile
    n_slots = devices * cap
    owned = means.shape[1]
    high = owned // LANES
    tiles_here, length = lists.shape[1:]
    pix = image_cot.shape[3]
    vmem = pl.BlockSpec(memory_space=pltpu.VMEM)
    smem = pl.BlockSpec(memory_space=pltpu.SMEM)
    small = (means, log_scales, quat_w, quat_v, opacity)
    few = sum(part.shape[0] for part in small)
    rows = few + sh_coeffs.shape[0]
    image_shape = jax.ShapeDtypeStruct(image_cot.shape, F32)
    rendered, back, asked, harm = pl.pallas_call(
        functools.partial(render_kernel, (n_img, n_tile, cap, tiles_here, length, pix)),
        out_shape=(
            image_shape,
            jax.ShapeDtypeStruct((devices, cap * NBACK), F32),
            jax.ShapeDtypeStruct((2, n_slots), jnp.int32),
            jax.ShapeDtypeStruct((n_img, 16, LANES), F32),
        ),
        in_specs=[vmem] * 6 + [smem, vmem, vmem, smem, vmem],
        out_specs=(vmem,) * 4,
        scratch_shapes=[
            pltpu.VMEM((devices, 1, cap), jnp.int32),
            pltpu.VMEM((devices, 1, cap * NSENT), F32),
            pltpu.VMEM((devices, 1, cap * NSENT), F32),
            pltpu.VMEM((devices, 1, cap * NBACK), F32),
            pltpu.VMEM((devices, 1, cap * NBACK), F32),
            pltpu.VMEM((rows * high + high, LANES), F32),
            pltpu.VMEM((high * NSENT + NSENT, LANES), F32),
            pltpu.VMEM((n_img, high * NSENT, 3 * LANES), BF16),
            pltpu.VMEM((n_slots + cap, LANES), F32),
            pltpu.VMEM((n_slots // LANES * NSENT + NSENT, LANES), F32),
            pltpu.VMEM((tiles_here, LANES, length), BF16),
            pltpu.VMEM((length // LANES, 16 * tiles_here + 16, LANES), F32),
            pltpu.VMEM((length // LANES, 32 * tiles_here + 32, LANES), F32),
            pltpu.VMEM((length // LANES, 32 * tiles_here + 32, LANES), F32),
            pltpu.VMEM((tiles_here, 32, pix), BF16),
            pltpu.VMEM((tiles_here, pix, 32), BF16),
            pltpu.VMEM((tiles_here, length), F32),
            pltpu.VMEM((length // LANES, 9 * tiles_here, LANES), F32),
            pltpu.VMEM((length // LANES, 4 * tiles_here, LANES), F32),
            pltpu.VMEM((length // LANES, 16 * tiles_here + 16, LANES), F32),
            pltpu.VMEM((n_img, 3, 16, LANES), F32),
            pltpu.SemaphoreType.DMA((3,)),
            pltpu.SemaphoreType.DMA((3,)),
            pltpu.SemaphoreType.DMA((3,)),
        ],
        compiler_params=pltpu.CompilerParams(
            collective_id=0, has_side_effects=True, vmem_limit_bytes=48 * 1024 * 1024
        ),
    )(
        *small,
        sh_coeffs,
        cameras,
        requests.reshape(devices, 1, cap),
        lists[0],
        counts,
        image_cot,
    )
    return pl.pallas_call(
        functools.partial(owner_kernel, (n_img, n_tile, cap)),
        out_shape=(
            image_shape,
            jax.ShapeDtypeStruct((rows, owned), F32),
            jax.ShapeDtypeStruct(cameras.shape, F32),
        ),
        in_specs=[vmem] * 5 + [smem] + [vmem] * 4,
        out_specs=(vmem,) * 3,
        scratch_shapes=[
            pltpu.VMEM((few * high + high, LANES), F32),
            pltpu.VMEM((n_slots + cap, LANES), F32),
            pltpu.VMEM((rows * high + high, LANES), F32),
        ],
        compiler_params=pltpu.CompilerParams(vmem_limit_bytes=16 * 1024 * 1024),
    )(*small, cameras, back, asked, harm, rendered)


def solution(mesh):
    owners = P(None, ("img", "tile"))
    images = P("img", None, "tile", None)
    return jax.shard_map(
        local,
        mesh=mesh,
        in_specs=(owners,) * 6
        + (P(), P("img", "tile", None, None, None), P("img", "tile", None), P("img", "tile"), images),
        out_specs=(images, owners, P()),
        check_vma=False,
    )
```

```python
import functools
import math

import jax
import jax.numpy as jnp
from jax import lax
from jax.experimental import pallas as pl
from jax.experimental.pallas import tpu as pltpu
from jax.sharding import PartitionSpec as P

TILE_SIDE = 16
TW = 16
NFEAT = 9
NSENT = 24
NBACK = 16
LANES = 128
F32 = jnp.float32
BF16 = jnp.bfloat16
MESH = pl.DeviceIdType.MESH

sh_first = 0.28209479177387814
sh_second = 0.4886025119029199
sh_third = (
    1.0925484305920792,
    -1.0925484305920792,
    0.31539156525252005,
    -1.0925484305920792,
    0.5462742152960396,
)
sh_fourth = (
    -0.5900435899266435,
    2.890611442640554,
    -0.4570457994644658,
    0.3731763325901154,
    -0.4570457994644658,
    1.445305721320277,
    -0.5900435899266435,
)
dilation = 0.3


def harmonics(x, y, z):
    xx, yy, zz = x * x, y * y, z * z
    zero = jnp.zeros_like(x)
    a, b = sh_third, sh_fourth
    c = sh_second
    values = [
        zero + sh_first,
        -c * y,
        c * z,
        -c * x,
        a[0] * x * y,
        a[1] * y * z,
        a[2] * (2.0 * zz - xx - yy),
        a[3] * x * z,
        a[4] * (xx - yy),
        b[0] * y * (3.0 * xx - yy),
        b[1] * x * y * z,
        b[2] * y * (4.0 * zz - xx - yy),
        b[3] * z * (2.0 * zz - 3.0 * xx - 3.0 * yy),
        b[4] * x * (4.0 * zz - xx - yy),
        b[5] * z * (xx - yy),
        b[6] * x * (xx - 3.0 * yy),
    ]
    by_x = [
        zero,
        zero,
        zero,
        zero - c,
        a[0] * y,
        zero,
        -2.0 * a[2] * x,
        a[3] * z,
        2.0 * a[4] * x,
        6.0 * b[0] * x * y,
        b[1] * y * z,
        -2.0 * b[2] * x * y,
        -6.0 * b[3] * x * z,
        b[4] * (4.0 * zz - 3.0 * xx - yy),
        2.0 * b[5] * x * z,
        b[6] * (3.0 * xx - 3.0 * yy),
    ]
    by_y = [
        zero,
        zero - c,
        zero,
        zero,
        a[0] * x,
        a[1] * z,
        -2.0 * a[2] * y,
        zero,
        -2.0 * a[4] * y,
        b[0] * (3.0 * xx - 3.0 * yy),
        b[1] * x * z,
        b[2] * (4.0 * zz - xx - 3.0 * yy),
        -6.0 * b[3] * y * z,
        -2.0 * b[4] * x * y,
        -2.0 * b[5] * y * z,
        -6.0 * b[6] * x * y,
    ]
    by_z = [
        zero,
        zero,
        zero + c,
        zero,
        zero,
        a[1] * y,
        4.0 * a[2] * z,
        a[3] * x,
        zero,
        zero,
        b[1] * x * y,
        8.0 * b[2] * y * z,
        b[3] * (6.0 * zz - 3.0 * xx - 3.0 * yy),
        8.0 * b[4] * x * z,
        b[5] * (xx - yy),
        zero,
    ]
    return values, by_x, by_y, by_z


def split(value, parts):
    terms, rest = [], value
    for at in range(parts):
        term = rest.astype(BF16).astype(F32)
        terms.append(term)
        if at < parts - 1:
            rest = rest - term
    return terms


def dot(a, b):
    return jnp.dot(a, b, preferred_element_type=F32)


def dot_nt(a, b):
    return lax.dot_general(a, b, (((1,), (1,)), ((), ())), preferred_element_type=F32)


def conic(cam, sigma):
    a0, a1 = cam[0:3], cam[3:6]

    def times(a):
        return (
            a[0] * sigma[0] + a[1] * sigma[1] + a[2] * sigma[2],
            a[0] * sigma[1] + a[1] * sigma[3] + a[2] * sigma[4],
            a[0] * sigma[2] + a[1] * sigma[4] + a[2] * sigma[5],
        )

    v0, v1 = times(a0), times(a1)
    s00 = a0[0] * v0[0] + a0[1] * v0[1] + a0[2] * v0[2] + dilation
    s01 = a1[0] * v0[0] + a1[1] * v0[1] + a1[2] * v0[2]
    s11 = a1[0] * v1[0] + a1[1] * v1[1] + a1[2] * v1[2] + dilation
    inverse = 1.0 / (s00 * s11 - s01 * s01)
    return v0, v1, (s11 * inverse, -s01 * inverse, s00 * inverse)


def cov_grad(con, grad):
    ca, cb, cc = con
    ga, gb, gc = grad[0], 0.5 * grad[1], grad[2]
    p00, p01 = ca * ga + cb * gb, ca * gb + cb * gc
    p10, p11 = cb * ga + cc * gb, cb * gb + cc * gc
    return (
        -(p00 * ca + p01 * cb),
        -(p00 * cb + p01 * cc),
        -(p10 * cb + p11 * cc),
    )


def rotation_of(quat):
    w, x, y, z = quat
    return (
        (1.0 - 2.0 * (y * y + z * z), 2.0 * (x * y - w * z), 2.0 * (x * z + w * y)),
        (2.0 * (x * y + w * z), 1.0 - 2.0 * (x * x + z * z), 2.0 * (y * z - w * x)),
        (2.0 * (x * z - w * y), 2.0 * (y * z + w * x), 1.0 - 2.0 * (x * x + y * y)),
    )


def load_dense(refs, dense):
    at = 0
    for ref in refs:
        rows, owned = ref.shape
        high = owned // LANES
        for h in range(high):
            part = ref[:, h * LANES : (h + 1) * LANES]
            if rows == 1:
                dense[at * high + h : at * high + h + 1, :] = part
            else:
                dense[pl.ds(at * high + h, rows, stride=high), :] = part
        at += rows


def geometry(row):
    raw = tuple(row(6 + a) for a in range(4))
    inverse = 1.0 / jnp.sqrt(
        raw[0] * raw[0] + raw[1] * raw[1] + raw[2] * raw[2] + raw[3] * raw[3]
    )
    quat = tuple(part * inverse for part in raw)
    rot = rotation_of(quat)
    squares = tuple(jnp.exp(2.0 * row(3 + a)) for a in range(3))

    def entry(a, b):
        return (
            rot[a][0] * rot[b][0] * squares[0]
            + rot[a][1] * rot[b][1] * squares[1]
            + rot[a][2] * rot[b][2] * squares[2]
        )

    sigma = tuple(entry(a, b) for a, b in ((0, 0), (0, 1), (0, 2), (1, 1), (1, 2), (2, 2)))
    return quat, inverse, rot, squares, sigma


def mask_of(index, rows):
    return lax.broadcasted_iota(jnp.int32, (rows, index.shape[1]), 0) == index


def as_bf16(mask):
    return mask.astype(F32).astype(BF16)


def two(value):
    hi = value.astype(BF16)
    return hi, (value - hi.astype(F32)).astype(BF16)


def scatter_rows(ref, start, stride, value):
    for h in range(ref.shape[0]):
        ref[h, pl.ds(start, value.shape[0], stride=stride), :] = value[
            :, h * LANES : (h + 1) * LANES
        ]


def take_rows(ref, rows):
    return jnp.concatenate([ref[h, rows, :] for h in range(ref.shape[0])], axis=1)


def render_kernel(
    sizes,
    means_hbm,
    log_scales_hbm,
    quat_w_hbm,
    quat_v_hbm,
    opacity_hbm,
    sh_hbm,
    cams,
    requests,
    lists_hbm,
    counts,
    cot_hbm,
    rendered,
    back_out,
    ask_out,
    harm_out,
    means,
    log_scales,
    quat_w,
    quat_v,
    opacity,
    sh,
    lists,
    cot,
    in_sem,
    ask_recv,
    feat_send,
    feat_recv,
    grad_send,
    grad_recv,
    dense,
    project,
    feats,
    slots,
    by_slot,
    low,
    gots,
    coefs,
    colours,
    cots,
    cots_t,
    live_op,
    moments,
    tints,
    grads,
    harm,
    send_sem,
    recv_sem,
    own_sem,
):
    n_img, n_tile, cap, tiles_here, length, pix = sizes
    owned = means.shape[1]
    high = owned // LANES
    devices = n_img * n_tile
    n_slots = devices * cap
    groups = n_slots // LANES
    per_img = n_tile * cap
    my_tile = lax.axis_index("tile")
    my_img = lax.axis_index("img")
    me = my_img * n_tile + my_tile

    def peer(k):
        other = lax.rem(me + k, devices)
        return other, (other // n_tile, lax.rem(other, n_tile))

    loads = [
        pltpu.make_async_copy(source, target, in_sem.at[at])
        for at, (source, target) in enumerate(
            (
                (means_hbm, means),
                (log_scales_hbm, log_scales),
                (quat_w_hbm, quat_w),
                (quat_v_hbm, quat_v),
                (opacity_hbm, opacity),
                (sh_hbm, sh),
                (lists_hbm, lists),
                (cot_hbm, cot),
            )
        )
    ]
    for load in loads:
        load.start()

    barrier = pltpu.get_barrier_semaphore()

    @pl.loop(1, devices)
    def _(k):
        pl.semaphore_signal(barrier, inc=1, device_id=peer(k)[1], device_id_type=MESH)

    def exchange(at, source, target):
        mine = pltpu.make_async_copy(source.at[me], target.at[me], own_sem.at[at])
        mine.start()

        @pl.loop(1, devices)
        def _(k):
            other, where = peer(k)
            pltpu.make_async_remote_copy(
                src_ref=source.at[other],
                dst_ref=target.at[me],
                send_sem=send_sem.at[at],
                recv_sem=recv_sem.at[at],
                device_id=where,
                device_id_type=MESH,
            ).start()

        return mine

    def arrive(at, target, mine):
        mine.wait()
        others = target.at[pl.ds(0, devices - 1)]
        pltpu.make_async_copy(others, others, recv_sem.at[at]).wait()

    def sent(at, source):
        others = source.at[pl.ds(0, devices - 1)]
        pltpu.make_async_copy(others, others, send_sem.at[at]).wait()

    cam = [[cams[i, c] for c in range(10)] for i in range(n_img)]
    img_rows = -(-n_img // 8) * 8
    img_row = lax.broadcasted_iota(jnp.int32, (img_rows, LANES), 0)
    polar = jnp.zeros((img_rows, LANES), F32)
    azimuth = jnp.zeros((img_rows, LANES), F32)
    for i in range(n_img):
        polar = jnp.where(img_row == i, cam[i][8], polar)
        azimuth = jnp.where(img_row == i, cam[i][9], azimuth)
    sp, cp = jnp.sin(polar), jnp.cos(polar)
    sz, cz = jnp.sin(azimuth), jnp.cos(azimuth)
    values, by_x, by_y, by_z = harmonics(sp * cz, sp * sz, cp)
    for m in range(16):
        by_polar = by_x[m] * (cp * cz) + by_y[m] * (cp * sz) - by_z[m] * sp
        by_azimuth = by_y[m] * (sp * cz) - by_x[m] * (sp * sz)
        for i in range(n_img):
            harm[i, 0, m : m + 1, :] = values[m][i : i + 1]
            harm[i, 1, m : m + 1, :] = by_polar[i : i + 1]
            harm[i, 2, m : m + 1, :] = by_azimuth[i : i + 1]
    for i in range(n_img):
        harm_out[i] = harm[i, 0]
    for load in loads[:6]:
        load.wait()
    load_dense((means, log_scales, quat_w, quat_v, opacity, sh), dense)

    pl.semaphore_wait(barrier, devices - 1)
    asking = exchange(0, requests, ask_recv)

    def row(at):
        return dense[at * high : (at + 1) * high, :]

    _, _, _, _, sigma = geometry(row)
    mean = tuple(row(a) for a in range(3))
    base = 1.0 / (1.0 + jnp.exp(-row(10)))
    for i in range(n_img):
        c = cam[i]
        _, _, con = conic(c, sigma)
        rows = [
            c[0] * mean[0] + c[1] * mean[1] + c[2] * mean[2] + c[6],
            c[3] * mean[0] + c[4] * mean[1] + c[5] * mean[2] + c[7],
            con[0],
            con[1],
            con[2],
            base,
        ]
        sums = [[None] * 3 for _ in range(3)]
        for k in range(3):
            for m in range(16):
                coeff = row(11 + 16 * k + m)
                for d in range(3):
                    term = coeff * harm[i, d, m : m + 1, :]
                    sums[d][k] = term if m == 0 else sums[d][k] + term
        rows += [total + 0.5 for total in sums[0]] + list(mean) + list(sigma) + sums[1] + sums[2]
        for at, value in enumerate(rows):
            project[pl.ds(at, high, stride=NSENT), :] = value
        for at, term in enumerate(split(project[0 : high * NSENT, :], 3)):
            feats[i, :, at * LANES : (at + 1) * LANES] = term.astype(BF16)

    for load in loads[6:]:
        load.wait()
    coefs[...] = jnp.zeros_like(coefs)
    colours[...] = jnp.zeros_like(colours)
    for j in range(tiles_here):
        low[j] = as_bf16(mask_of(jnp.bitwise_and(lists[j : j + 1, :], LANES - 1), LANES))
        cot3 = jnp.concatenate([cot[0, k, j : j + 1, :] for k in range(3)], axis=0)
        c1, c2, c3 = split(cot3, 3)
        stack = jnp.concatenate([c1, c1, c2, c2, c1, c3, jnp.zeros((14, pix), F32)], axis=0)
        cots[j] = stack.astype(BF16)
        cots_t[j] = jnp.transpose(stack).astype(BF16)

    def basis_of(pixel, which):
        half = 0.5 * TILE_SIDE - 0.5
        x = lax.rem(pixel, TILE_SIDE).astype(F32) - half
        y = (pixel // TILE_SIDE).astype(F32) - half
        out = jnp.where(which == 0, 1.0, 0.0)
        for at, term in enumerate((x, y, x * x, x * y, y * y)):
            out = jnp.where(which == at + 1, term, out)
        return out.astype(BF16)

    basis_pe = basis_of(
        lax.broadcasted_iota(jnp.int32, (pix, 32), 0),
        lax.rem(lax.broadcasted_iota(jnp.int32, (pix, 32), 1), 8),
    )
    basis_ep = basis_of(
        lax.broadcasted_iota(jnp.int32, (16, pix), 1), lax.broadcasted_iota(jnp.int32, (16, pix), 0)
    )
    first = lax.broadcasted_iota(jnp.int32, (length, length), 0)
    second = lax.broadcasted_iota(jnp.int32, (length, length), 1)
    before = as_bf16(first < second)
    after = as_bf16(first > second)
    height = TILE_SIDE * tiles_here * n_tile / TW

    arrive(0, ask_recv, asking)
    asks = ask_recv[...].reshape(devices, cap)
    halves = jnp.concatenate(
        [(asks // LANES).astype(F32), jnp.bitwise_and(asks, LANES - 1).astype(F32)], axis=0
    ).astype(BF16)
    repeat = as_bf16(
        lax.rem(lax.broadcasted_iota(jnp.int32, (cap, n_slots), 1), cap)
        == lax.broadcasted_iota(jnp.int32, (cap, n_slots), 0)
    )
    wide = dot(halves, repeat)
    here = (
        lax.broadcasted_iota(jnp.int32, (devices, n_slots), 1) // cap
        == lax.broadcasted_iota(jnp.int32, (devices, n_slots), 0)
    )
    ask_hi, ask_lo = (
        jnp.sum(
            jnp.where(here, wide[at * devices : (at + 1) * devices], 0.0), axis=0, keepdims=True
        ).astype(jnp.int32)
        for at in range(2)
    )
    ask_out[0:1, :] = ask_hi
    ask_out[1:2, :] = ask_lo
    for i in range(n_img):
        lanes = slice(i * per_img, (i + 1) * per_img)
        mask = as_bf16(mask_of(ask_lo[:, lanes], LANES))
        got = dot(feats[i], jnp.concatenate([mask] * 3, axis=0))
        pick = mask_of(ask_hi[:, lanes], high).astype(F32)
        total = got[0:NSENT] * pick[0:1]
        for h in range(1, high):
            total = total + got[h * NSENT : (h + 1) * NSENT] * pick[h : h + 1]
        slots[lanes, 0:NSENT] = jnp.transpose(total)
    feat_send[...] = jnp.concatenate(
        [slots[pl.ds(c, devices, stride=cap), 0:NSENT] for c in range(cap)], axis=1
    ).reshape(devices, 1, cap * NSENT)
    sending = exchange(1, feat_send, feat_recv)
    sent(0, requests)
    arrive(1, feat_recv, sending)
    packed = feat_recv[...].reshape(devices, cap * NSENT)
    for c in range(cap):
        slots[pl.ds(c, devices, stride=cap), 0:NSENT] = packed[:, c * NSENT : (c + 1) * NSENT]
    heads = []
    for h in range(groups):
        turned = jnp.transpose(slots[h * LANES : (h + 1) * LANES, :])[0:NSENT]
        by_slot[h * NSENT : (h + 1) * NSENT, :] = turned
        heads.append(turned[0:16])
    heads = jnp.concatenate(
        [term.astype(BF16) for term in split(jnp.concatenate(heads, axis=0), 3)], axis=1
    )

    for j in range(tiles_here):
        got = dot(heads, jnp.concatenate([low[j]] * 3, axis=0))
        group = lists[j : j + 1, :] // LANES
        total = jnp.where(group == 0, got[0:16], 0.0)
        for h in range(1, groups):
            total = total + jnp.where(group == h, got[h * 16 : (h + 1) * 16], 0.0)
        scatter_rows(gots, j, tiles_here, total)

    def feature(at):
        return take_rows(gots, slice(at * tiles_here, (at + 1) * tiles_here))

    tile_row = lax.broadcasted_iota(jnp.int32, (tiles_here, length), 0)
    number = my_tile * tiles_here + tile_row
    lx = feature(0) - (
        (lax.rem(number, TW) * TILE_SIDE).astype(F32) + 0.5 * TILE_SIDE * (1 - TW)
    )
    ly = feature(1) - ((number // TW * TILE_SIDE).astype(F32) + 0.5 * TILE_SIDE - 0.5 * height)
    ca, cb, cc, op = (feature(at) for at in range(2, 6))
    ux = ca * lx + cb * ly
    uy = cc * ly + cb * lx
    live = jnp.zeros((tiles_here, length), jnp.int32)
    for j in range(tiles_here):
        live = jnp.where(tile_row == j, counts[0, j], live)
    lane = lax.broadcasted_iota(jnp.int32, (tiles_here, length), 1)
    live_op[...] = jnp.where(lane < live, op, 0.0)
    for at, value in enumerate((-0.5 * (ux * lx + uy * ly), ux, uy, -0.5 * ca, -cb, -0.5 * cc)):
        for term_at, term in enumerate(split(value, 3)):
            scatter_rows(coefs, 8 * term_at + at, 32, term)
    for k in range(3):
        terms = split(feature(6 + k), 3)
        for at, term_at in enumerate((0, 1, 0, 1, 2, 0)):
            scatter_rows(colours, 3 * at + k, 32, terms[term_at])

    def render(j):
        rows = pl.ds(pl.multiple_of(j * 32, 32), 32)
        power = dot(basis_pe, take_rows(coefs, rows).astype(BF16))
        alpha = live_op[pl.ds(j, 1), :] * jnp.exp(power)
        keep = 1.0 - alpha
        hi, lo = two(jnp.log(keep))
        weight = alpha * jnp.exp(dot(hi, before) + dot(lo, before))
        hi, lo = two(weight)
        colour = take_rows(colours, rows).astype(BF16)
        image = dot_nt(colour, hi) + dot_nt(colour, lo)
        for k in range(3):
            rendered[0, k, pl.ds(j, 1), :] = (
                image[k : k + 1] + image[k + 3 : k + 4] + image[k + 12 : k + 13]
            )
        tint = dot(cots[j], hi) + dot(cots[j], lo)
        scatter_rows(tints, j, tiles_here, tint[0:3] + tint[6:9] + tint[15:18])
        pulled = dot(cots_t[j], colour) * weight
        hi, lo = two(pulled)
        later = dot(hi, after) + dot(lo, after)
        rough = pl.reciprocal(keep, approx=True)
        hi, lo = two(pulled - later * (alpha * (rough * (2.0 - keep * rough))))
        moment = dot(basis_ep, hi) + dot(basis_ep, lo)
        scatter_rows(moments, j, tiles_here, moment[0:8])

    step = 2 if tiles_here % 2 == 0 else 1

    @pl.loop(0, tiles_here // step)
    def _(at):
        for more in range(step):
            render(at * step + more)

    def moment(at):
        return take_rows(moments, slice(at * tiles_here, (at + 1) * tiles_here))

    m0, mx, my = moment(0), moment(1), moment(2)
    nx, ny = mx - lx * m0, my - ly * m0
    nxx = moment(3) - 2.0 * lx * mx + lx * lx * m0
    nxy = moment(4) - lx * my - ly * mx + lx * ly * m0
    nyy = moment(5) - 2.0 * ly * my + ly * ly * m0
    grads[...] = jnp.zeros_like(grads)
    for at, value in enumerate(
        (ca * nx + cb * ny, cc * ny + cb * nx, -0.5 * nxx, -nxy, -0.5 * nyy, m0 / op)
    ):
        scatter_rows(grads, at, 16, value)
    for k in range(3):
        scatter_rows(
            grads, 6 + k, 16, take_rows(tints, slice(k * tiles_here, (k + 1) * tiles_here))
        )
    back = 0.0
    for j in range(tiles_here):
        hi, lo = split(take_rows(grads, slice(16 * j, 16 * (j + 1))), 2)
        group = lists[j : j + 1, :] // LANES
        spread = [
            jnp.where(group == h, term, 0.0) for h in range(groups) for term in (hi, lo)
        ]
        back = back + dot_nt(jnp.concatenate(spread, axis=0).astype(BF16), low[j])
    slot_rows = [back[32 * h : 32 * h + 16] + back[32 * h + 16 : 32 * h + 32] for h in range(groups)]

    g = [
        jnp.concatenate([rows[at : at + 1] for rows in slot_rows], axis=0) for at in range(NFEAT)
    ]
    f = [by_slot[pl.ds(at, groups, stride=NSENT), :] for at in range(NSENT)]
    c = [cams[my_img, at] for at in range(10)]
    v0, v1, _ = conic(c, f[12:18])
    h = cov_grad((f[2], f[3], f[4]), (g[2], g[3], g[4]))
    shares = [g[0] * f[9 + a] + 2.0 * (h[0] * v0[a] + h[1] * v1[a]) for a in range(3)]
    shares += [g[1] * f[9 + a] + 2.0 * (h[2] * v1[a] + h[1] * v0[a]) for a in range(3)]
    shares += [g[0], g[1]]
    shares += [sum(g[6 + k] * f[18 + 3 * d + k] for k in range(3)) for d in range(2)]
    slot_lane = lax.rem(lax.broadcasted_iota(jnp.int32, (16, LANES), 1), cap)
    is_camera = lax.broadcasted_iota(jnp.int32, (16, LANES), 0) == NFEAT
    camera_row = jnp.zeros((1, LANES), F32)
    for at, share in enumerate(shares):
        total = jnp.sum(jnp.sum(share, axis=0, keepdims=True), axis=1, keepdims=True)
        camera_row = jnp.where(slot_lane[0:1] == at, total, camera_row)
    for at, rows in enumerate(slot_rows):
        slots[at * LANES : (at + 1) * LANES, 0:NBACK] = jnp.transpose(
            jnp.where(is_camera, camera_row, rows)
        )
    grad_send[...] = jnp.concatenate(
        [slots[pl.ds(c, devices, stride=cap), 0:NBACK] for c in range(cap)], axis=1
    ).reshape(devices, 1, cap * NBACK)
    returning = exchange(2, grad_send, grad_recv)
    sent(1, feat_send)
    arrive(2, grad_recv, returning)
    back_out[...] = grad_recv[...].reshape(devices, cap * NBACK)
    sent(2, grad_send)


def owner_kernel(
    sizes,
    means,
    log_scales,
    quat_w,
    quat_v,
    opacity,
    cams,
    back,
    asked,
    harm,
    rendered_in,
    rendered,
    param_grad,
    camera_grad,
    dense,
    slots,
    result,
):
    n_img, n_tile, cap = sizes
    owned = means.shape[1]
    high = owned // LANES
    devices = n_img * n_tile
    per_img = n_tile * cap
    rendered[...] = rendered_in[...]
    load_dense((means, log_scales, quat_w, quat_v, opacity), dense)

    def row(at):
        return dense[at * high : (at + 1) * high, :]

    quat, inverse, rot, squares, sigma = geometry(row)
    base = 1.0 / (1.0 + jnp.exp(-row(10)))
    packed = back[...]
    for c in range(cap):
        slots[pl.ds(c, devices, stride=cap), 0:NBACK] = packed[:, c * NBACK : (c + 1) * NBACK]
    g_mean = [0.0, 0.0, 0.0]
    g_base = 0.0
    g_sigma = [[0.0] * 3 for _ in range(3)]
    g_colour = []
    for i in range(n_img):
        mine = jnp.concatenate(
            [
                jnp.transpose(slots[at : at + LANES, :])[0:NBACK]
                for at in range(i * per_img, (i + 1) * per_img, LANES)
            ],
            axis=1,
        )
        fold = mine[NFEAT : NFEAT + 1, 0:LANES]
        for at in range(LANES, per_img, LANES):
            fold = fold + mine[NFEAT : NFEAT + 1, at : at + LANES]
        shift = LANES // 2
        while shift >= cap:
            fold = fold + pltpu.roll(fold, shift, 1)
            shift //= 2
        camera_grad[i : i + 1, :] = fold[:, 0:10]
        lanes = slice(i * per_img, (i + 1) * per_img)
        pick = mask_of(asked[0:1, lanes], high)
        low = as_bf16(mask_of(asked[1:2, lanes], LANES))
        spread = jnp.concatenate(
            [
                jnp.concatenate(
                    [jnp.where(pick, term[at : at + 1], 0.0) for at in range(NFEAT)], axis=0
                ).astype(BF16)
                for term in split(mine, 2)
            ],
            axis=1,
        )
        full = dot_nt(spread, jnp.concatenate([low] * 2, axis=1))
        g = [full[at * high : (at + 1) * high] for at in range(NFEAT)]
        c = [cams[i, at] for at in range(8)]
        _, _, con = conic(c, sigma)
        h = cov_grad(con, (g[2], g[3], g[4]))
        for a in range(3):
            g_mean[a] = g_mean[a] + c[a] * g[0] + c[3 + a] * g[1]
            for b in range(a, 3):
                g_sigma[a][b] = (
                    g_sigma[a][b]
                    + (c[a] * c[b]) * h[0]
                    + (c[a] * c[3 + b] + c[3 + a] * c[b]) * h[1]
                    + (c[3 + a] * c[3 + b]) * h[2]
                )
        g_base = g_base + g[5]
        g_colour.append(g[6:9])

    def put(at, value):
        result[at * high : (at + 1) * high, :] = value

    for k in range(3):
        for m in range(16):
            put(
                11 + 16 * k + m,
                sum(harm[i, m : m + 1, :] * g_colour[i][k] for i in range(n_img)),
            )
    for a in range(3):
        put(a, g_mean[a])
        for b in range(a):
            g_sigma[a][b] = g_sigma[b][a]
    r = [[None] * 3 for _ in range(3)]
    for b in range(3):
        pull = [
            g_sigma[a][0] * rot[0][b] + g_sigma[a][1] * rot[1][b] + g_sigma[a][2] * rot[2][b]
            for a in range(3)
        ]
        twice = 2.0 * squares[b]
        for a in range(3):
            r[a][b] = twice * pull[a]
        put(3 + b, r[0][b] * rot[0][b] + r[1][b] * rot[1][b] + r[2][b] * rot[2][b])
    w, x, y, z = quat
    g_quat = (
        z * (r[1][0] - r[0][1]) + y * (r[0][2] - r[2][0]) + x * (r[2][1] - r[1][2]),
        y * (r[0][1] + r[1][0])
        + z * (r[0][2] + r[2][0])
        + w * (r[2][1] - r[1][2])
        - 2.0 * x * (r[1][1] + r[2][2]),
        x * (r[0][1] + r[1][0])
        + z * (r[1][2] + r[2][1])
        + w * (r[0][2] - r[2][0])
        - 2.0 * y * (r[0][0] + r[2][2]),
        x * (r[0][2] + r[2][0])
        + y * (r[1][2] + r[2][1])
        + w * (r[1][0] - r[0][1])
        - 2.0 * z * (r[0][0] + r[1][1]),
    )
    along = sum(quat[a] * g_quat[a] for a in range(4))
    for a in range(4):
        put(6 + a, 2.0 * (g_quat[a] - quat[a] * along) * inverse)
    put(10, g_base * base * (1.0 - base))
    rows = param_grad.shape[0]
    for h in range(high):
        param_grad[:, h * LANES : (h + 1) * LANES] = result[pl.ds(h, rows, stride=high), :]


def local(
    means,
    log_scales,
    quat_w,
    quat_v,
    opacity,
    sh_coeffs,
    cameras,
    requests,
    lists,
    counts,
    image_cot,
):
    n_img, n_tile, cap = requests.shape[2:]
    devices = n_img * n_tile
    n_slots = devices * cap
    owned = means.shape[1]
    high = owned // LANES
    tiles_here, length = lists.shape[1:]
    pix = image_cot.shape[3]
    vmem = pl.BlockSpec(memory_space=pltpu.VMEM)
    smem = pl.BlockSpec(memory_space=pltpu.SMEM)
    hbm = pl.BlockSpec(memory_space=pl.ANY)
    small = (means, log_scales, quat_w, quat_v, opacity)
    few = sum(part.shape[0] for part in small)
    rows = few + sh_coeffs.shape[0]
    image_shape = jax.ShapeDtypeStruct(image_cot.shape, F32)
    rendered, back, asked, harm = pl.pallas_call(
        functools.partial(render_kernel, (n_img, n_tile, cap, tiles_here, length, pix)),
        out_shape=(
            image_shape,
            jax.ShapeDtypeStruct((devices, cap * NBACK), F32),
            jax.ShapeDtypeStruct((2, n_slots), jnp.int32),
            jax.ShapeDtypeStruct((n_img, 16, LANES), F32),
        ),
        in_specs=[hbm] * 6 + [smem, hbm, hbm, smem, hbm],
        out_specs=(vmem,) * 4,
        scratch_shapes=[
            *(pltpu.VMEM(part.shape, F32) for part in (*small, sh_coeffs)),
            pltpu.VMEM((tiles_here, length), jnp.int32),
            pltpu.VMEM(image_cot.shape, F32),
            pltpu.SemaphoreType.DMA((8,)),
            pltpu.VMEM((devices, 1, cap), jnp.int32),
            pltpu.VMEM((devices, 1, cap * NSENT), F32),
            pltpu.VMEM((devices, 1, cap * NSENT), F32),
            pltpu.VMEM((devices, 1, cap * NBACK), F32),
            pltpu.VMEM((devices, 1, cap * NBACK), F32),
            pltpu.VMEM((rows * high + high, LANES), F32),
            pltpu.VMEM((high * NSENT + NSENT, LANES), F32),
            pltpu.VMEM((n_img, high * NSENT, 3 * LANES), BF16),
            pltpu.VMEM((n_slots + cap, LANES), F32),
            pltpu.VMEM((n_slots // LANES * NSENT + NSENT, LANES), F32),
            pltpu.VMEM((tiles_here, LANES, length), BF16),
            pltpu.VMEM((length // LANES, 16 * tiles_here + 16, LANES), F32),
            pltpu.VMEM((length // LANES, 32 * tiles_here + 32, LANES), F32),
            pltpu.VMEM((length // LANES, 32 * tiles_here + 32, LANES), F32),
            pltpu.VMEM((tiles_here, 32, pix), BF16),
            pltpu.VMEM((tiles_here, pix, 32), BF16),
            pltpu.VMEM((tiles_here, length), F32),
            pltpu.VMEM((length // LANES, 9 * tiles_here, LANES), F32),
            pltpu.VMEM((length // LANES, 4 * tiles_here, LANES), F32),
            pltpu.VMEM((length // LANES, 16 * tiles_here + 16, LANES), F32),
            pltpu.VMEM((n_img, 3, 16, LANES), F32),
            pltpu.SemaphoreType.DMA((3,)),
            pltpu.SemaphoreType.DMA((3,)),
            pltpu.SemaphoreType.DMA((3,)),
        ],
        compiler_params=pltpu.CompilerParams(
            collective_id=0, has_side_effects=True, vmem_limit_bytes=60 * 1024 * 1024
        ),
    )(
        *small,
        sh_coeffs,
        cameras,
        requests.reshape(devices, 1, cap),
        lists[0],
        counts,
        image_cot,
    )
    return pl.pallas_call(
        functools.partial(owner_kernel, (n_img, n_tile, cap)),
        out_shape=(
            image_shape,
            jax.ShapeDtypeStruct((rows, owned), F32),
            jax.ShapeDtypeStruct(cameras.shape, F32),
        ),
        in_specs=[vmem] * 5 + [smem] + [vmem] * 4,
        out_specs=(vmem,) * 3,
        scratch_shapes=[
            pltpu.VMEM((few * high + high, LANES), F32),
            pltpu.VMEM((n_slots + cap, LANES), F32),
            pltpu.VMEM((rows * high + high, LANES), F32),
        ],
        compiler_params=pltpu.CompilerParams(vmem_limit_bytes=60 * 1024 * 1024),
    )(*small, cameras, back, asked, harm, rendered)


def solution(mesh):
    owners = P(None, ("img", "tile"))
    images = P("img", None, "tile", None)
    return jax.shard_map(
        local,
        mesh=mesh,
        in_specs=(owners,) * 6
        + (P(), P("img", "tile", None, None, None), P("img", "tile", None), P("img", "tile"), images),
        out_specs=(images, owners, P()),
        check_vma=False,
    )
```

```python
import functools
import math

import jax
import jax.numpy as jnp
from jax import lax
from jax.experimental import pallas as pl
from jax.experimental.pallas import tpu as pltpu
from jax.sharding import PartitionSpec as P

TILE_SIDE = 16
TW = 16
NFEAT = 9
NSENT = 24
NBACK = 16
LANES = 128
F32 = jnp.float32
BF16 = jnp.bfloat16
MESH = pl.DeviceIdType.MESH

sh_first = 0.28209479177387814
sh_second = 0.4886025119029199
sh_third = (
    1.0925484305920792,
    -1.0925484305920792,
    0.31539156525252005,
    -1.0925484305920792,
    0.5462742152960396,
)
sh_fourth = (
    -0.5900435899266435,
    2.890611442640554,
    -0.4570457994644658,
    0.3731763325901154,
    -0.4570457994644658,
    1.445305721320277,
    -0.5900435899266435,
)
dilation = 0.3


def harmonics(x, y, z):
    xx, yy, zz = x * x, y * y, z * z
    zero = jnp.zeros_like(x)
    a, b = sh_third, sh_fourth
    c = sh_second
    values = [
        zero + sh_first,
        -c * y,
        c * z,
        -c * x,
        a[0] * x * y,
        a[1] * y * z,
        a[2] * (2.0 * zz - xx - yy),
        a[3] * x * z,
        a[4] * (xx - yy),
        b[0] * y * (3.0 * xx - yy),
        b[1] * x * y * z,
        b[2] * y * (4.0 * zz - xx - yy),
        b[3] * z * (2.0 * zz - 3.0 * xx - 3.0 * yy),
        b[4] * x * (4.0 * zz - xx - yy),
        b[5] * z * (xx - yy),
        b[6] * x * (xx - 3.0 * yy),
    ]
    by_x = [
        zero,
        zero,
        zero,
        zero - c,
        a[0] * y,
        zero,
        -2.0 * a[2] * x,
        a[3] * z,
        2.0 * a[4] * x,
        6.0 * b[0] * x * y,
        b[1] * y * z,
        -2.0 * b[2] * x * y,
        -6.0 * b[3] * x * z,
        b[4] * (4.0 * zz - 3.0 * xx - yy),
        2.0 * b[5] * x * z,
        b[6] * (3.0 * xx - 3.0 * yy),
    ]
    by_y = [
        zero,
        zero - c,
        zero,
        zero,
        a[0] * x,
        a[1] * z,
        -2.0 * a[2] * y,
        zero,
        -2.0 * a[4] * y,
        b[0] * (3.0 * xx - 3.0 * yy),
        b[1] * x * z,
        b[2] * (4.0 * zz - xx - 3.0 * yy),
        -6.0 * b[3] * y * z,
        -2.0 * b[4] * x * y,
        -2.0 * b[5] * y * z,
        -6.0 * b[6] * x * y,
    ]
    by_z = [
        zero,
        zero,
        zero + c,
        zero,
        zero,
        a[1] * y,
        4.0 * a[2] * z,
        a[3] * x,
        zero,
        zero,
        b[1] * x * y,
        8.0 * b[2] * y * z,
        b[3] * (6.0 * zz - 3.0 * xx - 3.0 * yy),
        8.0 * b[4] * x * z,
        b[5] * (xx - yy),
        zero,
    ]
    return values, by_x, by_y, by_z


def split(value, parts):
    terms, rest = [], value
    for at in range(parts):
        term = rest.astype(BF16).astype(F32)
        terms.append(term)
        if at < parts - 1:
            rest = rest - term
    return terms


def dot(a, b):
    return jnp.dot(a, b, preferred_element_type=F32)


def dot_nt(a, b):
    return lax.dot_general(a, b, (((1,), (1,)), ((), ())), preferred_element_type=F32)


def conic(cam, sigma):
    a0, a1 = cam[0:3], cam[3:6]

    def times(a):
        return (
            a[0] * sigma[0] + a[1] * sigma[1] + a[2] * sigma[2],
            a[0] * sigma[1] + a[1] * sigma[3] + a[2] * sigma[4],
            a[0] * sigma[2] + a[1] * sigma[4] + a[2] * sigma[5],
        )

    v0, v1 = times(a0), times(a1)
    s00 = a0[0] * v0[0] + a0[1] * v0[1] + a0[2] * v0[2] + dilation
    s01 = a1[0] * v0[0] + a1[1] * v0[1] + a1[2] * v0[2]
    s11 = a1[0] * v1[0] + a1[1] * v1[1] + a1[2] * v1[2] + dilation
    inverse = 1.0 / (s00 * s11 - s01 * s01)
    return v0, v1, (s11 * inverse, -s01 * inverse, s00 * inverse)


def cov_grad(con, grad):
    ca, cb, cc = con
    ga, gb, gc = grad[0], 0.5 * grad[1], grad[2]
    p00, p01 = ca * ga + cb * gb, ca * gb + cb * gc
    p10, p11 = cb * ga + cc * gb, cb * gb + cc * gc
    return (
        -(p00 * ca + p01 * cb),
        -(p00 * cb + p01 * cc),
        -(p10 * cb + p11 * cc),
    )


def rotation_of(quat):
    w, x, y, z = quat
    return (
        (1.0 - 2.0 * (y * y + z * z), 2.0 * (x * y - w * z), 2.0 * (x * z + w * y)),
        (2.0 * (x * y + w * z), 1.0 - 2.0 * (x * x + z * z), 2.0 * (y * z - w * x)),
        (2.0 * (x * z - w * y), 2.0 * (y * z + w * x), 1.0 - 2.0 * (x * x + y * y)),
    )


def load_dense(refs, dense):
    at = 0
    for ref in refs:
        rows, owned = ref.shape
        high = owned // LANES
        for h in range(high):
            part = ref[:, h * LANES : (h + 1) * LANES]
            if rows == 1:
                dense[at * high + h : at * high + h + 1, :] = part
            else:
                dense[pl.ds(at * high + h, rows, stride=high), :] = part
        at += rows


def geometry(row):
    raw = tuple(row(6 + a) for a in range(4))
    inverse = 1.0 / jnp.sqrt(
        raw[0] * raw[0] + raw[1] * raw[1] + raw[2] * raw[2] + raw[3] * raw[3]
    )
    quat = tuple(part * inverse for part in raw)
    rot = rotation_of(quat)
    squares = tuple(jnp.exp(2.0 * row(3 + a)) for a in range(3))

    def entry(a, b):
        return (
            rot[a][0] * rot[b][0] * squares[0]
            + rot[a][1] * rot[b][1] * squares[1]
            + rot[a][2] * rot[b][2] * squares[2]
        )

    sigma = tuple(entry(a, b) for a, b in ((0, 0), (0, 1), (0, 2), (1, 1), (1, 2), (2, 2)))
    return quat, inverse, rot, squares, sigma


def mask_of(index, rows):
    return lax.broadcasted_iota(jnp.int32, (rows, index.shape[1]), 0) == index


def as_bf16(mask):
    return mask.astype(F32).astype(BF16)


def two(value):
    hi = value.astype(BF16)
    return hi, (value - hi.astype(F32)).astype(BF16)


def scatter_rows(ref, start, stride, value):
    for h in range(ref.shape[0]):
        ref[h, pl.ds(start, value.shape[0], stride=stride), :] = value[
            :, h * LANES : (h + 1) * LANES
        ]


def take_rows(ref, rows):
    return jnp.concatenate([ref[h, rows, :] for h in range(ref.shape[0])], axis=1)


def render_kernel(
    sizes,
    means_hbm,
    log_scales_hbm,
    quat_w_hbm,
    quat_v_hbm,
    opacity_hbm,
    sh_hbm,
    cams,
    requests,
    lists_hbm,
    counts,
    cot_hbm,
    rendered,
    back_out,
    ask_out,
    harm_out,
    means,
    log_scales,
    quat_w,
    quat_v,
    opacity,
    sh,
    lists,
    cot,
    in_sem,
    ask_mid,
    ask_recv,
    feat_send,
    feat_mid,
    feat_recv,
    grad_send,
    grad_mid,
    grad_recv,
    dense,
    project,
    feats,
    slots,
    by_slot,
    low,
    gots,
    coefs,
    colours,
    cots,
    cots_t,
    live_op,
    moments,
    tints,
    grads,
    harm,
    first_send,
    first_recv,
    second_send,
    second_recv,
    own_sem,
):
    n_img, n_tile, cap, tiles_here, length, pix = sizes
    owned = means.shape[1]
    high = owned // LANES
    devices = n_img * n_tile
    n_slots = devices * cap
    groups = n_slots // LANES
    per_img = n_tile * cap
    my_tile = lax.axis_index("tile")
    my_img = lax.axis_index("img")
    me = my_img * n_tile + my_tile

    above = math.gcd(n_tile, 4)
    below = n_tile // above
    my_high, my_low = my_tile // below, lax.rem(my_tile, below)
    plane = n_img * below
    my_place = my_img * below + my_low

    def along(k):
        other = lax.rem(my_high + k, above)
        return other, (my_img, other * below + my_low)

    def across(k):
        other = lax.rem(my_place + k, plane)
        img, place = other // below, lax.rem(other, below)
        return img, place, (img, my_high * below + place)

    loads = [
        pltpu.make_async_copy(source, target, in_sem.at[at])
        for at, (source, target) in enumerate(
            (
                (means_hbm, means),
                (log_scales_hbm, log_scales),
                (quat_w_hbm, quat_w),
                (quat_v_hbm, quat_v),
                (opacity_hbm, opacity),
                (sh_hbm, sh),
                (lists_hbm, lists),
                (cot_hbm, cot),
            )
        )
    ]
    for load in loads:
        load.start()

    barrier = pltpu.get_barrier_semaphore()

    for k in range(1, above):
        pl.semaphore_signal(barrier, inc=1, device_id=along(k)[1], device_id_type=MESH)

    @pl.loop(1, plane)
    def _(k):
        pl.semaphore_signal(barrier, inc=1, device_id=across(k)[2], device_id_type=MESH)

    def first_copy(at, source, middle, k):
        other, where = along(k)
        return pltpu.make_async_remote_copy(
            src_ref=source.at[:, other],
            dst_ref=middle.at[:, my_high],
            send_sem=first_send.at[at, k],
            recv_sem=first_recv.at[at, k],
            device_id=where,
            device_id_type=MESH,
        )

    def second_copy(at, middle, target, k):
        img, place, where = across(k)
        return pltpu.make_async_remote_copy(
            src_ref=middle.at[img, :, place],
            dst_ref=target.at[my_img, :, my_low],
            send_sem=second_send.at[at, k],
            recv_sem=second_recv.at[at, k],
            device_id=where,
            device_id_type=MESH,
        )

    def begin(at, source, middle):
        for k in range(1, above):
            first_copy(at, source, middle, k).start()
        pltpu.make_async_copy(
            source.at[:, my_high], middle.at[:, my_high], own_sem.at[at, 0]
        ).start()

    def finish(at, source, middle, target):
        pltpu.make_async_copy(
            source.at[:, my_high], middle.at[:, my_high], own_sem.at[at, 0]
        ).wait()
        for k in range(1, above):
            first_copy(at, source, middle, k).wait_recv()

        @pl.loop(1, plane)
        def _(k):
            second_copy(at, middle, target, k).start()

        mine = pltpu.make_async_copy(
            middle.at[my_img, :, my_low], target.at[my_img, :, my_low], own_sem.at[at, 1]
        )
        mine.start()
        for k in range(1, above):
            first_copy(at, source, middle, k).wait_send()
        mine.wait()

        @pl.loop(1, plane)
        def _(k):
            second_copy(at, middle, target, k).wait_recv()

    def sent(at, middle, target):
        @pl.loop(1, plane)
        def _(k):
            second_copy(at, middle, target, k).wait_send()

    cam = [[cams[i, c] for c in range(10)] for i in range(n_img)]
    img_rows = -(-n_img // 8) * 8
    img_row = lax.broadcasted_iota(jnp.int32, (img_rows, LANES), 0)
    polar = jnp.zeros((img_rows, LANES), F32)
    azimuth = jnp.zeros((img_rows, LANES), F32)
    for i in range(n_img):
        polar = jnp.where(img_row == i, cam[i][8], polar)
        azimuth = jnp.where(img_row == i, cam[i][9], azimuth)
    sp, cp = jnp.sin(polar), jnp.cos(polar)
    sz, cz = jnp.sin(azimuth), jnp.cos(azimuth)
    values, by_x, by_y, by_z = harmonics(sp * cz, sp * sz, cp)
    for m in range(16):
        by_polar = by_x[m] * (cp * cz) + by_y[m] * (cp * sz) - by_z[m] * sp
        by_azimuth = by_y[m] * (sp * cz) - by_x[m] * (sp * sz)
        for i in range(n_img):
            harm[i, 0, m : m + 1, :] = values[m][i : i + 1]
            harm[i, 1, m : m + 1, :] = by_polar[i : i + 1]
            harm[i, 2, m : m + 1, :] = by_azimuth[i : i + 1]
    for i in range(n_img):
        harm_out[i] = harm[i, 0]
    for load in loads[:6]:
        load.wait()
    load_dense((means, log_scales, quat_w, quat_v, opacity, sh), dense)

    pl.semaphore_wait(barrier, above + plane - 2)
    begin(0, requests, ask_mid)

    def row(at):
        return dense[at * high : (at + 1) * high, :]

    _, _, _, _, sigma = geometry(row)
    mean = tuple(row(a) for a in range(3))
    base = 1.0 / (1.0 + jnp.exp(-row(10)))
    for i in range(n_img):
        c = cam[i]
        _, _, con = conic(c, sigma)
        rows = [
            c[0] * mean[0] + c[1] * mean[1] + c[2] * mean[2] + c[6],
            c[3] * mean[0] + c[4] * mean[1] + c[5] * mean[2] + c[7],
            con[0],
            con[1],
            con[2],
            base,
        ]
        sums = [[None] * 3 for _ in range(3)]
        for k in range(3):
            for m in range(16):
                coeff = row(11 + 16 * k + m)
                for d in range(3):
                    term = coeff * harm[i, d, m : m + 1, :]
                    sums[d][k] = term if m == 0 else sums[d][k] + term
        rows += [total + 0.5 for total in sums[0]] + list(mean) + list(sigma) + sums[1] + sums[2]
        for at, value in enumerate(rows):
            project[pl.ds(at, high, stride=NSENT), :] = value
        for at, term in enumerate(split(project[0 : high * NSENT, :], 3)):
            feats[i, :, at * LANES : (at + 1) * LANES] = term.astype(BF16)

    for load in loads[6:]:
        load.wait()
    coefs[...] = jnp.zeros_like(coefs)
    colours[...] = jnp.zeros_like(colours)
    for j in range(tiles_here):
        low[j] = as_bf16(mask_of(jnp.bitwise_and(lists[j : j + 1, :], LANES - 1), LANES))
        cot3 = jnp.concatenate([cot[0, k, j : j + 1, :] for k in range(3)], axis=0)
        c1, c2, c3 = split(cot3, 3)
        stack = jnp.concatenate([c1, c1, c2, c2, c1, c3, jnp.zeros((14, pix), F32)], axis=0)
        cots[j] = stack.astype(BF16)
        cots_t[j] = jnp.transpose(stack).astype(BF16)

    def basis_of(pixel, which):
        half = 0.5 * TILE_SIDE - 0.5
        x = lax.rem(pixel, TILE_SIDE).astype(F32) - half
        y = (pixel // TILE_SIDE).astype(F32) - half
        out = jnp.where(which == 0, 1.0, 0.0)
        for at, term in enumerate((x, y, x * x, x * y, y * y)):
            out = jnp.where(which == at + 1, term, out)
        return out.astype(BF16)

    basis_pe = basis_of(
        lax.broadcasted_iota(jnp.int32, (pix, 32), 0),
        lax.rem(lax.broadcasted_iota(jnp.int32, (pix, 32), 1), 8),
    )
    basis_ep = basis_of(
        lax.broadcasted_iota(jnp.int32, (16, pix), 1), lax.broadcasted_iota(jnp.int32, (16, pix), 0)
    )
    first = lax.broadcasted_iota(jnp.int32, (length, length), 0)
    second = lax.broadcasted_iota(jnp.int32, (length, length), 1)
    before = as_bf16(first < second)
    after = as_bf16(first > second)
    height = TILE_SIDE * tiles_here * n_tile / TW

    finish(0, requests, ask_mid, ask_recv)
    asks = ask_recv[...].reshape(devices, cap)
    halves = jnp.concatenate(
        [(asks // LANES).astype(F32), jnp.bitwise_and(asks, LANES - 1).astype(F32)], axis=0
    ).astype(BF16)
    repeat = as_bf16(
        lax.rem(lax.broadcasted_iota(jnp.int32, (cap, n_slots), 1), cap)
        == lax.broadcasted_iota(jnp.int32, (cap, n_slots), 0)
    )
    wide = dot(halves, repeat)
    here = (
        lax.broadcasted_iota(jnp.int32, (devices, n_slots), 1) // cap
        == lax.broadcasted_iota(jnp.int32, (devices, n_slots), 0)
    )
    ask_hi, ask_lo = (
        jnp.sum(
            jnp.where(here, wide[at * devices : (at + 1) * devices], 0.0), axis=0, keepdims=True
        ).astype(jnp.int32)
        for at in range(2)
    )
    ask_out[0:1, :] = ask_hi
    ask_out[1:2, :] = ask_lo
    for i in range(n_img):
        lanes = slice(i * per_img, (i + 1) * per_img)
        mask = as_bf16(mask_of(ask_lo[:, lanes], LANES))
        got = dot(feats[i], jnp.concatenate([mask] * 3, axis=0))
        pick = mask_of(ask_hi[:, lanes], high).astype(F32)
        total = got[0:NSENT] * pick[0:1]
        for h in range(1, high):
            total = total + got[h * NSENT : (h + 1) * NSENT] * pick[h : h + 1]
        slots[lanes, 0:NSENT] = jnp.transpose(total)
    feat_send[...] = jnp.concatenate(
        [slots[pl.ds(c, devices, stride=cap), 0:NSENT] for c in range(cap)], axis=1
    ).reshape(feat_send.shape)
    begin(1, feat_send, feat_mid)
    sent(0, ask_mid, ask_recv)
    finish(1, feat_send, feat_mid, feat_recv)
    packed = feat_recv[...].reshape(devices, cap * NSENT)
    for c in range(cap):
        slots[pl.ds(c, devices, stride=cap), 0:NSENT] = packed[:, c * NSENT : (c + 1) * NSENT]
    heads = []
    for h in range(groups):
        turned = jnp.transpose(slots[h * LANES : (h + 1) * LANES, :])[0:NSENT]
        by_slot[h * NSENT : (h + 1) * NSENT, :] = turned
        heads.append(turned[0:16])
    heads = jnp.concatenate(
        [term.astype(BF16) for term in split(jnp.concatenate(heads, axis=0), 3)], axis=1
    )

    for j in range(tiles_here):
        got = dot(heads, jnp.concatenate([low[j]] * 3, axis=0))
        group = lists[j : j + 1, :] // LANES
        total = jnp.where(group == 0, got[0:16], 0.0)
        for h in range(1, groups):
            total = total + jnp.where(group == h, got[h * 16 : (h + 1) * 16], 0.0)
        scatter_rows(gots, j, tiles_here, total)

    def feature(at):
        return take_rows(gots, slice(at * tiles_here, (at + 1) * tiles_here))

    tile_row = lax.broadcasted_iota(jnp.int32, (tiles_here, length), 0)
    number = my_tile * tiles_here + tile_row
    lx = feature(0) - (
        (lax.rem(number, TW) * TILE_SIDE).astype(F32) + 0.5 * TILE_SIDE * (1 - TW)
    )
    ly = feature(1) - ((number // TW * TILE_SIDE).astype(F32) + 0.5 * TILE_SIDE - 0.5 * height)
    ca, cb, cc, op = (feature(at) for at in range(2, 6))
    ux = ca * lx + cb * ly
    uy = cc * ly + cb * lx
    live = jnp.zeros((tiles_here, length), jnp.int32)
    for j in range(tiles_here):
        live = jnp.where(tile_row == j, counts[0, j], live)
    lane = lax.broadcasted_iota(jnp.int32, (tiles_here, length), 1)
    live_op[...] = jnp.where(lane < live, op, 0.0)
    for at, value in enumerate((-0.5 * (ux * lx + uy * ly), ux, uy, -0.5 * ca, -cb, -0.5 * cc)):
        for term_at, term in enumerate(split(value, 3)):
            scatter_rows(coefs, 8 * term_at + at, 32, term)
    for k in range(3):
        terms = split(feature(6 + k), 3)
        for at, term_at in enumerate((0, 1, 0, 1, 2, 0)):
            scatter_rows(colours, 3 * at + k, 32, terms[term_at])

    def render(j):
        rows = pl.ds(pl.multiple_of(j * 32, 32), 32)
        power = dot(basis_pe, take_rows(coefs, rows).astype(BF16))
        alpha = live_op[pl.ds(j, 1), :] * jnp.exp(power)
        keep = 1.0 - alpha
        hi, lo = two(jnp.log(keep))
        weight = alpha * jnp.exp(dot(hi, before) + dot(lo, before))
        hi, lo = two(weight)
        colour = take_rows(colours, rows).astype(BF16)
        image = dot_nt(colour, hi) + dot_nt(colour, lo)
        for k in range(3):
            rendered[0, k, pl.ds(j, 1), :] = (
                image[k : k + 1] + image[k + 3 : k + 4] + image[k + 12 : k + 13]
            )
        tint = dot(cots[j], hi) + dot(cots[j], lo)
        scatter_rows(tints, j, tiles_here, tint[0:3] + tint[6:9] + tint[15:18])
        pulled = dot(cots_t[j], colour) * weight
        hi, lo = two(pulled)
        later = dot(hi, after) + dot(lo, after)
        rough = pl.reciprocal(keep, approx=True)
        hi, lo = two(pulled - later * (alpha * (rough * (2.0 - keep * rough))))
        moment = dot(basis_ep, hi) + dot(basis_ep, lo)
        scatter_rows(moments, j, tiles_here, moment[0:8])

    step = 2 if tiles_here % 2 == 0 else 1

    @pl.loop(0, tiles_here // step)
    def _(at):
        for more in range(step):
            render(at * step + more)

    def moment(at):
        return take_rows(moments, slice(at * tiles_here, (at + 1) * tiles_here))

    m0, mx, my = moment(0), moment(1), moment(2)
    nx, ny = mx - lx * m0, my - ly * m0
    nxx = moment(3) - 2.0 * lx * mx + lx * lx * m0
    nxy = moment(4) - lx * my - ly * mx + lx * ly * m0
    nyy = moment(5) - 2.0 * ly * my + ly * ly * m0
    grads[...] = jnp.zeros_like(grads)
    for at, value in enumerate(
        (ca * nx + cb * ny, cc * ny + cb * nx, -0.5 * nxx, -nxy, -0.5 * nyy, m0 / op)
    ):
        scatter_rows(grads, at, 16, value)
    for k in range(3):
        scatter_rows(
            grads, 6 + k, 16, take_rows(tints, slice(k * tiles_here, (k + 1) * tiles_here))
        )
    back = 0.0
    for j in range(tiles_here):
        hi, lo = split(take_rows(grads, slice(16 * j, 16 * (j + 1))), 2)
        group = lists[j : j + 1, :] // LANES
        spread = [
            jnp.where(group == h, term, 0.0) for h in range(groups) for term in (hi, lo)
        ]
        back = back + dot_nt(jnp.concatenate(spread, axis=0).astype(BF16), low[j])
    slot_rows = [back[32 * h : 32 * h + 16] + back[32 * h + 16 : 32 * h + 32] for h in range(groups)]

    g = [
        jnp.concatenate([rows[at : at + 1] for rows in slot_rows], axis=0) for at in range(NFEAT)
    ]
    f = [by_slot[pl.ds(at, groups, stride=NSENT), :] for at in range(NSENT)]
    c = [cams[my_img, at] for at in range(10)]
    v0, v1, _ = conic(c, f[12:18])
    h = cov_grad((f[2], f[3], f[4]), (g[2], g[3], g[4]))
    shares = [g[0] * f[9 + a] + 2.0 * (h[0] * v0[a] + h[1] * v1[a]) for a in range(3)]
    shares += [g[1] * f[9 + a] + 2.0 * (h[2] * v1[a] + h[1] * v0[a]) for a in range(3)]
    shares += [g[0], g[1]]
    shares += [sum(g[6 + k] * f[18 + 3 * d + k] for k in range(3)) for d in range(2)]
    slot_lane = lax.rem(lax.broadcasted_iota(jnp.int32, (16, LANES), 1), cap)
    is_camera = lax.broadcasted_iota(jnp.int32, (16, LANES), 0) == NFEAT
    camera_row = jnp.zeros((1, LANES), F32)
    for at, share in enumerate(shares):
        total = jnp.sum(jnp.sum(share, axis=0, keepdims=True), axis=1, keepdims=True)
        camera_row = jnp.where(slot_lane[0:1] == at, total, camera_row)
    for at, rows in enumerate(slot_rows):
        slots[at * LANES : (at + 1) * LANES, 0:NBACK] = jnp.transpose(
            jnp.where(is_camera, camera_row, rows)
        )
    grad_send[...] = jnp.concatenate(
        [slots[pl.ds(c, devices, stride=cap), 0:NBACK] for c in range(cap)], axis=1
    ).reshape(grad_send.shape)
    begin(2, grad_send, grad_mid)
    sent(1, feat_mid, feat_recv)
    finish(2, grad_send, grad_mid, grad_recv)
    back_out[...] = grad_recv[...].reshape(devices, cap * NBACK)
    sent(2, grad_mid, grad_recv)


def owner_kernel(
    sizes,
    means,
    log_scales,
    quat_w,
    quat_v,
    opacity,
    cams,
    back,
    asked,
    harm,
    rendered_in,
    rendered,
    param_grad,
    camera_grad,
    dense,
    slots,
    result,
):
    n_img, n_tile, cap = sizes
    owned = means.shape[1]
    high = owned // LANES
    devices = n_img * n_tile
    per_img = n_tile * cap
    rendered[...] = rendered_in[...]
    load_dense((means, log_scales, quat_w, quat_v, opacity), dense)

    def row(at):
        return dense[at * high : (at + 1) * high, :]

    quat, inverse, rot, squares, sigma = geometry(row)
    base = 1.0 / (1.0 + jnp.exp(-row(10)))
    packed = back[...]
    for c in range(cap):
        slots[pl.ds(c, devices, stride=cap), 0:NBACK] = packed[:, c * NBACK : (c + 1) * NBACK]
    g_mean = [0.0, 0.0, 0.0]
    g_base = 0.0
    g_sigma = [[0.0] * 3 for _ in range(3)]
    g_colour = []
    for i in range(n_img):
        mine = jnp.concatenate(
            [
                jnp.transpose(slots[at : at + LANES, :])[0:NBACK]
                for at in range(i * per_img, (i + 1) * per_img, LANES)
            ],
            axis=1,
        )
        fold = mine[NFEAT : NFEAT + 1, 0:LANES]
        for at in range(LANES, per_img, LANES):
            fold = fold + mine[NFEAT : NFEAT + 1, at : at + LANES]
        shift = LANES // 2
        while shift >= cap:
            fold = fold + pltpu.roll(fold, shift, 1)
            shift //= 2
        camera_grad[i : i + 1, :] = fold[:, 0:10]
        lanes = slice(i * per_img, (i + 1) * per_img)
        pick = mask_of(asked[0:1, lanes], high)
        low = as_bf16(mask_of(asked[1:2, lanes], LANES))
        spread = jnp.concatenate(
            [
                jnp.concatenate(
                    [jnp.where(pick, term[at : at + 1], 0.0) for at in range(NFEAT)], axis=0
                ).astype(BF16)
                for term in split(mine, 2)
            ],
            axis=1,
        )
        full = dot_nt(spread, jnp.concatenate([low] * 2, axis=1))
        g = [full[at * high : (at + 1) * high] for at in range(NFEAT)]
        c = [cams[i, at] for at in range(8)]
        _, _, con = conic(c, sigma)
        h = cov_grad(con, (g[2], g[3], g[4]))
        for a in range(3):
            g_mean[a] = g_mean[a] + c[a] * g[0] + c[3 + a] * g[1]
            for b in range(a, 3):
                g_sigma[a][b] = (
                    g_sigma[a][b]
                    + (c[a] * c[b]) * h[0]
                    + (c[a] * c[3 + b] + c[3 + a] * c[b]) * h[1]
                    + (c[3 + a] * c[3 + b]) * h[2]
                )
        g_base = g_base + g[5]
        g_colour.append(g[6:9])

    def put(at, value):
        result[at * high : (at + 1) * high, :] = value

    for k in range(3):
        for m in range(16):
            put(
                11 + 16 * k + m,
                sum(harm[i, m : m + 1, :] * g_colour[i][k] for i in range(n_img)),
            )
    for a in range(3):
        put(a, g_mean[a])
        for b in range(a):
            g_sigma[a][b] = g_sigma[b][a]
    r = [[None] * 3 for _ in range(3)]
    for b in range(3):
        pull = [
            g_sigma[a][0] * rot[0][b] + g_sigma[a][1] * rot[1][b] + g_sigma[a][2] * rot[2][b]
            for a in range(3)
        ]
        twice = 2.0 * squares[b]
        for a in range(3):
            r[a][b] = twice * pull[a]
        put(3 + b, r[0][b] * rot[0][b] + r[1][b] * rot[1][b] + r[2][b] * rot[2][b])
    w, x, y, z = quat
    g_quat = (
        z * (r[1][0] - r[0][1]) + y * (r[0][2] - r[2][0]) + x * (r[2][1] - r[1][2]),
        y * (r[0][1] + r[1][0])
        + z * (r[0][2] + r[2][0])
        + w * (r[2][1] - r[1][2])
        - 2.0 * x * (r[1][1] + r[2][2]),
        x * (r[0][1] + r[1][0])
        + z * (r[1][2] + r[2][1])
        + w * (r[0][2] - r[2][0])
        - 2.0 * y * (r[0][0] + r[2][2]),
        x * (r[0][2] + r[2][0])
        + y * (r[1][2] + r[2][1])
        + w * (r[1][0] - r[0][1])
        - 2.0 * z * (r[0][0] + r[1][1]),
    )
    along = sum(quat[a] * g_quat[a] for a in range(4))
    for a in range(4):
        put(6 + a, 2.0 * (g_quat[a] - quat[a] * along) * inverse)
    put(10, g_base * base * (1.0 - base))
    rows = param_grad.shape[0]
    for h in range(high):
        param_grad[:, h * LANES : (h + 1) * LANES] = result[pl.ds(h, rows, stride=high), :]


def local(
    means,
    log_scales,
    quat_w,
    quat_v,
    opacity,
    sh_coeffs,
    cameras,
    requests,
    lists,
    counts,
    image_cot,
):
    n_img, n_tile, cap = requests.shape[2:]
    devices = n_img * n_tile
    n_slots = devices * cap
    above = math.gcd(n_tile, 4)
    below = n_tile // above
    grid = (n_img, above, below)
    owned = means.shape[1]
    high = owned // LANES
    tiles_here, length = lists.shape[1:]
    pix = image_cot.shape[3]
    vmem = pl.BlockSpec(memory_space=pltpu.VMEM)
    smem = pl.BlockSpec(memory_space=pltpu.SMEM)
    hbm = pl.BlockSpec(memory_space=pl.ANY)
    small = (means, log_scales, quat_w, quat_v, opacity)
    few = sum(part.shape[0] for part in small)
    rows = few + sh_coeffs.shape[0]
    image_shape = jax.ShapeDtypeStruct(image_cot.shape, F32)
    rendered, back, asked, harm = pl.pallas_call(
        functools.partial(render_kernel, (n_img, n_tile, cap, tiles_here, length, pix)),
        out_shape=(
            image_shape,
            jax.ShapeDtypeStruct((devices, cap * NBACK), F32),
            jax.ShapeDtypeStruct((2, n_slots), jnp.int32),
            jax.ShapeDtypeStruct((n_img, 16, LANES), F32),
        ),
        in_specs=[hbm] * 6 + [smem, hbm, hbm, smem, hbm],
        out_specs=(vmem,) * 4,
        scratch_shapes=[
            *(pltpu.VMEM(part.shape, F32) for part in (*small, sh_coeffs)),
            pltpu.VMEM((tiles_here, length), jnp.int32),
            pltpu.VMEM(image_cot.shape, F32),
            pltpu.SemaphoreType.DMA((8,)),
            *[pltpu.VMEM((*grid, 1, cap), jnp.int32)] * 2,
            *[pltpu.VMEM((*grid, 1, cap * NSENT), F32)] * 3,
            *[pltpu.VMEM((*grid, 1, cap * NBACK), F32)] * 3,
            pltpu.VMEM((rows * high + high, LANES), F32),
            pltpu.VMEM((high * NSENT + NSENT, LANES), F32),
            pltpu.VMEM((n_img, high * NSENT, 3 * LANES), BF16),
            pltpu.VMEM((n_slots + cap, LANES), F32),
            pltpu.VMEM((n_slots // LANES * NSENT + NSENT, LANES), F32),
            pltpu.VMEM((tiles_here, LANES, length), BF16),
            pltpu.VMEM((length // LANES, 16 * tiles_here + 16, LANES), F32),
            pltpu.VMEM((length // LANES, 32 * tiles_here + 32, LANES), F32),
            pltpu.VMEM((length // LANES, 32 * tiles_here + 32, LANES), F32),
            pltpu.VMEM((tiles_here, 32, pix), BF16),
            pltpu.VMEM((tiles_here, pix, 32), BF16),
            pltpu.VMEM((tiles_here, length), F32),
            pltpu.VMEM((length // LANES, 9 * tiles_here, LANES), F32),
            pltpu.VMEM((length // LANES, 4 * tiles_here, LANES), F32),
            pltpu.VMEM((length // LANES, 16 * tiles_here + 16, LANES), F32),
            pltpu.VMEM((n_img, 3, 16, LANES), F32),
            *[pltpu.SemaphoreType.DMA((3, above))] * 2,
            *[pltpu.SemaphoreType.DMA((3, n_img * below))] * 2,
            pltpu.SemaphoreType.DMA((3, 2)),
        ],
        compiler_params=pltpu.CompilerParams(
            collective_id=0, has_side_effects=True, vmem_limit_bytes=60 * 1024 * 1024
        ),
    )(
        *small,
        sh_coeffs,
        cameras,
        requests.reshape(*grid, 1, cap),
        lists[0],
        counts,
        image_cot,
    )
    return pl.pallas_call(
        functools.partial(owner_kernel, (n_img, n_tile, cap)),
        out_shape=(
            image_shape,
            jax.ShapeDtypeStruct((rows, owned), F32),
            jax.ShapeDtypeStruct(cameras.shape, F32),
        ),
        in_specs=[vmem] * 5 + [smem] + [vmem] * 4,
        out_specs=(vmem,) * 3,
        scratch_shapes=[
            pltpu.VMEM((few * high + high, LANES), F32),
            pltpu.VMEM((n_slots + cap, LANES), F32),
            pltpu.VMEM((rows * high + high, LANES), F32),
        ],
        compiler_params=pltpu.CompilerParams(vmem_limit_bytes=60 * 1024 * 1024),
    )(*small, cameras, back, asked, harm, rendered)


def solution(mesh):
    owners = P(None, ("img", "tile"))
    images = P("img", None, "tile", None)
    return jax.shard_map(
        local,
        mesh=mesh,
        in_specs=(owners,) * 6
        + (P(), P("img", "tile", None, None, None), P("img", "tile", None), P("img", "tile"), images),
        out_specs=(images, owners, P()),
        check_vma=False,
    )
```

```python
import functools
import math

import jax
import jax.numpy as jnp
from jax import lax
from jax.experimental import pallas as pl
from jax.experimental.pallas import tpu as pltpu
from jax.sharding import PartitionSpec as P

TILE_SIDE = 16
TW = 16
NFEAT = 9
NSENT = 24
NBACK = 16
LANES = 128
F32 = jnp.float32
BF16 = jnp.bfloat16
MESH = pl.DeviceIdType.MESH

sh_first = 0.28209479177387814
sh_second = 0.4886025119029199
sh_third = (
    1.0925484305920792,
    -1.0925484305920792,
    0.31539156525252005,
    -1.0925484305920792,
    0.5462742152960396,
)
sh_fourth = (
    -0.5900435899266435,
    2.890611442640554,
    -0.4570457994644658,
    0.3731763325901154,
    -0.4570457994644658,
    1.445305721320277,
    -0.5900435899266435,
)
dilation = 0.3


def harmonics(x, y, z):
    xx, yy, zz = x * x, y * y, z * z
    zero = jnp.zeros_like(x)
    a, b = sh_third, sh_fourth
    c = sh_second
    values = [
        zero + sh_first,
        -c * y,
        c * z,
        -c * x,
        a[0] * x * y,
        a[1] * y * z,
        a[2] * (2.0 * zz - xx - yy),
        a[3] * x * z,
        a[4] * (xx - yy),
        b[0] * y * (3.0 * xx - yy),
        b[1] * x * y * z,
        b[2] * y * (4.0 * zz - xx - yy),
        b[3] * z * (2.0 * zz - 3.0 * xx - 3.0 * yy),
        b[4] * x * (4.0 * zz - xx - yy),
        b[5] * z * (xx - yy),
        b[6] * x * (xx - 3.0 * yy),
    ]
    by_x = [
        zero,
        zero,
        zero,
        zero - c,
        a[0] * y,
        zero,
        -2.0 * a[2] * x,
        a[3] * z,
        2.0 * a[4] * x,
        6.0 * b[0] * x * y,
        b[1] * y * z,
        -2.0 * b[2] * x * y,
        -6.0 * b[3] * x * z,
        b[4] * (4.0 * zz - 3.0 * xx - yy),
        2.0 * b[5] * x * z,
        b[6] * (3.0 * xx - 3.0 * yy),
    ]
    by_y = [
        zero,
        zero - c,
        zero,
        zero,
        a[0] * x,
        a[1] * z,
        -2.0 * a[2] * y,
        zero,
        -2.0 * a[4] * y,
        b[0] * (3.0 * xx - 3.0 * yy),
        b[1] * x * z,
        b[2] * (4.0 * zz - xx - 3.0 * yy),
        -6.0 * b[3] * y * z,
        -2.0 * b[4] * x * y,
        -2.0 * b[5] * y * z,
        -6.0 * b[6] * x * y,
    ]
    by_z = [
        zero,
        zero,
        zero + c,
        zero,
        zero,
        a[1] * y,
        4.0 * a[2] * z,
        a[3] * x,
        zero,
        zero,
        b[1] * x * y,
        8.0 * b[2] * y * z,
        b[3] * (6.0 * zz - 3.0 * xx - 3.0 * yy),
        8.0 * b[4] * x * z,
        b[5] * (xx - yy),
        zero,
    ]
    return values, by_x, by_y, by_z


def split(value, parts):
    terms, rest = [], value
    for at in range(parts):
        term = rest.astype(BF16).astype(F32)
        terms.append(term)
        if at < parts - 1:
            rest = rest - term
    return terms


def dot(a, b):
    return jnp.dot(a, b, preferred_element_type=F32)


def dot_nt(a, b):
    return lax.dot_general(a, b, (((1,), (1,)), ((), ())), preferred_element_type=F32)


def conic(cam, sigma):
    a0, a1 = cam[0:3], cam[3:6]

    def times(a):
        return (
            a[0] * sigma[0] + a[1] * sigma[1] + a[2] * sigma[2],
            a[0] * sigma[1] + a[1] * sigma[3] + a[2] * sigma[4],
            a[0] * sigma[2] + a[1] * sigma[4] + a[2] * sigma[5],
        )

    v0, v1 = times(a0), times(a1)
    s00 = a0[0] * v0[0] + a0[1] * v0[1] + a0[2] * v0[2] + dilation
    s01 = a1[0] * v0[0] + a1[1] * v0[1] + a1[2] * v0[2]
    s11 = a1[0] * v1[0] + a1[1] * v1[1] + a1[2] * v1[2] + dilation
    inverse = 1.0 / (s00 * s11 - s01 * s01)
    return v0, v1, (s11 * inverse, -s01 * inverse, s00 * inverse)


def cov_grad(con, grad):
    ca, cb, cc = con
    ga, gb, gc = grad[0], 0.5 * grad[1], grad[2]
    p00, p01 = ca * ga + cb * gb, ca * gb + cb * gc
    p10, p11 = cb * ga + cc * gb, cb * gb + cc * gc
    return (
        -(p00 * ca + p01 * cb),
        -(p00 * cb + p01 * cc),
        -(p10 * cb + p11 * cc),
    )


def rotation_of(quat):
    w, x, y, z = quat
    return (
        (1.0 - 2.0 * (y * y + z * z), 2.0 * (x * y - w * z), 2.0 * (x * z + w * y)),
        (2.0 * (x * y + w * z), 1.0 - 2.0 * (x * x + z * z), 2.0 * (y * z - w * x)),
        (2.0 * (x * z - w * y), 2.0 * (y * z + w * x), 1.0 - 2.0 * (x * x + y * y)),
    )


def load_dense(refs, dense):
    at = 0
    for ref in refs:
        rows, owned = ref.shape
        high = owned // LANES
        for h in range(high):
            part = ref[:, h * LANES : (h + 1) * LANES]
            if rows == 1:
                dense[at * high + h : at * high + h + 1, :] = part
            else:
                dense[pl.ds(at * high + h, rows, stride=high), :] = part
        at += rows


def geometry(row):
    raw = tuple(row(6 + a) for a in range(4))
    inverse = 1.0 / jnp.sqrt(
        raw[0] * raw[0] + raw[1] * raw[1] + raw[2] * raw[2] + raw[3] * raw[3]
    )
    quat = tuple(part * inverse for part in raw)
    rot = rotation_of(quat)
    squares = tuple(jnp.exp(2.0 * row(3 + a)) for a in range(3))

    def entry(a, b):
        return (
            rot[a][0] * rot[b][0] * squares[0]
            + rot[a][1] * rot[b][1] * squares[1]
            + rot[a][2] * rot[b][2] * squares[2]
        )

    sigma = tuple(entry(a, b) for a, b in ((0, 0), (0, 1), (0, 2), (1, 1), (1, 2), (2, 2)))
    return quat, inverse, rot, squares, sigma


def mask_of(index, rows):
    return lax.broadcasted_iota(jnp.int32, (rows, index.shape[1]), 0) == index


def as_bf16(mask):
    return mask.astype(F32).astype(BF16)


def two(value):
    hi = value.astype(BF16)
    return hi, (value - hi.astype(F32)).astype(BF16)


def scatter_rows(ref, start, stride, value):
    for h in range(ref.shape[0]):
        ref[h, pl.ds(start, value.shape[0], stride=stride), :] = value[
            :, h * LANES : (h + 1) * LANES
        ]


def take_rows(ref, rows):
    return jnp.concatenate([ref[h, rows, :] for h in range(ref.shape[0])], axis=1)


def render_kernel(
    sizes,
    means_hbm,
    log_scales_hbm,
    quat_w_hbm,
    quat_v_hbm,
    opacity_hbm,
    sh_hbm,
    cams,
    requests,
    lists_hbm,
    counts,
    cot_hbm,
    rendered,
    back_out,
    ask_out,
    harm_out,
    means,
    log_scales,
    quat_w,
    quat_v,
    opacity,
    sh,
    lists,
    cot,
    in_sem,
    ask_recv,
    feat_send,
    feat_recv,
    grad_send,
    grad_recv,
    dense,
    project,
    feats,
    slots,
    by_slot,
    low,
    gots,
    coefs,
    colours,
    cots,
    cots_t,
    live_op,
    moments,
    tints,
    grads,
    tinted,
    pictures,
    harm,
    send_sem,
    recv_sem,
    own_sem,
):
    n_img, n_tile, cap, tiles_here, length, pix = sizes
    owned = means.shape[1]
    high = owned // LANES
    devices = n_img * n_tile
    n_slots = devices * cap
    groups = n_slots // LANES
    per_img = n_tile * cap
    my_tile = lax.axis_index("tile")
    my_img = lax.axis_index("img")
    me = my_img * n_tile + my_tile

    def peer(k):
        other = lax.rem(me + k, devices)
        return other, (other // n_tile, lax.rem(other, n_tile))

    loads = [
        pltpu.make_async_copy(source, target, in_sem.at[at])
        for at, (source, target) in enumerate(
            (
                (means_hbm, means),
                (log_scales_hbm, log_scales),
                (quat_w_hbm, quat_w),
                (quat_v_hbm, quat_v),
                (opacity_hbm, opacity),
                (sh_hbm, sh),
                (lists_hbm, lists),
                (cot_hbm, cot),
            )
        )
    ]
    for load in loads:
        load.start()

    barrier = pltpu.get_barrier_semaphore()

    @pl.loop(1, devices)
    def _(k):
        pl.semaphore_signal(barrier, inc=1, device_id=peer(k)[1], device_id_type=MESH)

    def exchange(at, source, target):
        mine = pltpu.make_async_copy(source.at[me], target.at[me], own_sem.at[at])
        mine.start()

        @pl.loop(1, devices)
        def _(k):
            other, where = peer(k)
            pltpu.make_async_remote_copy(
                src_ref=source.at[other],
                dst_ref=target.at[me],
                send_sem=send_sem.at[at],
                recv_sem=recv_sem.at[at],
                device_id=where,
                device_id_type=MESH,
            ).start()

        return mine

    def arrive(at, target, mine):
        mine.wait()
        others = target.at[pl.ds(0, devices - 1)]
        pltpu.make_async_copy(others, others, recv_sem.at[at]).wait()

    def sent(at, source):
        others = source.at[pl.ds(0, devices - 1)]
        pltpu.make_async_copy(others, others, send_sem.at[at]).wait()

    cam = [[cams[i, c] for c in range(10)] for i in range(n_img)]
    img_rows = -(-n_img // 8) * 8
    img_row = lax.broadcasted_iota(jnp.int32, (img_rows, LANES), 0)
    polar = jnp.zeros((img_rows, LANES), F32)
    azimuth = jnp.zeros((img_rows, LANES), F32)
    for i in range(n_img):
        polar = jnp.where(img_row == i, cam[i][8], polar)
        azimuth = jnp.where(img_row == i, cam[i][9], azimuth)
    sp, cp = jnp.sin(polar), jnp.cos(polar)
    sz, cz = jnp.sin(azimuth), jnp.cos(azimuth)
    values, by_x, by_y, by_z = harmonics(sp * cz, sp * sz, cp)
    for m in range(16):
        by_polar = by_x[m] * (cp * cz) + by_y[m] * (cp * sz) - by_z[m] * sp
        by_azimuth = by_y[m] * (sp * cz) - by_x[m] * (sp * sz)
        for i in range(n_img):
            harm[i, 0, m : m + 1, :] = values[m][i : i + 1]
            harm[i, 1, m : m + 1, :] = by_polar[i : i + 1]
            harm[i, 2, m : m + 1, :] = by_azimuth[i : i + 1]
    for i in range(n_img):
        harm_out[i] = harm[i, 0]
    for load in loads[:6]:
        load.wait()
    load_dense((means, log_scales, quat_w, quat_v, opacity, sh), dense)

    pl.semaphore_wait(barrier, devices - 1)
    asking = exchange(0, requests, ask_recv)

    def row(at):
        return dense[at * high : (at + 1) * high, :]

    _, _, _, _, sigma = geometry(row)
    mean = tuple(row(a) for a in range(3))
    base = 1.0 / (1.0 + jnp.exp(-row(10)))
    for i in range(n_img):
        c = cam[i]
        _, _, con = conic(c, sigma)
        rows = [
            c[0] * mean[0] + c[1] * mean[1] + c[2] * mean[2] + c[6],
            c[3] * mean[0] + c[4] * mean[1] + c[5] * mean[2] + c[7],
            con[0],
            con[1],
            con[2],
            base,
        ]
        sums = [[None] * 3 for _ in range(3)]
        for k in range(3):
            for m in range(16):
                coeff = row(11 + 16 * k + m)
                for d in range(3):
                    term = coeff * harm[i, d, m : m + 1, :]
                    sums[d][k] = term if m == 0 else sums[d][k] + term
        rows += [total + 0.5 for total in sums[0]] + list(mean) + list(sigma) + sums[1] + sums[2]
        for at, value in enumerate(rows):
            project[pl.ds(at, high, stride=NSENT), :] = value
        for at, term in enumerate(split(project[0 : high * NSENT, :], 3)):
            feats[i, :, at * LANES : (at + 1) * LANES] = term.astype(BF16)

    for load in loads[6:]:
        load.wait()
    coefs[...] = jnp.zeros_like(coefs)
    colours[...] = jnp.zeros_like(colours)
    for j in range(tiles_here):
        low[j] = as_bf16(mask_of(jnp.bitwise_and(lists[j : j + 1, :], LANES - 1), LANES))
        cot3 = jnp.concatenate([cot[0, k, j : j + 1, :] for k in range(3)], axis=0)
        c1, c2, c3 = split(cot3, 3)
        stack = jnp.concatenate([c1, c1, c2, c2, c1, c3, jnp.zeros((14, pix), F32)], axis=0)
        cots[j] = stack.astype(BF16)
        cots_t[j] = jnp.transpose(stack).astype(BF16)

    def basis_of(pixel, which):
        half = 0.5 * TILE_SIDE - 0.5
        x = lax.rem(pixel, TILE_SIDE).astype(F32) - half
        y = (pixel // TILE_SIDE).astype(F32) - half
        out = jnp.where(which == 0, 1.0, 0.0)
        for at, term in enumerate((x, y, x * x, x * y, y * y)):
            out = jnp.where(which == at + 1, term, out)
        return out.astype(BF16)

    basis_pe = basis_of(
        lax.broadcasted_iota(jnp.int32, (pix, 32), 0),
        lax.rem(lax.broadcasted_iota(jnp.int32, (pix, 32), 1), 8),
    )
    basis_ep = basis_of(
        lax.broadcasted_iota(jnp.int32, (16, pix), 1), lax.broadcasted_iota(jnp.int32, (16, pix), 0)
    )
    first = lax.broadcasted_iota(jnp.int32, (length, length), 0)
    second = lax.broadcasted_iota(jnp.int32, (length, length), 1)
    before = as_bf16(first < second)
    after = as_bf16(first > second)
    height = TILE_SIDE * tiles_here * n_tile / TW

    arrive(0, ask_recv, asking)
    asks = ask_recv[...].reshape(devices, cap)
    halves = jnp.concatenate(
        [(asks // LANES).astype(F32), jnp.bitwise_and(asks, LANES - 1).astype(F32)], axis=0
    ).astype(BF16)
    repeat = as_bf16(
        lax.rem(lax.broadcasted_iota(jnp.int32, (cap, n_slots), 1), cap)
        == lax.broadcasted_iota(jnp.int32, (cap, n_slots), 0)
    )
    wide = dot(halves, repeat)
    here = (
        lax.broadcasted_iota(jnp.int32, (devices, n_slots), 1) // cap
        == lax.broadcasted_iota(jnp.int32, (devices, n_slots), 0)
    )
    ask_hi, ask_lo = (
        jnp.sum(
            jnp.where(here, wide[at * devices : (at + 1) * devices], 0.0), axis=0, keepdims=True
        ).astype(jnp.int32)
        for at in range(2)
    )
    ask_out[0:1, :] = ask_hi
    ask_out[1:2, :] = ask_lo
    for i in range(n_img):
        lanes = slice(i * per_img, (i + 1) * per_img)
        mask = as_bf16(mask_of(ask_lo[:, lanes], LANES))
        got = dot(feats[i], jnp.concatenate([mask] * 3, axis=0))
        pick = mask_of(ask_hi[:, lanes], high).astype(F32)
        total = got[0:NSENT] * pick[0:1]
        for h in range(1, high):
            total = total + got[h * NSENT : (h + 1) * NSENT] * pick[h : h + 1]
        slots[lanes, 0:NSENT] = jnp.transpose(total)
        feat_send[i * n_tile : (i + 1) * n_tile] = jnp.concatenate(
            [
                slots[pl.ds(i * per_img + c, n_tile, stride=cap), 0:NSENT]
                for c in range(cap)
            ],
            axis=1,
        ).reshape(n_tile, 1, cap * NSENT)

        @pl.loop(0, n_tile)
        def _(k):
            place = lax.rem(my_tile + k, n_tile)
            other = i * n_tile + place

            @pl.when(other != me)
            def _():
                pltpu.make_async_remote_copy(
                    src_ref=feat_send.at[other],
                    dst_ref=feat_recv.at[me],
                    send_sem=send_sem.at[1],
                    recv_sem=recv_sem.at[1],
                    device_id=(i, place),
                    device_id_type=MESH,
                ).start()

    sending = pltpu.make_async_copy(feat_send.at[me], feat_recv.at[me], own_sem.at[1])
    sending.start()
    sent(0, requests)
    tinted[...] = jnp.zeros_like(tinted)
    pictures[...] = jnp.zeros_like(pictures)
    arrive(1, feat_recv, sending)
    packed = feat_recv[...].reshape(devices, cap * NSENT)
    for c in range(cap):
        slots[pl.ds(c, devices, stride=cap), 0:NSENT] = packed[:, c * NSENT : (c + 1) * NSENT]
    heads = []
    for h in range(groups):
        turned = jnp.transpose(slots[h * LANES : (h + 1) * LANES, :])[0:NSENT]
        by_slot[h * NSENT : (h + 1) * NSENT, :] = turned
        heads.append(turned[0:16])
    heads = jnp.concatenate(
        [term.astype(BF16) for term in split(jnp.concatenate(heads, axis=0), 3)], axis=1
    )

    for j in range(tiles_here):
        got = dot(heads, jnp.concatenate([low[j]] * 3, axis=0))
        group = lists[j : j + 1, :] // LANES
        total = jnp.where(group == 0, got[0:16], 0.0)
        for h in range(1, groups):
            total = total + jnp.where(group == h, got[h * 16 : (h + 1) * 16], 0.0)
        scatter_rows(gots, j, tiles_here, total)

    def feature(at):
        return take_rows(gots, slice(at * tiles_here, (at + 1) * tiles_here))

    tile_row = lax.broadcasted_iota(jnp.int32, (tiles_here, length), 0)
    number = my_tile * tiles_here + tile_row
    lx = feature(0) - (
        (lax.rem(number, TW) * TILE_SIDE).astype(F32) + 0.5 * TILE_SIDE * (1 - TW)
    )
    ly = feature(1) - ((number // TW * TILE_SIDE).astype(F32) + 0.5 * TILE_SIDE - 0.5 * height)
    ca, cb, cc, op = (feature(at) for at in range(2, 6))
    ux = ca * lx + cb * ly
    uy = cc * ly + cb * lx
    live = jnp.zeros((tiles_here, length), jnp.int32)
    for j in range(tiles_here):
        live = jnp.where(tile_row == j, counts[0, j], live)
    lane = lax.broadcasted_iota(jnp.int32, (tiles_here, length), 1)
    live_op[...] = jnp.where(lane < live, op, 0.0)
    for at, value in enumerate((-0.5 * (ux * lx + uy * ly), ux, uy, -0.5 * ca, -cb, -0.5 * cc)):
        for term_at, term in enumerate(split(value, 3)):
            scatter_rows(coefs, 8 * term_at + at, 32, term)
    for k in range(3):
        terms = split(feature(6 + k), 3)
        for at, term_at in enumerate((0, 1, 0, 1, 2, 0)):
            scatter_rows(colours, 3 * at + k, 32, terms[term_at])
        for at in range(2):
            scatter_rows(tinted, at * 4 * tiles_here + k, 4, terms[at])
    painted = jnp.transpose(take_rows(tinted, slice(0, 8 * tiles_here)))
    painted_lane = lax.rem(
        lax.broadcasted_iota(jnp.int32, (length, 8 * tiles_here), 1), 4 * tiles_here
    )

    chunk = 64 if pix % 64 == 0 else pix
    before2 = jnp.concatenate([before, before], axis=0)
    after2 = jnp.concatenate([after, after], axis=0)
    basis2 = jnp.concatenate([basis_ep, basis_ep], axis=1)

    def chunks(function, *arrays):
        parts = [
            function(*(array[at : at + chunk] for array in arrays))
            for at in range(0, pix, chunk)
        ]
        return tuple(jnp.concatenate(part, axis=0) for part in zip(*parts))

    def render(tiles):
        rows = [pl.ds(pl.multiple_of(j * 32, 32), 32) for j in tiles]
        power = [dot(basis_pe, take_rows(coefs, r).astype(BF16)) for r in rows]
        colour = [take_rows(colours, r).astype(BF16) for r in rows]
        opacities = [live_op[pl.ds(j, 1), :] for j in tiles]
        alpha, summed, weight, pair, pull, pulled, later = ([] for _ in range(7))
        for at, j in enumerate(tiles):

            def first_part(p, op_row=opacities[at]):
                a = op_row * jnp.exp(p)
                hi, lo = two(jnp.log(1.0 - a))
                return a, jnp.concatenate([hi, lo], axis=1)

            a, logs = chunks(first_part, power[at])
            alpha.append(a)
            summed.append(dot(logs, before2))
            pull.append(dot(cots_t[j], colour[at]))
        for at, j in enumerate(tiles):

            def second_part(a, total, force):
                w = a * jnp.exp(total)
                p = force * w
                return (*two(w), p, jnp.concatenate(two(p), axis=1))

            hi, lo, p, wide = chunks(second_part, alpha[at], summed[at], pull[at])
            pulled.append(p)
            later.append(dot(wide, after2))
            weight.append(jnp.concatenate([hi, lo], axis=0))
            pair.append(jnp.concatenate([hi, lo], axis=1))
        for at, j in enumerate(tiles):

            def third_part(a, p, l):
                keep = 1.0 - a
                rough = pl.reciprocal(keep, approx=True)
                return two(p - l * (a * (rough * (2.0 - keep * rough))))

            hi, lo = chunks(third_part, alpha[at], pulled[at], later[at])
            moment = dot(basis2, jnp.concatenate([hi, lo], axis=0))
            scatter_rows(moments, j, tiles_here, moment[0:8])
        picture = 0.0
        for at, j in enumerate(tiles):
            cot2 = jnp.concatenate([cots[j], cots[j]], axis=1)
            tint = dot(cot2, weight[at])
            scatter_rows(tints, j, tiles_here, tint[0:3] + tint[6:9] + tint[15:18])
            brush = jnp.where(painted_lane // 4 == j, painted, 0.0).astype(BF16)
            picture = picture + dot(pair[at], jnp.concatenate([brush, brush], axis=0))
        pictures[...] += picture

    step = 2 if tiles_here % 2 == 0 else 1

    @pl.loop(0, tiles_here // step)
    def _(at):
        render([at * step + more for more in range(step)])

    picture = jnp.transpose(pictures[...])
    picture = picture[0 : 4 * tiles_here] + picture[4 * tiles_here : 8 * tiles_here]
    for j in range(tiles_here):
        for k in range(3):
            rendered[0, k, j : j + 1, :] = picture[4 * j + k : 4 * j + k + 1]

    def moment(at):
        return take_rows(moments, slice(at * tiles_here, (at + 1) * tiles_here))

    m0, mx, my = moment(0), moment(1), moment(2)
    nx, ny = mx - lx * m0, my - ly * m0
    nxx = moment(3) - 2.0 * lx * mx + lx * lx * m0
    nxy = moment(4) - lx * my - ly * mx + lx * ly * m0
    nyy = moment(5) - 2.0 * ly * my + ly * ly * m0
    grads[...] = jnp.zeros_like(grads)
    for at, value in enumerate(
        (ca * nx + cb * ny, cc * ny + cb * nx, -0.5 * nxx, -nxy, -0.5 * nyy, m0 / op)
    ):
        scatter_rows(grads, at, 16, value)
    for k in range(3):
        scatter_rows(
            grads, 6 + k, 16, take_rows(tints, slice(k * tiles_here, (k + 1) * tiles_here))
        )
    back = 0.0
    for j in range(tiles_here):
        hi, lo = split(take_rows(grads, slice(16 * j, 16 * (j + 1))), 2)
        group = lists[j : j + 1, :] // LANES
        spread = [
            jnp.where(group == h, term, 0.0) for h in range(groups) for term in (hi, lo)
        ]
        back = back + dot_nt(jnp.concatenate(spread, axis=0).astype(BF16), low[j])
    slot_rows = [back[32 * h : 32 * h + 16] + back[32 * h + 16 : 32 * h + 32] for h in range(groups)]

    g = [
        jnp.concatenate([rows[at : at + 1] for rows in slot_rows], axis=0) for at in range(NFEAT)
    ]
    f = [by_slot[pl.ds(at, groups, stride=NSENT), :] for at in range(NSENT)]
    c = [cams[my_img, at] for at in range(10)]
    v0, v1, _ = conic(c, f[12:18])
    h = cov_grad((f[2], f[3], f[4]), (g[2], g[3], g[4]))
    shares = [g[0] * f[9 + a] + 2.0 * (h[0] * v0[a] + h[1] * v1[a]) for a in range(3)]
    shares += [g[1] * f[9 + a] + 2.0 * (h[2] * v1[a] + h[1] * v0[a]) for a in range(3)]
    shares += [g[0], g[1]]
    shares += [sum(g[6 + k] * f[18 + 3 * d + k] for k in range(3)) for d in range(2)]
    slot_lane = lax.rem(lax.broadcasted_iota(jnp.int32, (16, LANES), 1), cap)
    is_camera = lax.broadcasted_iota(jnp.int32, (16, LANES), 0) == NFEAT
    camera_row = jnp.zeros((1, LANES), F32)
    for at, share in enumerate(shares):
        total = jnp.sum(jnp.sum(share, axis=0, keepdims=True), axis=1, keepdims=True)
        camera_row = jnp.where(slot_lane[0:1] == at, total, camera_row)
    for at, rows in enumerate(slot_rows):
        slots[at * LANES : (at + 1) * LANES, 0:NBACK] = jnp.transpose(
            jnp.where(is_camera, camera_row, rows)
        )
    grad_send[...] = jnp.concatenate(
        [slots[pl.ds(c, devices, stride=cap), 0:NBACK] for c in range(cap)], axis=1
    ).reshape(devices, 1, cap * NBACK)
    returning = exchange(2, grad_send, grad_recv)
    sent(1, feat_send)
    arrive(2, grad_recv, returning)
    back_out[...] = grad_recv[...].reshape(devices, cap * NBACK)
    sent(2, grad_send)


def owner_kernel(
    sizes,
    means,
    log_scales,
    quat_w,
    quat_v,
    opacity,
    cams,
    back,
    asked,
    harm,
    rendered_in,
    rendered,
    param_grad,
    camera_grad,
    dense,
    slots,
    result,
):
    n_img, n_tile, cap = sizes
    owned = means.shape[1]
    high = owned // LANES
    devices = n_img * n_tile
    per_img = n_tile * cap
    rendered[...] = rendered_in[...]
    load_dense((means, log_scales, quat_w, quat_v, opacity), dense)

    def row(at):
        return dense[at * high : (at + 1) * high, :]

    quat, inverse, rot, squares, sigma = geometry(row)
    base = 1.0 / (1.0 + jnp.exp(-row(10)))
    packed = back[...]
    for c in range(cap):
        slots[pl.ds(c, devices, stride=cap), 0:NBACK] = packed[:, c * NBACK : (c + 1) * NBACK]
    g_mean = [0.0, 0.0, 0.0]
    g_base = 0.0
    g_sigma = [[0.0] * 3 for _ in range(3)]
    g_colour = []
    for i in range(n_img):
        mine = jnp.concatenate(
            [
                jnp.transpose(slots[at : at + LANES, :])[0:NBACK]
                for at in range(i * per_img, (i + 1) * per_img, LANES)
            ],
            axis=1,
        )
        fold = mine[NFEAT : NFEAT + 1, 0:LANES]
        for at in range(LANES, per_img, LANES):
            fold = fold + mine[NFEAT : NFEAT + 1, at : at + LANES]
        shift = LANES // 2
        while shift >= cap:
            fold = fold + pltpu.roll(fold, shift, 1)
            shift //= 2
        camera_grad[i : i + 1, :] = fold[:, 0:10]
        lanes = slice(i * per_img, (i + 1) * per_img)
        pick = mask_of(asked[0:1, lanes], high)
        low = as_bf16(mask_of(asked[1:2, lanes], LANES))
        spread = jnp.concatenate(
            [
                jnp.concatenate(
                    [jnp.where(pick, term[at : at + 1], 0.0) for at in range(NFEAT)], axis=0
                ).astype(BF16)
                for term in split(mine, 2)
            ],
            axis=1,
        )
        full = dot_nt(spread, jnp.concatenate([low] * 2, axis=1))
        g = [full[at * high : (at + 1) * high] for at in range(NFEAT)]
        c = [cams[i, at] for at in range(8)]
        _, _, con = conic(c, sigma)
        h = cov_grad(con, (g[2], g[3], g[4]))
        for a in range(3):
            g_mean[a] = g_mean[a] + c[a] * g[0] + c[3 + a] * g[1]
            for b in range(a, 3):
                g_sigma[a][b] = (
                    g_sigma[a][b]
                    + (c[a] * c[b]) * h[0]
                    + (c[a] * c[3 + b] + c[3 + a] * c[b]) * h[1]
                    + (c[3 + a] * c[3 + b]) * h[2]
                )
        g_base = g_base + g[5]
        g_colour.append(g[6:9])

    def put(at, value):
        result[at * high : (at + 1) * high, :] = value

    for k in range(3):
        for m in range(16):
            put(
                11 + 16 * k + m,
                sum(harm[i, m : m + 1, :] * g_colour[i][k] for i in range(n_img)),
            )
    for a in range(3):
        put(a, g_mean[a])
        for b in range(a):
            g_sigma[a][b] = g_sigma[b][a]
    r = [[None] * 3 for _ in range(3)]
    for b in range(3):
        pull = [
            g_sigma[a][0] * rot[0][b] + g_sigma[a][1] * rot[1][b] + g_sigma[a][2] * rot[2][b]
            for a in range(3)
        ]
        twice = 2.0 * squares[b]
        for a in range(3):
            r[a][b] = twice * pull[a]
        put(3 + b, r[0][b] * rot[0][b] + r[1][b] * rot[1][b] + r[2][b] * rot[2][b])
    w, x, y, z = quat
    g_quat = (
        z * (r[1][0] - r[0][1]) + y * (r[0][2] - r[2][0]) + x * (r[2][1] - r[1][2]),
        y * (r[0][1] + r[1][0])
        + z * (r[0][2] + r[2][0])
        + w * (r[2][1] - r[1][2])
        - 2.0 * x * (r[1][1] + r[2][2]),
        x * (r[0][1] + r[1][0])
        + z * (r[1][2] + r[2][1])
        + w * (r[0][2] - r[2][0])
        - 2.0 * y * (r[0][0] + r[2][2]),
        x * (r[0][2] + r[2][0])
        + y * (r[1][2] + r[2][1])
        + w * (r[1][0] - r[0][1])
        - 2.0 * z * (r[0][0] + r[1][1]),
    )
    along = sum(quat[a] * g_quat[a] for a in range(4))
    for a in range(4):
        put(6 + a, 2.0 * (g_quat[a] - quat[a] * along) * inverse)
    put(10, g_base * base * (1.0 - base))
    rows = param_grad.shape[0]
    for h in range(high):
        param_grad[:, h * LANES : (h + 1) * LANES] = result[pl.ds(h, rows, stride=high), :]


def local(
    means,
    log_scales,
    quat_w,
    quat_v,
    opacity,
    sh_coeffs,
    cameras,
    requests,
    lists,
    counts,
    image_cot,
):
    n_img, n_tile, cap = requests.shape[2:]
    devices = n_img * n_tile
    n_slots = devices * cap
    owned = means.shape[1]
    high = owned // LANES
    tiles_here, length = lists.shape[1:]
    pix = image_cot.shape[3]
    vmem = pl.BlockSpec(memory_space=pltpu.VMEM)
    smem = pl.BlockSpec(memory_space=pltpu.SMEM)
    hbm = pl.BlockSpec(memory_space=pl.ANY)
    small = (means, log_scales, quat_w, quat_v, opacity)
    few = sum(part.shape[0] for part in small)
    rows = few + sh_coeffs.shape[0]
    image_shape = jax.ShapeDtypeStruct(image_cot.shape, F32)
    rendered, back, asked, harm = pl.pallas_call(
        functools.partial(render_kernel, (n_img, n_tile, cap, tiles_here, length, pix)),
        out_shape=(
            image_shape,
            jax.ShapeDtypeStruct((devices, cap * NBACK), F32),
            jax.ShapeDtypeStruct((2, n_slots), jnp.int32),
            jax.ShapeDtypeStruct((n_img, 16, LANES), F32),
        ),
        in_specs=[hbm] * 6 + [smem, hbm, hbm, smem, hbm],
        out_specs=(vmem,) * 4,
        scratch_shapes=[
            *(pltpu.VMEM(part.shape, F32) for part in (*small, sh_coeffs)),
            pltpu.VMEM((tiles_here, length), jnp.int32),
            pltpu.VMEM(image_cot.shape, F32),
            pltpu.SemaphoreType.DMA((8,)),
            pltpu.VMEM((devices, 1, cap), jnp.int32),
            pltpu.VMEM((devices, 1, cap * NSENT), F32),
            pltpu.VMEM((devices, 1, cap * NSENT), F32),
            pltpu.VMEM((devices, 1, cap * NBACK), F32),
            pltpu.VMEM((devices, 1, cap * NBACK), F32),
            pltpu.VMEM((rows * high + high, LANES), F32),
            pltpu.VMEM((high * NSENT + NSENT, LANES), F32),
            pltpu.VMEM((n_img, high * NSENT, 3 * LANES), BF16),
            pltpu.VMEM((n_slots + cap, LANES), F32),
            pltpu.VMEM((n_slots // LANES * NSENT + NSENT, LANES), F32),
            pltpu.VMEM((tiles_here, LANES, length), BF16),
            pltpu.VMEM((length // LANES, 16 * tiles_here + 16, LANES), F32),
            pltpu.VMEM((length // LANES, 32 * tiles_here + 32, LANES), F32),
            pltpu.VMEM((length // LANES, 32 * tiles_here + 32, LANES), F32),
            pltpu.VMEM((tiles_here, 32, pix), BF16),
            pltpu.VMEM((tiles_here, pix, 32), BF16),
            pltpu.VMEM((tiles_here, length), F32),
            pltpu.VMEM((length // LANES, 9 * tiles_here, LANES), F32),
            pltpu.VMEM((length // LANES, 4 * tiles_here, LANES), F32),
            pltpu.VMEM((length // LANES, 16 * tiles_here + 16, LANES), F32),
            pltpu.VMEM((length // LANES, 8 * tiles_here + 4, LANES), F32),
            pltpu.VMEM((pix, 8 * tiles_here), F32),
            pltpu.VMEM((n_img, 3, 16, LANES), F32),
            pltpu.SemaphoreType.DMA((3,)),
            pltpu.SemaphoreType.DMA((3,)),
            pltpu.SemaphoreType.DMA((3,)),
        ],
        compiler_params=pltpu.CompilerParams(
            collective_id=0, has_side_effects=True, vmem_limit_bytes=60 * 1024 * 1024
        ),
    )(
        *small,
        sh_coeffs,
        cameras,
        requests.reshape(devices, 1, cap),
        lists[0],
        counts,
        image_cot,
    )
    return pl.pallas_call(
        functools.partial(owner_kernel, (n_img, n_tile, cap)),
        out_shape=(
            image_shape,
            jax.ShapeDtypeStruct((rows, owned), F32),
            jax.ShapeDtypeStruct(cameras.shape, F32),
        ),
        in_specs=[vmem] * 5 + [smem] + [vmem] * 4,
        out_specs=(vmem,) * 3,
        scratch_shapes=[
            pltpu.VMEM((few * high + high, LANES), F32),
            pltpu.VMEM((n_slots + cap, LANES), F32),
            pltpu.VMEM((rows * high + high, LANES), F32),
        ],
        compiler_params=pltpu.CompilerParams(vmem_limit_bytes=60 * 1024 * 1024),
    )(*small, cameras, back, asked, harm, rendered)


def solution(mesh):
    owners = P(None, ("img", "tile"))
    images = P("img", None, "tile", None)
    return jax.shard_map(
        local,
        mesh=mesh,
        in_specs=(owners,) * 6
        + (P(), P("img", "tile", None, None, None), P("img", "tile", None), P("img", "tile"), images),
        out_specs=(images, owners, P()),
        check_vma=False,
    )
```

```python
import functools
import math

import jax
import jax.numpy as jnp
from jax import lax
from jax.experimental import pallas as pl
from jax.experimental.pallas import tpu as pltpu
from jax.sharding import PartitionSpec as P

TILE_SIDE = 16
TW = 16
NFEAT = 9
NSENT = 24
NBACK = 16
LANES = 128
F32 = jnp.float32
BF16 = jnp.bfloat16
MESH = pl.DeviceIdType.MESH

sh_first = 0.28209479177387814
sh_second = 0.4886025119029199
sh_third = (
    1.0925484305920792,
    -1.0925484305920792,
    0.31539156525252005,
    -1.0925484305920792,
    0.5462742152960396,
)
sh_fourth = (
    -0.5900435899266435,
    2.890611442640554,
    -0.4570457994644658,
    0.3731763325901154,
    -0.4570457994644658,
    1.445305721320277,
    -0.5900435899266435,
)
dilation = 0.3


def harmonics(x, y, z):
    xx, yy, zz = x * x, y * y, z * z
    zero = jnp.zeros_like(x)
    a, b = sh_third, sh_fourth
    c = sh_second
    values = [
        zero + sh_first,
        -c * y,
        c * z,
        -c * x,
        a[0] * x * y,
        a[1] * y * z,
        a[2] * (2.0 * zz - xx - yy),
        a[3] * x * z,
        a[4] * (xx - yy),
        b[0] * y * (3.0 * xx - yy),
        b[1] * x * y * z,
        b[2] * y * (4.0 * zz - xx - yy),
        b[3] * z * (2.0 * zz - 3.0 * xx - 3.0 * yy),
        b[4] * x * (4.0 * zz - xx - yy),
        b[5] * z * (xx - yy),
        b[6] * x * (xx - 3.0 * yy),
    ]
    by_x = [
        zero,
        zero,
        zero,
        zero - c,
        a[0] * y,
        zero,
        -2.0 * a[2] * x,
        a[3] * z,
        2.0 * a[4] * x,
        6.0 * b[0] * x * y,
        b[1] * y * z,
        -2.0 * b[2] * x * y,
        -6.0 * b[3] * x * z,
        b[4] * (4.0 * zz - 3.0 * xx - yy),
        2.0 * b[5] * x * z,
        b[6] * (3.0 * xx - 3.0 * yy),
    ]
    by_y = [
        zero,
        zero - c,
        zero,
        zero,
        a[0] * x,
        a[1] * z,
        -2.0 * a[2] * y,
        zero,
        -2.0 * a[4] * y,
        b[0] * (3.0 * xx - 3.0 * yy),
        b[1] * x * z,
        b[2] * (4.0 * zz - xx - 3.0 * yy),
        -6.0 * b[3] * y * z,
        -2.0 * b[4] * x * y,
        -2.0 * b[5] * y * z,
        -6.0 * b[6] * x * y,
    ]
    by_z = [
        zero,
        zero,
        zero + c,
        zero,
        zero,
        a[1] * y,
        4.0 * a[2] * z,
        a[3] * x,
        zero,
        zero,
        b[1] * x * y,
        8.0 * b[2] * y * z,
        b[3] * (6.0 * zz - 3.0 * xx - 3.0 * yy),
        8.0 * b[4] * x * z,
        b[5] * (xx - yy),
        zero,
    ]
    return values, by_x, by_y, by_z


def split(value, parts):
    terms, rest = [], value
    for at in range(parts):
        term = rest.astype(BF16).astype(F32)
        terms.append(term)
        if at < parts - 1:
            rest = rest - term
    return terms


def dot(a, b):
    return jnp.dot(a, b, preferred_element_type=F32)


def dot_nt(a, b):
    return lax.dot_general(a, b, (((1,), (1,)), ((), ())), preferred_element_type=F32)


def conic(cam, sigma):
    a0, a1 = cam[0:3], cam[3:6]

    def times(a):
        return (
            a[0] * sigma[0] + a[1] * sigma[1] + a[2] * sigma[2],
            a[0] * sigma[1] + a[1] * sigma[3] + a[2] * sigma[4],
            a[0] * sigma[2] + a[1] * sigma[4] + a[2] * sigma[5],
        )

    v0, v1 = times(a0), times(a1)
    s00 = a0[0] * v0[0] + a0[1] * v0[1] + a0[2] * v0[2] + dilation
    s01 = a1[0] * v0[0] + a1[1] * v0[1] + a1[2] * v0[2]
    s11 = a1[0] * v1[0] + a1[1] * v1[1] + a1[2] * v1[2] + dilation
    inverse = 1.0 / (s00 * s11 - s01 * s01)
    return v0, v1, (s11 * inverse, -s01 * inverse, s00 * inverse)


def cov_grad(con, grad):
    ca, cb, cc = con
    ga, gb, gc = grad[0], 0.5 * grad[1], grad[2]
    p00, p01 = ca * ga + cb * gb, ca * gb + cb * gc
    p10, p11 = cb * ga + cc * gb, cb * gb + cc * gc
    return (
        -(p00 * ca + p01 * cb),
        -(p00 * cb + p01 * cc),
        -(p10 * cb + p11 * cc),
    )


def rotation_of(quat):
    w, x, y, z = quat
    return (
        (1.0 - 2.0 * (y * y + z * z), 2.0 * (x * y - w * z), 2.0 * (x * z + w * y)),
        (2.0 * (x * y + w * z), 1.0 - 2.0 * (x * x + z * z), 2.0 * (y * z - w * x)),
        (2.0 * (x * z - w * y), 2.0 * (y * z + w * x), 1.0 - 2.0 * (x * x + y * y)),
    )


def load_dense(refs, dense):
    at = 0
    for ref in refs:
        rows, owned = ref.shape
        high = owned // LANES
        for h in range(high):
            part = ref[:, h * LANES : (h + 1) * LANES]
            if rows == 1:
                dense[at * high + h : at * high + h + 1, :] = part
            else:
                dense[pl.ds(at * high + h, rows, stride=high), :] = part
        at += rows


def geometry(row):
    raw = tuple(row(6 + a) for a in range(4))
    inverse = 1.0 / jnp.sqrt(
        raw[0] * raw[0] + raw[1] * raw[1] + raw[2] * raw[2] + raw[3] * raw[3]
    )
    quat = tuple(part * inverse for part in raw)
    rot = rotation_of(quat)
    squares = tuple(jnp.exp(2.0 * row(3 + a)) for a in range(3))

    def entry(a, b):
        return (
            rot[a][0] * rot[b][0] * squares[0]
            + rot[a][1] * rot[b][1] * squares[1]
            + rot[a][2] * rot[b][2] * squares[2]
        )

    sigma = tuple(entry(a, b) for a, b in ((0, 0), (0, 1), (0, 2), (1, 1), (1, 2), (2, 2)))
    return quat, inverse, rot, squares, sigma


def mask_of(index, rows):
    return lax.broadcasted_iota(jnp.int32, (rows, index.shape[1]), 0) == index


def as_bf16(mask):
    return mask.astype(F32).astype(BF16)


def two(value):
    hi = value.astype(BF16)
    return hi, (value - hi.astype(F32)).astype(BF16)


def scatter_rows(ref, start, stride, value):
    for h in range(ref.shape[0]):
        ref[h, pl.ds(start, value.shape[0], stride=stride), :] = value[
            :, h * LANES : (h + 1) * LANES
        ]


def take_rows(ref, rows):
    return jnp.concatenate([ref[h, rows, :] for h in range(ref.shape[0])], axis=1)


def render_kernel(
    sizes,
    means_hbm,
    log_scales_hbm,
    quat_w_hbm,
    quat_v_hbm,
    opacity_hbm,
    sh_hbm,
    cams,
    requests,
    lists_hbm,
    counts,
    cot_hbm,
    rendered,
    back_out,
    ask_out,
    harm_out,
    means,
    log_scales,
    quat_w,
    quat_v,
    opacity,
    sh,
    lists,
    cot,
    in_sem,
    ask_recv,
    feat_send,
    feat_recv,
    grad_send,
    grad_recv,
    dense,
    project,
    feats,
    slots,
    by_slot,
    low,
    gots,
    coefs,
    colours,
    cots,
    cots_t,
    live_op,
    moments,
    tints,
    grads,
    tinted,
    pictures,
    harm,
    send_sem,
    recv_sem,
    own_sem,
):
    n_img, n_tile, cap, tiles_here, length, pix = sizes
    owned = means.shape[1]
    high = owned // LANES
    devices = n_img * n_tile
    n_slots = devices * cap
    groups = n_slots // LANES
    per_img = n_tile * cap
    my_tile = lax.axis_index("tile")
    my_img = lax.axis_index("img")
    me = my_img * n_tile + my_tile

    def peer(k):
        other = lax.rem(me + k, devices)
        return other, (other // n_tile, lax.rem(other, n_tile))

    loads = [
        pltpu.make_async_copy(source, target, in_sem.at[at])
        for at, (source, target) in enumerate(
            (
                (means_hbm, means),
                (log_scales_hbm, log_scales),
                (quat_w_hbm, quat_w),
                (quat_v_hbm, quat_v),
                (opacity_hbm, opacity),
                (sh_hbm, sh),
                (lists_hbm, lists),
                (cot_hbm, cot),
            )
        )
    ]
    for load in loads:
        load.start()

    barrier = pltpu.get_barrier_semaphore()

    @pl.loop(1, devices, unroll=devices <= 32)
    def _(k):
        pl.semaphore_signal(barrier, inc=1, device_id=peer(k)[1], device_id_type=MESH)

    def exchange(at, source, target):
        mine = pltpu.make_async_copy(source.at[me], target.at[me], own_sem.at[at])
        mine.start()

        @pl.loop(1, devices, unroll=devices <= 32)
        def _(k):
            other, where = peer(k)
            pltpu.make_async_remote_copy(
                src_ref=source.at[other],
                dst_ref=target.at[me],
                send_sem=send_sem.at[at],
                recv_sem=recv_sem.at[at],
                device_id=where,
                device_id_type=MESH,
            ).start()

        return mine

    def arrive(at, target, mine):
        mine.wait()
        others = target.at[pl.ds(0, devices - 1)]
        pltpu.make_async_copy(others, others, recv_sem.at[at]).wait()

    def sent(at, source):
        others = source.at[pl.ds(0, devices - 1)]
        pltpu.make_async_copy(others, others, send_sem.at[at]).wait()

    cam = [[cams[i, c] for c in range(10)] for i in range(n_img)]
    img_rows = -(-n_img // 8) * 8
    img_row = lax.broadcasted_iota(jnp.int32, (img_rows, LANES), 0)
    polar = jnp.zeros((img_rows, LANES), F32)
    azimuth = jnp.zeros((img_rows, LANES), F32)
    for i in range(n_img):
        polar = jnp.where(img_row == i, cam[i][8], polar)
        azimuth = jnp.where(img_row == i, cam[i][9], azimuth)
    sp, cp = jnp.sin(polar), jnp.cos(polar)
    sz, cz = jnp.sin(azimuth), jnp.cos(azimuth)
    values, by_x, by_y, by_z = harmonics(sp * cz, sp * sz, cp)
    for m in range(16):
        by_polar = by_x[m] * (cp * cz) + by_y[m] * (cp * sz) - by_z[m] * sp
        by_azimuth = by_y[m] * (sp * cz) - by_x[m] * (sp * sz)
        for i in range(n_img):
            harm[i, 0, m : m + 1, :] = values[m][i : i + 1]
            harm[i, 1, m : m + 1, :] = by_polar[i : i + 1]
            harm[i, 2, m : m + 1, :] = by_azimuth[i : i + 1]
    for i in range(n_img):
        harm_out[i] = harm[i, 0]
    for load in loads[:6]:
        load.wait()
    load_dense((means, log_scales, quat_w, quat_v, opacity, sh), dense)

    pl.semaphore_wait(barrier, devices - 1)
    asking = exchange(0, requests, ask_recv)

    def row(at):
        return dense[at * high : (at + 1) * high, :]

    _, _, _, _, sigma = geometry(row)
    mean = tuple(row(a) for a in range(3))
    base = 1.0 / (1.0 + jnp.exp(-row(10)))
    for i in range(n_img):
        c = cam[i]
        _, _, con = conic(c, sigma)
        rows = [
            c[0] * mean[0] + c[1] * mean[1] + c[2] * mean[2] + c[6],
            c[3] * mean[0] + c[4] * mean[1] + c[5] * mean[2] + c[7],
            con[0],
            con[1],
            con[2],
            base,
        ]
        sums = [[None] * 3 for _ in range(3)]
        for k in range(3):
            for m in range(16):
                coeff = row(11 + 16 * k + m)
                for d in range(3):
                    term = coeff * harm[i, d, m : m + 1, :]
                    sums[d][k] = term if m == 0 else sums[d][k] + term
        rows += [total + 0.5 for total in sums[0]] + list(mean) + list(sigma) + sums[1] + sums[2]
        for at, value in enumerate(rows):
            project[pl.ds(at, high, stride=NSENT), :] = value
        for at, term in enumerate(split(project[0 : high * NSENT, :], 3)):
            feats[i, :, at * LANES : (at + 1) * LANES] = term.astype(BF16)

    arrive(0, ask_recv, asking)
    asks = ask_recv[...].reshape(devices, cap)
    halves = jnp.concatenate(
        [(asks // LANES).astype(F32), jnp.bitwise_and(asks, LANES - 1).astype(F32)], axis=0
    ).astype(BF16)
    repeat = as_bf16(
        lax.rem(lax.broadcasted_iota(jnp.int32, (cap, n_slots), 1), cap)
        == lax.broadcasted_iota(jnp.int32, (cap, n_slots), 0)
    )
    wide = dot(halves, repeat)
    here = (
        lax.broadcasted_iota(jnp.int32, (devices, n_slots), 1) // cap
        == lax.broadcasted_iota(jnp.int32, (devices, n_slots), 0)
    )
    ask_hi, ask_lo = (
        jnp.sum(
            jnp.where(here, wide[at * devices : (at + 1) * devices], 0.0), axis=0, keepdims=True
        ).astype(jnp.int32)
        for at in range(2)
    )
    ask_out[0:1, :] = ask_hi
    ask_out[1:2, :] = ask_lo
    for i in range(n_img):
        lanes = slice(i * per_img, (i + 1) * per_img)
        mask = as_bf16(mask_of(ask_lo[:, lanes], LANES))
        got = dot(feats[i], jnp.concatenate([mask] * 3, axis=0))
        pick = mask_of(ask_hi[:, lanes], high).astype(F32)
        total = got[0:NSENT] * pick[0:1]
        for h in range(1, high):
            total = total + got[h * NSENT : (h + 1) * NSENT] * pick[h : h + 1]
        slots[lanes, 0:NSENT] = jnp.transpose(total)
        feat_send[i * n_tile : (i + 1) * n_tile] = jnp.concatenate(
            [
                slots[pl.ds(i * per_img + c, n_tile, stride=cap), 0:NSENT]
                for c in range(cap)
            ],
            axis=1,
        ).reshape(n_tile, 1, cap * NSENT)

        @pl.loop(0, n_tile, unroll=n_tile <= 32)
        def _(k):
            place = lax.rem(my_tile + k, n_tile)
            other = i * n_tile + place

            @pl.when(other != me)
            def _():
                pltpu.make_async_remote_copy(
                    src_ref=feat_send.at[other],
                    dst_ref=feat_recv.at[me],
                    send_sem=send_sem.at[1],
                    recv_sem=recv_sem.at[1],
                    device_id=(i, place),
                    device_id_type=MESH,
                ).start()

    sending = pltpu.make_async_copy(feat_send.at[me], feat_recv.at[me], own_sem.at[1])
    sending.start()
    sent(0, requests)

    for load in loads[6:]:
        load.wait()
    coefs[...] = jnp.zeros_like(coefs)
    colours[...] = jnp.zeros_like(colours)
    for j in range(tiles_here):
        low[j] = as_bf16(mask_of(jnp.bitwise_and(lists[j : j + 1, :], LANES - 1), LANES))
        cot3 = jnp.concatenate([cot[0, k, j : j + 1, :] for k in range(3)], axis=0)
        c1, c2, c3 = split(cot3, 3)
        stack = jnp.concatenate([c1, c1, c2, c2, c1, c3, jnp.zeros((14, pix), F32)], axis=0)
        cots[j] = stack.astype(BF16)
        cots_t[j] = jnp.transpose(stack).astype(BF16)

    def basis_of(pixel, which):
        half = 0.5 * TILE_SIDE - 0.5
        x = lax.rem(pixel, TILE_SIDE).astype(F32) - half
        y = (pixel // TILE_SIDE).astype(F32) - half
        out = jnp.where(which == 0, 1.0, 0.0)
        for at, term in enumerate((x, y, x * x, x * y, y * y)):
            out = jnp.where(which == at + 1, term, out)
        return out.astype(BF16)

    basis_pe = basis_of(
        lax.broadcasted_iota(jnp.int32, (pix, 32), 0),
        lax.rem(lax.broadcasted_iota(jnp.int32, (pix, 32), 1), 8),
    )
    basis_ep = basis_of(
        lax.broadcasted_iota(jnp.int32, (16, pix), 1), lax.broadcasted_iota(jnp.int32, (16, pix), 0)
    )
    first = lax.broadcasted_iota(jnp.int32, (length, length), 0)
    second = lax.broadcasted_iota(jnp.int32, (length, length), 1)
    before = as_bf16(first < second)
    after = as_bf16(first > second)
    height = TILE_SIDE * tiles_here * n_tile / TW

    tinted[...] = jnp.zeros_like(tinted)
    pictures[...] = jnp.zeros_like(pictures)
    arrive(1, feat_recv, sending)
    packed = feat_recv[...].reshape(devices, cap * NSENT)
    for c in range(cap):
        slots[pl.ds(c, devices, stride=cap), 0:NSENT] = packed[:, c * NSENT : (c + 1) * NSENT]
    heads = []
    for h in range(groups):
        turned = jnp.transpose(slots[h * LANES : (h + 1) * LANES, :])[0:NSENT]
        by_slot[h * NSENT : (h + 1) * NSENT, :] = turned
        heads.append(turned[0:16])
    heads = jnp.concatenate(
        [term.astype(BF16) for term in split(jnp.concatenate(heads, axis=0), 3)], axis=1
    )

    for j in range(tiles_here):
        got = dot(heads, jnp.concatenate([low[j]] * 3, axis=0))
        group = lists[j : j + 1, :] // LANES
        total = jnp.where(group == 0, got[0:16], 0.0)
        for h in range(1, groups):
            total = total + jnp.where(group == h, got[h * 16 : (h + 1) * 16], 0.0)
        scatter_rows(gots, j, tiles_here, total)

    def feature(at):
        return take_rows(gots, slice(at * tiles_here, (at + 1) * tiles_here))

    tile_row = lax.broadcasted_iota(jnp.int32, (tiles_here, length), 0)
    number = my_tile * tiles_here + tile_row
    lx = feature(0) - (
        (lax.rem(number, TW) * TILE_SIDE).astype(F32) + 0.5 * TILE_SIDE * (1 - TW)
    )
    ly = feature(1) - ((number // TW * TILE_SIDE).astype(F32) + 0.5 * TILE_SIDE - 0.5 * height)
    ca, cb, cc, op = (feature(at) for at in range(2, 6))
    ux = ca * lx + cb * ly
    uy = cc * ly + cb * lx
    live = jnp.zeros((tiles_here, length), jnp.int32)
    for j in range(tiles_here):
        live = jnp.where(tile_row == j, counts[0, j], live)
    lane = lax.broadcasted_iota(jnp.int32, (tiles_here, length), 1)
    live_op[...] = jnp.where(lane < live, op, 0.0)
    for at, value in enumerate((-0.5 * (ux * lx + uy * ly), ux, uy, -0.5 * ca, -cb, -0.5 * cc)):
        for term_at, term in enumerate(split(value, 3)):
            scatter_rows(coefs, 8 * term_at + at, 32, term)
    for k in range(3):
        terms = split(feature(6 + k), 3)
        for at, term_at in enumerate((0, 1, 0, 1, 2, 0)):
            scatter_rows(colours, 3 * at + k, 32, terms[term_at])
        for at in range(2):
            scatter_rows(tinted, at * 4 * tiles_here + k, 4, terms[at])
    painted = jnp.transpose(take_rows(tinted, slice(0, 8 * tiles_here)))
    painted_lane = lax.rem(
        lax.broadcasted_iota(jnp.int32, (length, 8 * tiles_here), 1), 4 * tiles_here
    )

    chunk = 64 if pix % 64 == 0 else pix
    before2 = jnp.concatenate([before, before], axis=0)
    after2 = jnp.concatenate([after, after], axis=0)
    basis2 = jnp.concatenate([basis_ep, basis_ep], axis=1)

    def chunks(function, *arrays):
        parts = [
            function(*(array[at : at + chunk] for array in arrays))
            for at in range(0, pix, chunk)
        ]
        return tuple(jnp.concatenate(part, axis=0) for part in zip(*parts))

    def render(tiles):
        rows = [pl.ds(pl.multiple_of(j * 32, 32), 32) for j in tiles]
        power = [dot(basis_pe, take_rows(coefs, r).astype(BF16)) for r in rows]
        colour = [take_rows(colours, r).astype(BF16) for r in rows]
        opacities = [live_op[pl.ds(j, 1), :] for j in tiles]
        alpha, summed, weight, pair, pull, pulled, later = ([] for _ in range(7))
        for at, j in enumerate(tiles):

            def first_part(p, op_row=opacities[at]):
                a = op_row * jnp.exp(p)
                hi, lo = two(jnp.log(1.0 - a))
                return a, jnp.concatenate([hi, lo], axis=1)

            a, logs = chunks(first_part, power[at])
            alpha.append(a)
            summed.append(dot(logs, before2))
            pull.append(dot(cots_t[j], colour[at]))
        for at, j in enumerate(tiles):

            def second_part(a, total, force):
                w = a * jnp.exp(total)
                p = force * w
                return (*two(w), p, jnp.concatenate(two(p), axis=1))

            hi, lo, p, wide = chunks(second_part, alpha[at], summed[at], pull[at])
            pulled.append(p)
            later.append(dot(wide, after2))
            weight.append(jnp.concatenate([hi, lo], axis=0))
            pair.append(jnp.concatenate([hi, lo], axis=1))
        for at, j in enumerate(tiles):

            def third_part(a, p, l):
                keep = 1.0 - a
                rough = pl.reciprocal(keep, approx=True)
                return two(p - l * (a * (rough * (2.0 - keep * rough))))

            hi, lo = chunks(third_part, alpha[at], pulled[at], later[at])
            moment = dot(basis2, jnp.concatenate([hi, lo], axis=0))
            scatter_rows(moments, j, tiles_here, moment[0:8])
        picture = 0.0
        for at, j in enumerate(tiles):
            cot2 = jnp.concatenate([cots[j], cots[j]], axis=1)
            tint = dot(cot2, weight[at])
            scatter_rows(tints, j, tiles_here, tint[0:3] + tint[6:9] + tint[15:18])
            brush = jnp.where(painted_lane // 4 == j, painted, 0.0).astype(BF16)
            picture = picture + dot(pair[at], jnp.concatenate([brush, brush], axis=0))
        pictures[...] += picture

    step = 2 if tiles_here % 2 == 0 else 1

    @pl.loop(0, tiles_here // step)
    def _(at):
        render([at * step + more for more in range(step)])

    picture = jnp.transpose(pictures[...])
    picture = picture[0 : 4 * tiles_here] + picture[4 * tiles_here : 8 * tiles_here]
    for j in range(tiles_here):
        for k in range(3):
            rendered[0, k, j : j + 1, :] = picture[4 * j + k : 4 * j + k + 1]

    def moment(at):
        return take_rows(moments, slice(at * tiles_here, (at + 1) * tiles_here))

    m0, mx, my = moment(0), moment(1), moment(2)
    nx, ny = mx - lx * m0, my - ly * m0
    nxx = moment(3) - 2.0 * lx * mx + lx * lx * m0
    nxy = moment(4) - lx * my - ly * mx + lx * ly * m0
    nyy = moment(5) - 2.0 * ly * my + ly * ly * m0
    grads[...] = jnp.zeros_like(grads)
    for at, value in enumerate(
        (ca * nx + cb * ny, cc * ny + cb * nx, -0.5 * nxx, -nxy, -0.5 * nyy, m0 / op)
    ):
        scatter_rows(grads, at, 16, value)
    for k in range(3):
        scatter_rows(
            grads, 6 + k, 16, take_rows(tints, slice(k * tiles_here, (k + 1) * tiles_here))
        )
    spreads = []
    for j in range(tiles_here):
        hi, lo = split(take_rows(grads, slice(16 * j, 16 * (j + 1))), 2)
        group = lists[j : j + 1, :] // LANES
        spread = [
            jnp.where(group == h, term, 0.0) for h in range(groups) for term in (hi, lo)
        ]
        spreads.append(jnp.concatenate(spread, axis=0).astype(BF16))
    back = dot_nt(
        jnp.concatenate(spreads, axis=1),
        jnp.concatenate([low[j] for j in range(tiles_here)], axis=1),
    )
    slot_rows = [back[32 * h : 32 * h + 16] + back[32 * h + 16 : 32 * h + 32] for h in range(groups)]

    g = [
        jnp.concatenate([rows[at : at + 1] for rows in slot_rows], axis=0) for at in range(NFEAT)
    ]
    f = [by_slot[pl.ds(at, groups, stride=NSENT), :] for at in range(NSENT)]
    c = [cams[my_img, at] for at in range(10)]
    v0, v1, _ = conic(c, f[12:18])
    h = cov_grad((f[2], f[3], f[4]), (g[2], g[3], g[4]))
    shares = [g[0] * f[9 + a] + 2.0 * (h[0] * v0[a] + h[1] * v1[a]) for a in range(3)]
    shares += [g[1] * f[9 + a] + 2.0 * (h[2] * v1[a] + h[1] * v0[a]) for a in range(3)]
    shares += [g[0], g[1]]
    shares += [sum(g[6 + k] * f[18 + 3 * d + k] for k in range(3)) for d in range(2)]
    slot_lane = lax.rem(lax.broadcasted_iota(jnp.int32, (16, LANES), 1), cap)
    is_camera = lax.broadcasted_iota(jnp.int32, (16, LANES), 0) == NFEAT
    camera_row = jnp.zeros((1, LANES), F32)
    for at, share in enumerate(shares):
        total = jnp.sum(jnp.sum(share, axis=0, keepdims=True), axis=1, keepdims=True)
        camera_row = jnp.where(slot_lane[0:1] == at, total, camera_row)
    for at, rows in enumerate(slot_rows):
        slots[at * LANES : (at + 1) * LANES, 0:NBACK] = jnp.transpose(
            jnp.where(is_camera, camera_row, rows)
        )
    grad_send[...] = jnp.concatenate(
        [slots[pl.ds(c, devices, stride=cap), 0:NBACK] for c in range(cap)], axis=1
    ).reshape(devices, 1, cap * NBACK)
    returning = exchange(2, grad_send, grad_recv)
    sent(1, feat_send)
    arrive(2, grad_recv, returning)
    back_out[...] = grad_recv[...].reshape(devices, cap * NBACK)
    sent(2, grad_send)


def owner_kernel(
    sizes,
    means,
    log_scales,
    quat_w,
    quat_v,
    opacity,
    cams,
    back,
    asked,
    harm,
    rendered_in,
    rendered,
    param_grad,
    camera_grad,
    dense,
    slots,
    result,
):
    n_img, n_tile, cap = sizes
    owned = means.shape[1]
    high = owned // LANES
    devices = n_img * n_tile
    per_img = n_tile * cap
    rendered[...] = rendered_in[...]
    load_dense((means, log_scales, quat_w, quat_v, opacity), dense)

    def row(at):
        return dense[at * high : (at + 1) * high, :]

    quat, inverse, rot, squares, sigma = geometry(row)
    base = 1.0 / (1.0 + jnp.exp(-row(10)))
    packed = back[...]
    for c in range(cap):
        slots[pl.ds(c, devices, stride=cap), 0:NBACK] = packed[:, c * NBACK : (c + 1) * NBACK]
    g_mean = [0.0, 0.0, 0.0]
    g_base = 0.0
    g_sigma = [[0.0] * 3 for _ in range(3)]
    g_colour = []
    for i in range(n_img):
        mine = jnp.concatenate(
            [
                jnp.transpose(slots[at : at + LANES, :])[0:NBACK]
                for at in range(i * per_img, (i + 1) * per_img, LANES)
            ],
            axis=1,
        )
        fold = mine[NFEAT : NFEAT + 1, 0:LANES]
        for at in range(LANES, per_img, LANES):
            fold = fold + mine[NFEAT : NFEAT + 1, at : at + LANES]
        shift = LANES // 2
        while shift >= cap:
            fold = fold + pltpu.roll(fold, shift, 1)
            shift //= 2
        camera_grad[i : i + 1, :] = fold[:, 0:10]
        lanes = slice(i * per_img, (i + 1) * per_img)
        pick = mask_of(asked[0:1, lanes], high)
        low = as_bf16(mask_of(asked[1:2, lanes], LANES))
        spread = jnp.concatenate(
            [
                jnp.concatenate(
                    [jnp.where(pick, term[at : at + 1], 0.0) for at in range(NFEAT)], axis=0
                ).astype(BF16)
                for term in split(mine, 2)
            ],
            axis=1,
        )
        full = dot_nt(spread, jnp.concatenate([low] * 2, axis=1))
        g = [full[at * high : (at + 1) * high] for at in range(NFEAT)]
        c = [cams[i, at] for at in range(8)]
        _, _, con = conic(c, sigma)
        h = cov_grad(con, (g[2], g[3], g[4]))
        for a in range(3):
            g_mean[a] = g_mean[a] + c[a] * g[0] + c[3 + a] * g[1]
            for b in range(a, 3):
                g_sigma[a][b] = (
                    g_sigma[a][b]
                    + (c[a] * c[b]) * h[0]
                    + (c[a] * c[3 + b] + c[3 + a] * c[b]) * h[1]
                    + (c[3 + a] * c[3 + b]) * h[2]
                )
        g_base = g_base + g[5]
        g_colour.append(g[6:9])

    def put(at, value):
        result[at * high : (at + 1) * high, :] = value

    for k in range(3):
        for m in range(16):
            put(
                11 + 16 * k + m,
                sum(harm[i, m : m + 1, :] * g_colour[i][k] for i in range(n_img)),
            )
    for a in range(3):
        put(a, g_mean[a])
        for b in range(a):
            g_sigma[a][b] = g_sigma[b][a]
    r = [[None] * 3 for _ in range(3)]
    for b in range(3):
        pull = [
            g_sigma[a][0] * rot[0][b] + g_sigma[a][1] * rot[1][b] + g_sigma[a][2] * rot[2][b]
            for a in range(3)
        ]
        twice = 2.0 * squares[b]
        for a in range(3):
            r[a][b] = twice * pull[a]
        put(3 + b, r[0][b] * rot[0][b] + r[1][b] * rot[1][b] + r[2][b] * rot[2][b])
    w, x, y, z = quat
    g_quat = (
        z * (r[1][0] - r[0][1]) + y * (r[0][2] - r[2][0]) + x * (r[2][1] - r[1][2]),
        y * (r[0][1] + r[1][0])
        + z * (r[0][2] + r[2][0])
        + w * (r[2][1] - r[1][2])
        - 2.0 * x * (r[1][1] + r[2][2]),
        x * (r[0][1] + r[1][0])
        + z * (r[1][2] + r[2][1])
        + w * (r[0][2] - r[2][0])
        - 2.0 * y * (r[0][0] + r[2][2]),
        x * (r[0][2] + r[2][0])
        + y * (r[1][2] + r[2][1])
        + w * (r[1][0] - r[0][1])
        - 2.0 * z * (r[0][0] + r[1][1]),
    )
    along = sum(quat[a] * g_quat[a] for a in range(4))
    for a in range(4):
        put(6 + a, 2.0 * (g_quat[a] - quat[a] * along) * inverse)
    put(10, g_base * base * (1.0 - base))
    rows = param_grad.shape[0]
    for h in range(high):
        param_grad[:, h * LANES : (h + 1) * LANES] = result[pl.ds(h, rows, stride=high), :]


def local(
    means,
    log_scales,
    quat_w,
    quat_v,
    opacity,
    sh_coeffs,
    cameras,
    requests,
    lists,
    counts,
    image_cot,
):
    n_img, n_tile, cap = requests.shape[2:]
    devices = n_img * n_tile
    n_slots = devices * cap
    owned = means.shape[1]
    high = owned // LANES
    tiles_here, length = lists.shape[1:]
    pix = image_cot.shape[3]
    vmem = pl.BlockSpec(memory_space=pltpu.VMEM)
    smem = pl.BlockSpec(memory_space=pltpu.SMEM)
    hbm = pl.BlockSpec(memory_space=pl.ANY)
    small = (means, log_scales, quat_w, quat_v, opacity)
    few = sum(part.shape[0] for part in small)
    rows = few + sh_coeffs.shape[0]
    image_shape = jax.ShapeDtypeStruct(image_cot.shape, F32)
    rendered, back, asked, harm = pl.pallas_call(
        functools.partial(render_kernel, (n_img, n_tile, cap, tiles_here, length, pix)),
        out_shape=(
            image_shape,
            jax.ShapeDtypeStruct((devices, cap * NBACK), F32),
            jax.ShapeDtypeStruct((2, n_slots), jnp.int32),
            jax.ShapeDtypeStruct((n_img, 16, LANES), F32),
        ),
        in_specs=[hbm] * 6 + [smem, hbm, hbm, smem, hbm],
        out_specs=(vmem,) * 4,
        scratch_shapes=[
            *(pltpu.VMEM(part.shape, F32) for part in (*small, sh_coeffs)),
            pltpu.VMEM((tiles_here, length), jnp.int32),
            pltpu.VMEM(image_cot.shape, F32),
            pltpu.SemaphoreType.DMA((8,)),
            pltpu.VMEM((devices, 1, cap), jnp.int32),
            pltpu.VMEM((devices, 1, cap * NSENT), F32),
            pltpu.VMEM((devices, 1, cap * NSENT), F32),
            pltpu.VMEM((devices, 1, cap * NBACK), F32),
            pltpu.VMEM((devices, 1, cap * NBACK), F32),
            pltpu.VMEM((rows * high + high, LANES), F32),
            pltpu.VMEM((high * NSENT + NSENT, LANES), F32),
            pltpu.VMEM((n_img, high * NSENT, 3 * LANES), BF16),
            pltpu.VMEM((n_slots + cap, LANES), F32),
            pltpu.VMEM((n_slots // LANES * NSENT + NSENT, LANES), F32),
            pltpu.VMEM((tiles_here, LANES, length), BF16),
            pltpu.VMEM((length // LANES, 16 * tiles_here + 16, LANES), F32),
            pltpu.VMEM((length // LANES, 32 * tiles_here + 32, LANES), F32),
            pltpu.VMEM((length // LANES, 32 * tiles_here + 32, LANES), F32),
            pltpu.VMEM((tiles_here, 32, pix), BF16),
            pltpu.VMEM((tiles_here, pix, 32), BF16),
            pltpu.VMEM((tiles_here, length), F32),
            pltpu.VMEM((length // LANES, 9 * tiles_here, LANES), F32),
            pltpu.VMEM((length // LANES, 4 * tiles_here, LANES), F32),
            pltpu.VMEM((length // LANES, 16 * tiles_here + 16, LANES), F32),
            pltpu.VMEM((length // LANES, 8 * tiles_here + 4, LANES), F32),
            pltpu.VMEM((pix, 8 * tiles_here), F32),
            pltpu.VMEM((n_img, 3, 16, LANES), F32),
            pltpu.SemaphoreType.DMA((3,)),
            pltpu.SemaphoreType.DMA((3,)),
            pltpu.SemaphoreType.DMA((3,)),
        ],
        compiler_params=pltpu.CompilerParams(
            collective_id=0, has_side_effects=True, vmem_limit_bytes=60 * 1024 * 1024
        ),
    )(
        *small,
        sh_coeffs,
        cameras,
        requests.reshape(devices, 1, cap),
        lists[0],
        counts,
        image_cot,
    )
    return pl.pallas_call(
        functools.partial(owner_kernel, (n_img, n_tile, cap)),
        out_shape=(
            image_shape,
            jax.ShapeDtypeStruct((rows, owned), F32),
            jax.ShapeDtypeStruct(cameras.shape, F32),
        ),
        in_specs=[vmem] * 5 + [smem] + [vmem] * 4,
        out_specs=(vmem,) * 3,
        scratch_shapes=[
            pltpu.VMEM((few * high + high, LANES), F32),
            pltpu.VMEM((n_slots + cap, LANES), F32),
            pltpu.VMEM((rows * high + high, LANES), F32),
        ],
        compiler_params=pltpu.CompilerParams(vmem_limit_bytes=60 * 1024 * 1024),
    )(*small, cameras, back, asked, harm, rendered)


def solution(mesh):
    owners = P(None, ("img", "tile"))
    images = P("img", None, "tile", None)
    return jax.shard_map(
        local,
        mesh=mesh,
        in_specs=(owners,) * 6
        + (P(), P("img", "tile", None, None, None), P("img", "tile", None), P("img", "tile"), images),
        out_specs=(images, owners, P()),
        check_vma=False,
    )
```

```python
import functools
import math

import jax
import jax.numpy as jnp
from jax import lax
from jax.experimental import pallas as pl
from jax.experimental.pallas import tpu as pltpu
from jax.sharding import PartitionSpec as P

TILE_SIDE = 16
TW = 16
NFEAT = 9
NSENT = 24
NBACK = 16
LANES = 128
F32 = jnp.float32
BF16 = jnp.bfloat16
MESH = pl.DeviceIdType.MESH

sh_first = 0.28209479177387814
sh_second = 0.4886025119029199
sh_third = (
    1.0925484305920792,
    -1.0925484305920792,
    0.31539156525252005,
    -1.0925484305920792,
    0.5462742152960396,
)
sh_fourth = (
    -0.5900435899266435,
    2.890611442640554,
    -0.4570457994644658,
    0.3731763325901154,
    -0.4570457994644658,
    1.445305721320277,
    -0.5900435899266435,
)
dilation = 0.3


def harmonics(x, y, z):
    xx, yy, zz = x * x, y * y, z * z
    zero = jnp.zeros_like(x)
    a, b = sh_third, sh_fourth
    c = sh_second
    values = [
        zero + sh_first,
        -c * y,
        c * z,
        -c * x,
        a[0] * x * y,
        a[1] * y * z,
        a[2] * (2.0 * zz - xx - yy),
        a[3] * x * z,
        a[4] * (xx - yy),
        b[0] * y * (3.0 * xx - yy),
        b[1] * x * y * z,
        b[2] * y * (4.0 * zz - xx - yy),
        b[3] * z * (2.0 * zz - 3.0 * xx - 3.0 * yy),
        b[4] * x * (4.0 * zz - xx - yy),
        b[5] * z * (xx - yy),
        b[6] * x * (xx - 3.0 * yy),
    ]
    by_x = [
        zero,
        zero,
        zero,
        zero - c,
        a[0] * y,
        zero,
        -2.0 * a[2] * x,
        a[3] * z,
        2.0 * a[4] * x,
        6.0 * b[0] * x * y,
        b[1] * y * z,
        -2.0 * b[2] * x * y,
        -6.0 * b[3] * x * z,
        b[4] * (4.0 * zz - 3.0 * xx - yy),
        2.0 * b[5] * x * z,
        b[6] * (3.0 * xx - 3.0 * yy),
    ]
    by_y = [
        zero,
        zero - c,
        zero,
        zero,
        a[0] * x,
        a[1] * z,
        -2.0 * a[2] * y,
        zero,
        -2.0 * a[4] * y,
        b[0] * (3.0 * xx - 3.0 * yy),
        b[1] * x * z,
        b[2] * (4.0 * zz - xx - 3.0 * yy),
        -6.0 * b[3] * y * z,
        -2.0 * b[4] * x * y,
        -2.0 * b[5] * y * z,
        -6.0 * b[6] * x * y,
    ]
    by_z = [
        zero,
        zero,
        zero + c,
        zero,
        zero,
        a[1] * y,
        4.0 * a[2] * z,
        a[3] * x,
        zero,
        zero,
        b[1] * x * y,
        8.0 * b[2] * y * z,
        b[3] * (6.0 * zz - 3.0 * xx - 3.0 * yy),
        8.0 * b[4] * x * z,
        b[5] * (xx - yy),
        zero,
    ]
    return values, by_x, by_y, by_z


def split(value, parts):
    terms, rest = [], value
    for at in range(parts):
        term = rest.astype(BF16).astype(F32)
        terms.append(term)
        if at < parts - 1:
            rest = rest - term
    return terms


def dot(a, b):
    return jnp.dot(a, b, preferred_element_type=F32)


def dot_nt(a, b):
    return lax.dot_general(a, b, (((1,), (1,)), ((), ())), preferred_element_type=F32)


def conic(cam, sigma):
    a0, a1 = cam[0:3], cam[3:6]

    def times(a):
        return (
            a[0] * sigma[0] + a[1] * sigma[1] + a[2] * sigma[2],
            a[0] * sigma[1] + a[1] * sigma[3] + a[2] * sigma[4],
            a[0] * sigma[2] + a[1] * sigma[4] + a[2] * sigma[5],
        )

    v0, v1 = times(a0), times(a1)
    s00 = a0[0] * v0[0] + a0[1] * v0[1] + a0[2] * v0[2] + dilation
    s01 = a1[0] * v0[0] + a1[1] * v0[1] + a1[2] * v0[2]
    s11 = a1[0] * v1[0] + a1[1] * v1[1] + a1[2] * v1[2] + dilation
    inverse = 1.0 / (s00 * s11 - s01 * s01)
    return v0, v1, (s11 * inverse, -s01 * inverse, s00 * inverse)


def cov_grad(con, grad):
    ca, cb, cc = con
    ga, gb, gc = grad[0], 0.5 * grad[1], grad[2]
    p00, p01 = ca * ga + cb * gb, ca * gb + cb * gc
    p10, p11 = cb * ga + cc * gb, cb * gb + cc * gc
    return (
        -(p00 * ca + p01 * cb),
        -(p00 * cb + p01 * cc),
        -(p10 * cb + p11 * cc),
    )


def rotation_of(quat):
    w, x, y, z = quat
    return (
        (1.0 - 2.0 * (y * y + z * z), 2.0 * (x * y - w * z), 2.0 * (x * z + w * y)),
        (2.0 * (x * y + w * z), 1.0 - 2.0 * (x * x + z * z), 2.0 * (y * z - w * x)),
        (2.0 * (x * z - w * y), 2.0 * (y * z + w * x), 1.0 - 2.0 * (x * x + y * y)),
    )


def load_dense(refs, dense):
    at = 0
    for ref in refs:
        rows, owned = ref.shape
        high = owned // LANES
        for h in range(high):
            part = ref[:, h * LANES : (h + 1) * LANES]
            if rows == 1:
                dense[at * high + h : at * high + h + 1, :] = part
            else:
                dense[pl.ds(at * high + h, rows, stride=high), :] = part
        at += rows


def geometry(row):
    raw = tuple(row(6 + a) for a in range(4))
    inverse = 1.0 / jnp.sqrt(
        raw[0] * raw[0] + raw[1] * raw[1] + raw[2] * raw[2] + raw[3] * raw[3]
    )
    quat = tuple(part * inverse for part in raw)
    rot = rotation_of(quat)
    squares = tuple(jnp.exp(2.0 * row(3 + a)) for a in range(3))

    def entry(a, b):
        return (
            rot[a][0] * rot[b][0] * squares[0]
            + rot[a][1] * rot[b][1] * squares[1]
            + rot[a][2] * rot[b][2] * squares[2]
        )

    sigma = tuple(entry(a, b) for a, b in ((0, 0), (0, 1), (0, 2), (1, 1), (1, 2), (2, 2)))
    return quat, inverse, rot, squares, sigma


def mask_of(index, rows):
    return lax.broadcasted_iota(jnp.int32, (rows, index.shape[1]), 0) == index


def as_bf16(mask):
    return mask.astype(F32).astype(BF16)


def two(value):
    hi = value.astype(BF16)
    return hi, (value - hi.astype(F32)).astype(BF16)


def scatter_rows(ref, start, stride, value):
    for h in range(ref.shape[0]):
        ref[h, pl.ds(start, value.shape[0], stride=stride), :] = value[
            :, h * LANES : (h + 1) * LANES
        ]


def take_rows(ref, rows):
    return jnp.concatenate([ref[h, rows, :] for h in range(ref.shape[0])], axis=1)


def render_kernel(
    sizes,
    means_hbm,
    log_scales_hbm,
    quat_w_hbm,
    quat_v_hbm,
    opacity_hbm,
    sh_hbm,
    cams,
    requests,
    lists_hbm,
    counts,
    cot_hbm,
    rendered,
    back_out,
    ask_out,
    harm_out,
    means,
    log_scales,
    quat_w,
    quat_v,
    opacity,
    sh,
    lists,
    cot,
    in_sem,
    ask_recv,
    feat_send,
    feat_recv,
    grad_send,
    grad_recv,
    dense,
    project,
    feats,
    slots,
    by_slot,
    low,
    gots,
    coefs,
    colours,
    cots,
    cots_t,
    live_op,
    moments,
    tints,
    grads,
    tinted,
    pictures,
    harm,
    send_sem,
    recv_sem,
    own_sem,
):
    n_img, n_tile, cap, tiles_here, length, pix = sizes
    owned = means.shape[1]
    high = owned // LANES
    devices = n_img * n_tile
    n_slots = devices * cap
    groups = n_slots // LANES
    per_img = n_tile * cap
    my_tile = lax.axis_index("tile")
    my_img = lax.axis_index("img")
    me = my_img * n_tile + my_tile

    def peer(k):
        other = lax.rem(me + k, devices)
        return other, (other // n_tile, lax.rem(other, n_tile))

    loads = [
        pltpu.make_async_copy(source, target, in_sem.at[at])
        for at, (source, target) in enumerate(
            (
                (means_hbm, means),
                (log_scales_hbm, log_scales),
                (quat_w_hbm, quat_w),
                (quat_v_hbm, quat_v),
                (opacity_hbm, opacity),
                (sh_hbm, sh),
                (lists_hbm, lists),
                (cot_hbm, cot),
            )
        )
    ]
    for load in loads:
        load.start()

    barrier = pltpu.get_barrier_semaphore()

    @pl.loop(1, devices, unroll=devices <= 32)
    def _(k):
        pl.semaphore_signal(barrier, inc=1, device_id=peer(k)[1], device_id_type=MESH)

    def exchange(at, source, target):
        mine = pltpu.make_async_copy(source.at[me], target.at[me], own_sem.at[at])
        mine.start()

        @pl.loop(1, devices, unroll=devices <= 32)
        def _(k):
            other, where = peer(k)
            pltpu.make_async_remote_copy(
                src_ref=source.at[other],
                dst_ref=target.at[me],
                send_sem=send_sem.at[at],
                recv_sem=recv_sem.at[at],
                device_id=where,
                device_id_type=MESH,
            ).start()

        return mine

    def arrive(at, target, mine):
        mine.wait()
        others = target.at[pl.ds(0, devices - 1)]
        pltpu.make_async_copy(others, others, recv_sem.at[at]).wait()

    def sent(at, source):
        others = source.at[pl.ds(0, devices - 1)]
        pltpu.make_async_copy(others, others, send_sem.at[at]).wait()

    cam = [[cams[i, c] for c in range(10)] for i in range(n_img)]
    img_rows = -(-n_img // 8) * 8
    img_row = lax.broadcasted_iota(jnp.int32, (img_rows, LANES), 0)
    polar = jnp.zeros((img_rows, LANES), F32)
    azimuth = jnp.zeros((img_rows, LANES), F32)
    for i in range(n_img):
        polar = jnp.where(img_row == i, cam[i][8], polar)
        azimuth = jnp.where(img_row == i, cam[i][9], azimuth)
    sp, cp = jnp.sin(polar), jnp.cos(polar)
    sz, cz = jnp.sin(azimuth), jnp.cos(azimuth)
    values, by_x, by_y, by_z = harmonics(sp * cz, sp * sz, cp)
    for m in range(16):
        by_polar = by_x[m] * (cp * cz) + by_y[m] * (cp * sz) - by_z[m] * sp
        by_azimuth = by_y[m] * (sp * cz) - by_x[m] * (sp * sz)
        for i in range(n_img):
            harm[i, 0, m : m + 1, :] = values[m][i : i + 1]
            harm[i, 1, m : m + 1, :] = by_polar[i : i + 1]
            harm[i, 2, m : m + 1, :] = by_azimuth[i : i + 1]
    for i in range(n_img):
        harm_out[i] = harm[i, 0]
    for load in loads[:6]:
        load.wait()
    load_dense((means, log_scales, quat_w, quat_v, opacity, sh), dense)

    pl.semaphore_wait(barrier, devices - 1)
    asking = exchange(0, requests, ask_recv)

    def row(at):
        return dense[at * high : (at + 1) * high, :]

    _, _, _, _, sigma = geometry(row)
    mean = tuple(row(a) for a in range(3))
    base = 1.0 / (1.0 + jnp.exp(-row(10)))
    for i in range(n_img):
        c = cam[i]
        _, _, con = conic(c, sigma)
        rows = [
            c[0] * mean[0] + c[1] * mean[1] + c[2] * mean[2] + c[6],
            c[3] * mean[0] + c[4] * mean[1] + c[5] * mean[2] + c[7],
            con[0],
            con[1],
            con[2],
            base,
        ]
        sums = [[None] * 3 for _ in range(3)]
        for k in range(3):
            for m in range(16):
                coeff = row(11 + 16 * k + m)
                for d in range(3):
                    term = coeff * harm[i, d, m : m + 1, :]
                    sums[d][k] = term if m == 0 else sums[d][k] + term
        rows += [total + 0.5 for total in sums[0]] + list(mean) + list(sigma) + sums[1] + sums[2]
        for at, value in enumerate(rows):
            project[pl.ds(at, high, stride=NSENT), :] = value
        for at, term in enumerate(split(project[0 : high * NSENT, :], 3)):
            feats[i, :, at * LANES : (at + 1) * LANES] = term.astype(BF16)

    arrive(0, ask_recv, asking)
    asks = ask_recv[...].reshape(devices, cap)
    halves = jnp.concatenate(
        [(asks // LANES).astype(F32), jnp.bitwise_and(asks, LANES - 1).astype(F32)], axis=0
    ).astype(BF16)
    repeat = as_bf16(
        lax.rem(lax.broadcasted_iota(jnp.int32, (cap, n_slots), 1), cap)
        == lax.broadcasted_iota(jnp.int32, (cap, n_slots), 0)
    )
    wide = dot(halves, repeat)
    here = (
        lax.broadcasted_iota(jnp.int32, (devices, n_slots), 1) // cap
        == lax.broadcasted_iota(jnp.int32, (devices, n_slots), 0)
    )
    ask_hi, ask_lo = (
        jnp.sum(
            jnp.where(here, wide[at * devices : (at + 1) * devices], 0.0), axis=0, keepdims=True
        ).astype(jnp.int32)
        for at in range(2)
    )
    ask_out[0:1, :] = ask_hi
    ask_out[1:2, :] = ask_lo
    for i in range(n_img):
        lanes = slice(i * per_img, (i + 1) * per_img)
        mask = as_bf16(mask_of(ask_lo[:, lanes], LANES))
        got = dot(feats[i], jnp.concatenate([mask] * 3, axis=0))
        pick = mask_of(ask_hi[:, lanes], high).astype(F32)
        total = got[0:NSENT] * pick[0:1]
        for h in range(1, high):
            total = total + got[h * NSENT : (h + 1) * NSENT] * pick[h : h + 1]
        slots[lanes, 0:NSENT] = jnp.transpose(total)
        feat_send[i * n_tile : (i + 1) * n_tile] = jnp.concatenate(
            [
                slots[pl.ds(i * per_img + c, n_tile, stride=cap), 0:NSENT]
                for c in range(cap)
            ],
            axis=1,
        ).reshape(n_tile, 1, cap * NSENT)

        @pl.loop(0, n_tile, unroll=n_tile <= 32)
        def _(k):
            place = lax.rem(my_tile + k, n_tile)
            other = i * n_tile + place

            @pl.when(other != me)
            def _():
                pltpu.make_async_remote_copy(
                    src_ref=feat_send.at[other],
                    dst_ref=feat_recv.at[me],
                    send_sem=send_sem.at[1],
                    recv_sem=recv_sem.at[1],
                    device_id=(i, place),
                    device_id_type=MESH,
                ).start()

    sending = pltpu.make_async_copy(feat_send.at[me], feat_recv.at[me], own_sem.at[1])
    sending.start()
    sent(0, requests)

    for load in loads[6:]:
        load.wait()
    coefs[...] = jnp.zeros_like(coefs)
    colours[...] = jnp.zeros_like(colours)
    for j in range(tiles_here):
        low[j] = as_bf16(mask_of(jnp.bitwise_and(lists[j : j + 1, :], LANES - 1), LANES))
        cot3 = jnp.concatenate([cot[0, k, j : j + 1, :] for k in range(3)], axis=0)
        c1, c2, c3 = split(cot3, 3)
        stack = jnp.concatenate([c1, c1, c2, c2, c1, c3, jnp.zeros((14, pix), F32)], axis=0)
        cots[j] = stack.astype(BF16)
        cots_t[j] = jnp.transpose(stack).astype(BF16)

    def basis_of(pixel, which):
        half = 0.5 * TILE_SIDE - 0.5
        x = lax.rem(pixel, TILE_SIDE).astype(F32) - half
        y = (pixel // TILE_SIDE).astype(F32) - half
        out = jnp.where(which == 0, 1.0, 0.0)
        for at, term in enumerate((x, y, x * x, x * y, y * y)):
            out = jnp.where(which == at + 1, term, out)
        return out.astype(BF16)

    basis_pe = basis_of(
        lax.broadcasted_iota(jnp.int32, (pix, 32), 0),
        lax.rem(lax.broadcasted_iota(jnp.int32, (pix, 32), 1), 8),
    )
    basis_ep = basis_of(
        lax.broadcasted_iota(jnp.int32, (16, pix), 1), lax.broadcasted_iota(jnp.int32, (16, pix), 0)
    )
    first = lax.broadcasted_iota(jnp.int32, (length, length), 0)
    second = lax.broadcasted_iota(jnp.int32, (length, length), 1)
    before = as_bf16(first < second)
    after = as_bf16(first > second)
    height = TILE_SIDE * tiles_here * n_tile / TW

    tinted[...] = jnp.zeros_like(tinted)
    pictures[...] = jnp.zeros_like(pictures)
    arrive(1, feat_recv, sending)
    packed = feat_recv[...].reshape(devices, cap * NSENT)
    for c in range(cap):
        slots[pl.ds(c, devices, stride=cap), 0:NSENT] = packed[:, c * NSENT : (c + 1) * NSENT]
    heads = []
    for h in range(groups):
        turned = jnp.transpose(slots[h * LANES : (h + 1) * LANES, :])[0:NSENT]
        by_slot[h * NSENT : (h + 1) * NSENT, :] = turned
        heads.append(turned[0:16])
    heads = jnp.concatenate(
        [term.astype(BF16) for term in split(jnp.concatenate(heads, axis=0), 3)], axis=0
    )

    for j in range(tiles_here):
        got = dot(heads, low[j])
        got = got[0 : 16 * groups] + got[16 * groups : 32 * groups] + got[32 * groups :]
        group = lists[j : j + 1, :] // LANES
        total = jnp.where(group == 0, got[0:16], 0.0)
        for h in range(1, groups):
            total = total + jnp.where(group == h, got[h * 16 : (h + 1) * 16], 0.0)
        scatter_rows(gots, j, tiles_here, total)

    def feature(at):
        return take_rows(gots, slice(at * tiles_here, (at + 1) * tiles_here))

    tile_row = lax.broadcasted_iota(jnp.int32, (tiles_here, length), 0)
    number = my_tile * tiles_here + tile_row
    lx = feature(0) - (
        (lax.rem(number, TW) * TILE_SIDE).astype(F32) + 0.5 * TILE_SIDE * (1 - TW)
    )
    ly = feature(1) - ((number // TW * TILE_SIDE).astype(F32) + 0.5 * TILE_SIDE - 0.5 * height)
    ca, cb, cc, op = (feature(at) for at in range(2, 6))
    ux = ca * lx + cb * ly
    uy = cc * ly + cb * lx
    live = jnp.zeros((tiles_here, length), jnp.int32)
    for j in range(tiles_here):
        live = jnp.where(tile_row == j, counts[0, j], live)
    lane = lax.broadcasted_iota(jnp.int32, (tiles_here, length), 1)
    live_op[...] = jnp.where(lane < live, op, 0.0)
    for at, value in enumerate((-0.5 * (ux * lx + uy * ly), ux, uy, -0.5 * ca, -cb, -0.5 * cc)):
        for term_at, term in enumerate(split(value, 3)):
            scatter_rows(coefs, 8 * term_at + at, 32, term)
    for k in range(3):
        terms = split(feature(6 + k), 3)
        for at, term_at in enumerate((0, 1, 0, 1, 2, 0)):
            scatter_rows(colours, 3 * at + k, 32, terms[term_at])
        for at in range(2):
            scatter_rows(tinted, at * 4 * tiles_here + k, 4, terms[at])
    painted = jnp.transpose(take_rows(tinted, slice(0, 8 * tiles_here)))
    painted_lane = lax.rem(
        lax.broadcasted_iota(jnp.int32, (length, 8 * tiles_here), 1), 4 * tiles_here
    )

    chunk = 32 if pix % 32 == 0 else pix
    before2 = jnp.concatenate([before, before], axis=0)
    after2 = jnp.concatenate([after, after], axis=0)
    basis2 = jnp.concatenate([basis_ep, basis_ep], axis=1)

    def chunks(function, *arrays):
        parts = [
            function(*(array[at : at + chunk] for array in arrays))
            for at in range(0, pix, chunk)
        ]
        return tuple(jnp.concatenate(part, axis=0) for part in zip(*parts))

    def render(tiles):
        rows = [pl.ds(pl.multiple_of(j * 32, 32), 32) for j in tiles]
        power = [dot(basis_pe, take_rows(coefs, r).astype(BF16)) for r in rows]
        colour = [take_rows(colours, r).astype(BF16) for r in rows]
        opacities = [live_op[pl.ds(j, 1), :] for j in tiles]
        alpha, summed, weight, pair, pull, pulled, later = ([] for _ in range(7))
        for at, j in enumerate(tiles):

            def first_part(p, op_row=opacities[at]):
                a = op_row * jnp.exp(p)
                hi, lo = two(jnp.log(1.0 - a))
                return a, jnp.concatenate([hi, lo], axis=1)

            a, logs = chunks(first_part, power[at])
            alpha.append(a)
            summed.append(dot(logs, before2))
            pull.append(dot(cots_t[j], colour[at]))
        for at, j in enumerate(tiles):

            def second_part(a, total, force):
                w = a * jnp.exp(total)
                p = force * w
                return (*two(w), p, jnp.concatenate(two(p), axis=1))

            hi, lo, p, wide = chunks(second_part, alpha[at], summed[at], pull[at])
            pulled.append(p)
            later.append(dot(wide, after2))
            weight.append(jnp.concatenate([hi, lo], axis=0))
            pair.append(jnp.concatenate([hi, lo], axis=1))
        for at, j in enumerate(tiles):

            def third_part(a, p, l):
                keep = 1.0 - a
                rough = pl.reciprocal(keep, approx=True)
                return two(p - l * (a * (rough * (2.0 - keep * rough))))

            hi, lo = chunks(third_part, alpha[at], pulled[at], later[at])
            moment = dot(basis2, jnp.concatenate([hi, lo], axis=0))
            scatter_rows(moments, j, tiles_here, moment[0:8])
        picture = 0.0
        for at, j in enumerate(tiles):
            cot2 = jnp.concatenate([cots[j], cots[j]], axis=1)
            tint = dot(cot2, weight[at])
            scatter_rows(tints, j, tiles_here, tint[0:3] + tint[6:9] + tint[15:18])
            brush = jnp.where(painted_lane // 4 == j, painted, 0.0).astype(BF16)
            picture = picture + dot(pair[at], jnp.concatenate([brush, brush], axis=0))
        pictures[...] += picture

    step = 2 if tiles_here % 2 == 0 else 1

    @pl.loop(0, tiles_here // step)
    def _(at):
        render([at * step + more for more in range(step)])

    picture = jnp.transpose(pictures[...])
    picture = picture[0 : 4 * tiles_here] + picture[4 * tiles_here : 8 * tiles_here]
    for j in range(tiles_here):
        for k in range(3):
            rendered[0, k, j : j + 1, :] = picture[4 * j + k : 4 * j + k + 1]

    def moment(at):
        return take_rows(moments, slice(at * tiles_here, (at + 1) * tiles_here))

    m0, mx, my = moment(0), moment(1), moment(2)
    nx, ny = mx - lx * m0, my - ly * m0
    nxx = moment(3) - 2.0 * lx * mx + lx * lx * m0
    nxy = moment(4) - lx * my - ly * mx + lx * ly * m0
    nyy = moment(5) - 2.0 * ly * my + ly * ly * m0
    grads[...] = jnp.zeros_like(grads)
    for at, value in enumerate(
        (ca * nx + cb * ny, cc * ny + cb * nx, -0.5 * nxx, -nxy, -0.5 * nyy, m0 / op)
    ):
        scatter_rows(grads, at, 16, value)
    for k in range(3):
        scatter_rows(
            grads, 6 + k, 16, take_rows(tints, slice(k * tiles_here, (k + 1) * tiles_here))
        )
    spreads = []
    for j in range(tiles_here):
        hi, lo = split(take_rows(grads, slice(16 * j, 16 * (j + 1))), 2)
        group = lists[j : j + 1, :] // LANES
        spread = [
            jnp.where(group == h, term, 0.0) for h in range(groups) for term in (hi, lo)
        ]
        spreads.append(jnp.concatenate(spread, axis=0).astype(BF16))
    back = dot_nt(
        jnp.concatenate(spreads, axis=1),
        jnp.concatenate([low[j] for j in range(tiles_here)], axis=1),
    )
    slot_rows = [back[32 * h : 32 * h + 16] + back[32 * h + 16 : 32 * h + 32] for h in range(groups)]

    g = [
        jnp.concatenate([rows[at : at + 1] for rows in slot_rows], axis=0) for at in range(NFEAT)
    ]
    f = [by_slot[pl.ds(at, groups, stride=NSENT), :] for at in range(NSENT)]
    c = [cams[my_img, at] for at in range(10)]
    v0, v1, _ = conic(c, f[12:18])
    h = cov_grad((f[2], f[3], f[4]), (g[2], g[3], g[4]))
    shares = [g[0] * f[9 + a] + 2.0 * (h[0] * v0[a] + h[1] * v1[a]) for a in range(3)]
    shares += [g[1] * f[9 + a] + 2.0 * (h[2] * v1[a] + h[1] * v0[a]) for a in range(3)]
    shares += [g[0], g[1]]
    shares += [sum(g[6 + k] * f[18 + 3 * d + k] for k in range(3)) for d in range(2)]
    slot_lane = lax.rem(lax.broadcasted_iota(jnp.int32, (16, LANES), 1), cap)
    is_camera = lax.broadcasted_iota(jnp.int32, (16, LANES), 0) == NFEAT
    camera_row = jnp.zeros((1, LANES), F32)
    for at, share in enumerate(shares):
        total = jnp.sum(jnp.sum(share, axis=0, keepdims=True), axis=1, keepdims=True)
        camera_row = jnp.where(slot_lane[0:1] == at, total, camera_row)
    for at, rows in enumerate(slot_rows):
        slots[at * LANES : (at + 1) * LANES, 0:NBACK] = jnp.transpose(
            jnp.where(is_camera, camera_row, rows)
        )
    grad_send[...] = jnp.concatenate(
        [slots[pl.ds(c, devices, stride=cap), 0:NBACK] for c in range(cap)], axis=1
    ).reshape(devices, 1, cap * NBACK)
    returning = exchange(2, grad_send, grad_recv)
    sent(1, feat_send)
    arrive(2, grad_recv, returning)
    back_out[...] = grad_recv[...].reshape(devices, cap * NBACK)
    sent(2, grad_send)


def owner_kernel(
    sizes,
    means,
    log_scales,
    quat_w,
    quat_v,
    opacity,
    cams,
    back,
    asked,
    harm,
    rendered_in,
    rendered,
    param_grad,
    camera_grad,
    dense,
    slots,
    result,
):
    n_img, n_tile, cap = sizes
    owned = means.shape[1]
    high = owned // LANES
    devices = n_img * n_tile
    per_img = n_tile * cap
    rendered[...] = rendered_in[...]
    load_dense((means, log_scales, quat_w, quat_v, opacity), dense)

    def row(at):
        return dense[at * high : (at + 1) * high, :]

    quat, inverse, rot, squares, sigma = geometry(row)
    base = 1.0 / (1.0 + jnp.exp(-row(10)))
    packed = back[...]
    for c in range(cap):
        slots[pl.ds(c, devices, stride=cap), 0:NBACK] = packed[:, c * NBACK : (c + 1) * NBACK]
    g_mean = [0.0, 0.0, 0.0]
    g_base = 0.0
    g_sigma = [[0.0] * 3 for _ in range(3)]
    g_colour = []
    for i in range(n_img):
        mine = jnp.concatenate(
            [
                jnp.transpose(slots[at : at + LANES, :])[0:NBACK]
                for at in range(i * per_img, (i + 1) * per_img, LANES)
            ],
            axis=1,
        )
        fold = mine[NFEAT : NFEAT + 1, 0:LANES]
        for at in range(LANES, per_img, LANES):
            fold = fold + mine[NFEAT : NFEAT + 1, at : at + LANES]
        shift = LANES // 2
        while shift >= cap:
            fold = fold + pltpu.roll(fold, shift, 1)
            shift //= 2
        camera_grad[i : i + 1, :] = fold[:, 0:10]
        lanes = slice(i * per_img, (i + 1) * per_img)
        pick = mask_of(asked[0:1, lanes], high)
        low = as_bf16(mask_of(asked[1:2, lanes], LANES))
        spread = jnp.concatenate(
            [
                jnp.concatenate(
                    [jnp.where(pick, term[at : at + 1], 0.0) for at in range(NFEAT)], axis=0
                ).astype(BF16)
                for term in split(mine, 2)
            ],
            axis=1,
        )
        full = dot_nt(spread, jnp.concatenate([low] * 2, axis=1))
        g = [full[at * high : (at + 1) * high] for at in range(NFEAT)]
        c = [cams[i, at] for at in range(8)]
        _, _, con = conic(c, sigma)
        h = cov_grad(con, (g[2], g[3], g[4]))
        for a in range(3):
            g_mean[a] = g_mean[a] + c[a] * g[0] + c[3 + a] * g[1]
            for b in range(a, 3):
                g_sigma[a][b] = (
                    g_sigma[a][b]
                    + (c[a] * c[b]) * h[0]
                    + (c[a] * c[3 + b] + c[3 + a] * c[b]) * h[1]
                    + (c[3 + a] * c[3 + b]) * h[2]
                )
        g_base = g_base + g[5]
        g_colour.append(g[6:9])

    def put(at, value):
        result[at * high : (at + 1) * high, :] = value

    for k in range(3):
        for m in range(16):
            put(
                11 + 16 * k + m,
                sum(harm[i, m : m + 1, :] * g_colour[i][k] for i in range(n_img)),
            )
    for a in range(3):
        put(a, g_mean[a])
        for b in range(a):
            g_sigma[a][b] = g_sigma[b][a]
    r = [[None] * 3 for _ in range(3)]
    for b in range(3):
        pull = [
            g_sigma[a][0] * rot[0][b] + g_sigma[a][1] * rot[1][b] + g_sigma[a][2] * rot[2][b]
            for a in range(3)
        ]
        twice = 2.0 * squares[b]
        for a in range(3):
            r[a][b] = twice * pull[a]
        put(3 + b, r[0][b] * rot[0][b] + r[1][b] * rot[1][b] + r[2][b] * rot[2][b])
    w, x, y, z = quat
    g_quat = (
        z * (r[1][0] - r[0][1]) + y * (r[0][2] - r[2][0]) + x * (r[2][1] - r[1][2]),
        y * (r[0][1] + r[1][0])
        + z * (r[0][2] + r[2][0])
        + w * (r[2][1] - r[1][2])
        - 2.0 * x * (r[1][1] + r[2][2]),
        x * (r[0][1] + r[1][0])
        + z * (r[1][2] + r[2][1])
        + w * (r[0][2] - r[2][0])
        - 2.0 * y * (r[0][0] + r[2][2]),
        x * (r[0][2] + r[2][0])
        + y * (r[1][2] + r[2][1])
        + w * (r[1][0] - r[0][1])
        - 2.0 * z * (r[0][0] + r[1][1]),
    )
    along = sum(quat[a] * g_quat[a] for a in range(4))
    for a in range(4):
        put(6 + a, 2.0 * (g_quat[a] - quat[a] * along) * inverse)
    put(10, g_base * base * (1.0 - base))
    rows = param_grad.shape[0]
    for h in range(high):
        param_grad[:, h * LANES : (h + 1) * LANES] = result[pl.ds(h, rows, stride=high), :]


def local(
    means,
    log_scales,
    quat_w,
    quat_v,
    opacity,
    sh_coeffs,
    cameras,
    requests,
    lists,
    counts,
    image_cot,
):
    n_img, n_tile, cap = requests.shape[2:]
    devices = n_img * n_tile
    n_slots = devices * cap
    owned = means.shape[1]
    high = owned // LANES
    tiles_here, length = lists.shape[1:]
    pix = image_cot.shape[3]
    vmem = pl.BlockSpec(memory_space=pltpu.VMEM)
    smem = pl.BlockSpec(memory_space=pltpu.SMEM)
    hbm = pl.BlockSpec(memory_space=pl.ANY)
    small = (means, log_scales, quat_w, quat_v, opacity)
    few = sum(part.shape[0] for part in small)
    rows = few + sh_coeffs.shape[0]
    image_shape = jax.ShapeDtypeStruct(image_cot.shape, F32)
    rendered, back, asked, harm = pl.pallas_call(
        functools.partial(render_kernel, (n_img, n_tile, cap, tiles_here, length, pix)),
        out_shape=(
            image_shape,
            jax.ShapeDtypeStruct((devices, cap * NBACK), F32),
            jax.ShapeDtypeStruct((2, n_slots), jnp.int32),
            jax.ShapeDtypeStruct((n_img, 16, LANES), F32),
        ),
        in_specs=[hbm] * 6 + [smem, hbm, hbm, smem, hbm],
        out_specs=(vmem,) * 4,
        scratch_shapes=[
            *(pltpu.VMEM(part.shape, F32) for part in (*small, sh_coeffs)),
            pltpu.VMEM((tiles_here, length), jnp.int32),
            pltpu.VMEM(image_cot.shape, F32),
            pltpu.SemaphoreType.DMA((8,)),
            pltpu.VMEM((devices, 1, cap), jnp.int32),
            pltpu.VMEM((devices, 1, cap * NSENT), F32),
            pltpu.VMEM((devices, 1, cap * NSENT), F32),
            pltpu.VMEM((devices, 1, cap * NBACK), F32),
            pltpu.VMEM((devices, 1, cap * NBACK), F32),
            pltpu.VMEM((rows * high + high, LANES), F32),
            pltpu.VMEM((high * NSENT + NSENT, LANES), F32),
            pltpu.VMEM((n_img, high * NSENT, 3 * LANES), BF16),
            pltpu.VMEM((n_slots + cap, LANES), F32),
            pltpu.VMEM((n_slots // LANES * NSENT + NSENT, LANES), F32),
            pltpu.VMEM((tiles_here, LANES, length), BF16),
            pltpu.VMEM((length // LANES, 16 * tiles_here + 16, LANES), F32),
            pltpu.VMEM((length // LANES, 32 * tiles_here + 32, LANES), F32),
            pltpu.VMEM((length // LANES, 32 * tiles_here + 32, LANES), F32),
            pltpu.VMEM((tiles_here, 32, pix), BF16),
            pltpu.VMEM((tiles_here, pix, 32), BF16),
            pltpu.VMEM((tiles_here, length), F32),
            pltpu.VMEM((length // LANES, 9 * tiles_here, LANES), F32),
            pltpu.VMEM((length // LANES, 4 * tiles_here, LANES), F32),
            pltpu.VMEM((length // LANES, 16 * tiles_here + 16, LANES), F32),
            pltpu.VMEM((length // LANES, 8 * tiles_here + 4, LANES), F32),
            pltpu.VMEM((pix, 8 * tiles_here), F32),
            pltpu.VMEM((n_img, 3, 16, LANES), F32),
            pltpu.SemaphoreType.DMA((3,)),
            pltpu.SemaphoreType.DMA((3,)),
            pltpu.SemaphoreType.DMA((3,)),
        ],
        compiler_params=pltpu.CompilerParams(
            collective_id=0, has_side_effects=True, vmem_limit_bytes=60 * 1024 * 1024
        ),
    )(
        *small,
        sh_coeffs,
        cameras,
        requests.reshape(devices, 1, cap),
        lists[0],
        counts,
        image_cot,
    )
    return pl.pallas_call(
        functools.partial(owner_kernel, (n_img, n_tile, cap)),
        out_shape=(
            image_shape,
            jax.ShapeDtypeStruct((rows, owned), F32),
            jax.ShapeDtypeStruct(cameras.shape, F32),
        ),
        in_specs=[vmem] * 5 + [smem] + [vmem] * 4,
        out_specs=(vmem,) * 3,
        scratch_shapes=[
            pltpu.VMEM((few * high + high, LANES), F32),
            pltpu.VMEM((n_slots + cap, LANES), F32),
            pltpu.VMEM((rows * high + high, LANES), F32),
        ],
        compiler_params=pltpu.CompilerParams(vmem_limit_bytes=60 * 1024 * 1024),
    )(*small, cameras, back, asked, harm, rendered)


def solution(mesh):
    owners = P(None, ("img", "tile"))
    images = P("img", None, "tile", None)
    return jax.shard_map(
        local,
        mesh=mesh,
        in_specs=(owners,) * 6
        + (P(), P("img", "tile", None, None, None), P("img", "tile", None), P("img", "tile"), images),
        out_specs=(images, owners, P()),
        check_vma=False,
    )
```
